32 devices in a mesh: img: 4 (over z), ch: 8 (over y, x, core).
Axes of the slice: x: 2, y: 2, z: 4, core: 2. Of those that a mesh axis runs over, the one named last changes fastest.
Arguments:
- features: bfloat16 [1024, 4, 576], P('ch', 'img'), may hold values from -6 to 6
- grid: int32 [4], P('img'), may hold values from 16 to 24, as said below
- reduce_w: bfloat16 [2, 1024, 256], P(None, None, 'ch'), may hold values from -0.1875 to 0.1875
- conv_w: bfloat16 [2, 9, 256, 256], P(None, None, None, 'ch'), may hold values from -0.125 to 0.125
- expand_w: bfloat16 [2, 256, 1024], P(None, 'ch'), may hold values from -0.375 to 0.375
- mid_gain: float32 [2, 2, 256], P(None, None, 'ch'), may hold values from 0.5 to 1.5
- mid_bias: float32 [2, 2, 256], P(None, None, 'ch'), may hold values from -2 to 2
- out_gain: float32 [2, 1024], P(None, 'ch'), may hold values from 0.5 to 1.5
- out_bias: float32 [2, 1024], P(None, 'ch'), may hold values from -2 to 2
- read_w1: bfloat16 [1024, 4096], P(None, 'ch'), may hold values from -0.1875 to 0.1875
- read_b1: float32 [4096], P('ch'), may hold values from -2 to 2
- read_w2: bfloat16 [4096, 4096], P('ch'), may hold values from -0.09375 to 0.09375
- read_b2: float32 [4096], P('ch'), may hold values from -2 to 2
- cotangent: bfloat16 [4096, 4, 144], P('ch', 'img'), may hold values from -6 to 6
Outputs:
- tokens: bfloat16 [4096, 4, 144], P('ch', 'img')
- features_grad: float32 [1024, 4, 576], P('ch', 'img')
- reduce_w_grad: float32 [2, 1024, 256], P(None, None, 'ch')
- conv_w_grad: float32 [2, 9, 256, 256], P(None, None, None, 'ch')
- expand_w_grad: float32 [2, 256, 1024], P(None, 'ch')
- mid_gain_grad: float32 [2, 2, 256], P(None, None, 'ch')
- mid_bias_grad: float32 [2, 2, 256], P(None, None, 'ch')
- out_gain_grad: float32 [2, 1024], P(None, 'ch')
- out_bias_grad: float32 [2, 1024], P(None, 'ch')
- read_w1_grad: float32 [1024, 4096], P(None, 'ch')
- read_b1_grad: float32 [4096], P('ch')
- read_w2_grad: float32 [4096, 4096], P('ch')
- read_b2_grad: float32 [4096], P('ch')
The draws below stay inside these ranges and needn't reach their ends.
Inputs may be any that keep to these rules, and one draw needn't show every extreme that they name: `grid`: each image is 16 or 24 patches a side; both sides occur in every draw.
All inputs are finite; a program needn't handle non-finite values.
Results may differ from the reference program's by a relative error of at most 0.028.
Values may be sent and summed in bfloat16 or wider, within the bound.
No kernel may reach another device: no remote copies, remote signals or barrier semaphores. Data moves between devices by JAX's collectives and lax.ppermute only.
A program may use at most 128 MiB of HBM per device.

```python
import jax
import jax.numpy as jnp
from jax import lax

C = 1024
MID = 256
HID = 4096
OUT = 4096
GRID = 24
POOLED = 12
IMAGES = 4


def draw_grid(key, part):
    key = jax.random.fold_in(key, 11)
    first_key, second_key = jax.random.split(key)
    larger = jax.random.randint(first_key, (IMAGES,), 0, 2)
    chosen = jax.random.randint(second_key, (), 0, IMAGES)
    position = jnp.arange(IMAGES)
    larger = jnp.where(position == chosen, 1, larger)
    larger = jnp.where(position == (chosen + IMAGES // 2) % IMAGES, 0, larger)
    return (16 + 8 * larger).astype(jnp.int32)


def block_scale(key, dims, shards, least, largest):
    def one(axis_at, parts):
        draws = jax.random.uniform(jax.random.fold_in(jax.random.fold_in(key, 6), axis_at), (parts,), jnp.float32, least / len(shards), largest / len(shards))
        return jnp.repeat(jnp.exp(draws), dims[axis_at] // parts).reshape((-1,) + (1,) * (len(dims) - axis_at - 1))

    loudness = one(*shards[0])
    for cut in shards[1:]:
        loudness = loudness * one(*cut)
    return loudness


def centred(rng, shape, width, reach, pieces=(), held_as=jnp.bfloat16):
    values = width * jax.random.normal(rng, shape, jnp.float32)
    if pieces:
        values = values * block_scale(rng, shape, pieces, -0.22, 0.18)
    return jnp.clip(values, -reach, reach).astype(held_as)


def setup_inputs(seed: int = 0) -> dict:
    keys = jax.random.split(jax.random.key(seed), 15)
    return {
        "features": centred(keys[0], (C, IMAGES, GRID * GRID), 1.0, 6.0, ((0, 8), (1, 4))),
        "grid": draw_grid(jax.random.fold_in(keys[14], 71), 0),
        "reduce_w": centred(keys[2], (2, C, MID), C ** -0.5, 0.1875, ((2, 8),)),
        "conv_w": centred(keys[3], (2, 9, MID, MID), (9 * MID) ** -0.5, 0.125, ((3, 8),)),
        "expand_w": centred(keys[4], (2, MID, C), MID ** -0.5, 0.375, ((1, 8),)),
        "mid_gain": jnp.clip(1.0 + 0.1 * jax.random.normal(keys[5], (2, 2, MID), jnp.float32), 0.5, 1.5),
        "mid_bias": centred(keys[6], (2, 2, MID), 0.3, 2.0, ((2, 8),), jnp.float32),
        "out_gain": jnp.clip(1.0 + 0.1 * jax.random.normal(keys[7], (2, C), jnp.float32), 0.5, 1.5),
        "out_bias": centred(keys[8], (2, C), 0.3, 2.0, ((1, 8),), jnp.float32),
        "read_w1": centred(keys[9], (C, HID), C ** -0.5, 0.1875, ((1, 8),)),
        "read_b1": centred(keys[10], (HID,), 0.3, 2.0, ((0, 8),), jnp.float32),
        "read_w2": centred(keys[11], (HID, OUT), HID ** -0.5, 0.09375, ((0, 8),)),
        "read_b2": centred(keys[12], (OUT,), 0.3, 2.0, ((0, 8),), jnp.float32),
        "cotangent": centred(keys[13], (OUT, IMAGES, POOLED * POOLED), 1.0, 6.0, ((0, 8), (1, 4))),
    }


PRECISE = lax.Precision.HIGHEST
EPSILON = 1e-06
OFFSETS = [(-1, -1), (-1, 0), (-1, 1), (0, -1), (0, 0), (0, 1), (1, -1), (1, 0), (1, 1)]

@jax.custom_vjp
def low(v):
    return lax.optimization_barrier(v.astype(jnp.bfloat16)).astype(jnp.float32)

@jax.custom_vjp
def low_back(v):
    return v

def low_keep(v):
    return (low(v), None)

def low_pass(kept, grad):
    return (grad,)

def back_keep(v):
    return (v, None)

def back_low(kept, grad):
    return (low(grad),)
low.defvjp(low_keep, low_pass)
low_back.defvjp(back_keep, back_low)

def valid_mask(grid, side):
    place = jnp.arange(side, dtype=jnp.int32)
    inside = (place[None, :] < grid[:, None]).astype(jnp.float32)
    return (inside[:, :, None] * inside[:, None, :]).reshape(grid.shape[0], side * side)

def pool_table(grid):
    target = jnp.arange(POOLED, dtype=jnp.int32)
    place = jnp.arange(GRID, dtype=jnp.int32)
    extent = grid[:, None]
    begin = target[None, :] * extent // POOLED
    finish = ((target[None, :] + 1) * extent + POOLED - 1) // POOLED
    inside = (place[None, None, :] >= begin[:, :, None]) & (place[None, None, :] < finish[:, :, None])
    return inside.astype(jnp.float32) / (finish - begin)[:, :, None].astype(jnp.float32)

def shifted(field, side, rise, step):
    leading = field.shape[:-1]
    square = field.reshape(leading + (side, side))
    padded = jnp.pad(square, [(0, 0)] * len(leading) + [(1, 1), (1, 1)])
    window = padded[..., 1 + rise:1 + rise + side, 1 + step:1 + step + side]
    return window.reshape(leading + (side * side,))

def pooled_of(field, table):
    square = field.reshape(field.shape[0], field.shape[1], GRID, GRID)
    across = jnp.einsum('cbrk,bir->cbik', square, table, precision=PRECISE)
    result = jnp.einsum('cbik,bjk->cbij', across, table, precision=PRECISE)
    return result.reshape(field.shape[0], field.shape[1], POOLED * POOLED)

def normalize(values, gain, bias):
    center = lax.optimization_barrier(jnp.mean(values, axis=0))
    spread = lax.optimization_barrier(jnp.mean(values * values, axis=0)) - center * center
    unit = (values - center) * lax.rsqrt(spread + EPSILON)
    return unit * gain[:, None, None] + bias[:, None, None]

def convolve(field, kernel, side):
    total = jnp.zeros((kernel.shape[2],) + field.shape[1:], jnp.float32)
    for index, (rise, step) in enumerate(OFFSETS):
        total = total + jnp.einsum('mbs,mn->nbs', shifted(field, side, rise, step), kernel[index], precision=PRECISE)
    return total

def bottleneck(inputs, weights, layer, mask, side):
    reduce_w, conv_w, expand_w, mid_gain, mid_bias, out_gain, out_bias = weights
    reduced = low_back(jnp.einsum('cbs,cm->mbs', inputs, reduce_w[layer], precision=PRECISE))
    first_act = low(jax.nn.silu(normalize(reduced, mid_gain[layer, 0], mid_bias[layer, 0])) * mask)
    conv_out = low_back(convolve(first_act, conv_w[layer], side))
    second_act = low(jax.nn.silu(normalize(conv_out, mid_gain[layer, 1], mid_bias[layer, 1])))
    expanded = low_back(jnp.einsum('mbs,mc->cbs', second_act, expand_w[layer], precision=PRECISE))
    return jax.nn.silu(normalize(expanded, out_gain[layer], out_bias[layer]) + inputs) * mask

def reference(features, grid, reduce_w, conv_w, expand_w, mid_gain, mid_bias, out_gain, out_bias, read_w1, read_b1, read_w2, read_b2, cotangent):
    mask = valid_mask(grid, GRID)[None]
    table = pool_table(grid)

    def forward(inputs, rw, cw, ew, mg, mb, og, ob, first_w, first_b, second_w, second_b):
        weights = (rw, cw, ew, mg, mb, og, ob)
        first = bottleneck(inputs, weights, 0, mask, GRID)
        pooled = low(pooled_of(first, table))
        second = bottleneck(pooled, weights, 1, 1.0, POOLED)
        readin = low(second)
        hidden = low_back(jnp.einsum('cbt,ch->hbt', readin, first_w, precision=PRECISE) + first_b[:, None, None])
        hidden_act = low(jax.nn.gelu(hidden))
        return jnp.einsum('hbt,ho->obt', hidden_act, second_w, precision=PRECISE) + second_b[:, None, None]
    floats = [arg.astype(jnp.float32) for arg in (features, reduce_w, conv_w, expand_w, mid_gain, mid_bias, out_gain, out_bias, read_w1, read_b1, read_w2, read_b2)]
    result, pullback = jax.vjp(forward, *floats)
    grads = pullback(cotangent.astype(jnp.float32))
    return (result.astype(jnp.bfloat16), grads[0], grads[1], grads[2], grads[3], grads[4], grads[5], grads[6], grads[7], grads[8], grads[9], grads[10], grads[11])
```

```python
import functools

import jax
import jax.numpy as jnp
from jax import lax
from jax.experimental import pallas as pl
from jax.experimental.pallas import tpu as pltpu
from jax.sharding import PartitionSpec as P

GRID = 24
POOLED = 12
EPSILON = 1e-06
OFFSETS = [(-1, -1), (-1, 0), (-1, 1), (0, -1), (0, 0), (0, 1), (1, -1), (1, 0), (1, 1)]
TAPS = len(OFFSETS)
LANES = 128
BF16 = jnp.bfloat16
F32 = jnp.float32
VMEM = pl.BlockSpec(memory_space=pltpu.VMEM)
SMEM = pl.BlockSpec(memory_space=pltpu.SMEM)
HBM = pl.BlockSpec(memory_space=pl.ANY)


def dot_nn(left, right):
    return lax.dot_general(left, right, (((1,), (0,)), ((), ())), preferred_element_type=F32)


def dot_nt(left, right):
    return lax.dot_general(left, right, (((1,), (1,)), ((), ())), preferred_element_type=F32)


def dot_tn(left, right):
    return lax.dot_general(left, right, (((0,), (0,)), ((), ())), preferred_element_type=F32)


def sds(shape, dtype):
    return jax.ShapeDtypeStruct(tuple(shape), dtype)


def call(kernel, out_shape, in_specs, scratch=(), out_specs=None, vmem=32, flops=0, moved=0, grid=()):
    return pl.pallas_call(
        kernel,
        out_shape=out_shape,
        grid=grid,
        in_specs=in_specs,
        out_specs=out_specs if out_specs is not None else jax.tree.map(lambda _: VMEM, out_shape),
        scratch_shapes=list(scratch),
        compiler_params=pltpu.CompilerParams(vmem_limit_bytes=vmem << 20),
        cost_estimate=pl.CostEstimate(flops=flops, bytes_accessed=moved, transcendentals=0),
    )


def ppermute_xor(x, axis, mask):
    return lax.ppermute(x, axis, [(i, i ^ mask) for i in range(lax.axis_size(axis))])


def gather_pieces(x):
    n = lax.axis_size("ch")
    if n > 8:
        whole = lax.all_gather(x, "ch", axis=0)
        me = lax.axis_index("ch")
        return [lax.dynamic_index_in_dim(whole, me ^ r, 0, keepdims=False) for r in range(n)]
    pieces = [None] * n
    pieces[0] = x
    for r in range(2, n, 2):
        pieces[r] = ppermute_xor(x, "ch", r)
    for r in range(0, n, 2):
        pieces[r + 1] = ppermute_xor(pieces[r], "ch", 1)
    return pieces


def along_images(x):
    return [ppermute_xor(x, "img", m) for m in range(1, lax.axis_size("img"))]


def columns(chan, mid):
    reduce_end = chan
    conv_end = reduce_end + TAPS * mid
    expand_end = conv_end + chan
    return reduce_end, conv_end, expand_end, expand_end + LANES, expand_end + 2 * LANES


def split_low(value):
    high = value.astype(BF16).astype(F32)
    return high, value - high


def pack_kernel(slots, *refs):
    if slots:
        feat, *refs = refs
    red, conv, exp, mid_gain, mid_bias, out_gain, out_bias, packet, scr = refs
    held = red.shape[0]
    chan, mid = red.shape[1], conv.shape[2]
    base = 0
    if slots:
        for b in range(slots // held):
            packet[:, b * LANES : (b + 1) * LANES] = feat[b * held : (b + 1) * held, :]
        base = slots // held * LANES
    reduce_end, conv_end, expand_end, mid_end, end = columns(chan, mid)
    packet[:, base : base + reduce_end] = red[...]
    for j in range(TAPS):
        at = base + reduce_end + j * mid
        packet[:, at : at + mid] = conv[j]
    packet[:, base + conv_end : base + expand_end] = exp[...]
    scr[...] = jnp.zeros_like(scr)
    for which in range(2):
        for kind, ref in enumerate((mid_gain, mid_bias)):
            high, low = split_low(ref[which : which + 1, :])
            at = 4 * which + 2 * kind
            scr[at : at + 1, 0:held] = high
            scr[at + 1 : at + 2, 0:held] = low
    packet[:, base + expand_end : base + mid_end] = scr[...].T[0:held, :].astype(BF16)
    scr[...] = jnp.zeros_like(scr)
    for kind, ref in enumerate((out_gain, out_bias)):
        high, low = split_low(ref[...])
        scr[2 * kind : 2 * kind + 1, :] = high
        scr[2 * kind + 1 : 2 * kind + 2, :] = low
    packet[:, base + mid_end : base + end] = scr[0:held, :].astype(BF16)


def pack(layer, feat, red, conv, exp, mid_gain, mid_bias, out_gain, out_bias):
    held, chan = red.shape[1:]
    mid = conv.shape[3]
    width = columns(chan, mid)[-1]
    slots = 0 if feat is None else feat.shape[0]
    width += slots // held * LANES

    def layered(x):
        return pl.BlockSpec((None,) + x.shape[1:], lambda i: (layer,) + (0,) * (x.ndim - 1))

    args = [red, conv, exp, mid_gain, mid_bias, out_gain[:, None, :], out_bias[:, None, :]]
    specs = [layered(x) for x in args]
    if slots:
        args, specs = [feat] + args, [VMEM] + specs
    return call(
        functools.partial(pack_kernel, slots),
        sds((held, width), BF16),
        specs,
        [pltpu.VMEM((LANES, LANES), F32)],
        vmem=8,
        moved=2 * held * width * 2,
        grid=(1,),
    )(*args)


def assemble(me, slots, pieces, x_ref, w_ref, mid_ref, out_ref, scr):
    held = pieces[0].shape[0]
    chan, mid = out_ref.shape[1], w_ref.shape[0]
    reduce_end, conv_end, expand_end, mid_end, end = columns(chan, mid)
    base = slots // held * LANES
    for r, piece in enumerate(pieces):
        owner = me ^ r
        rows = pl.ds(pl.multiple_of(owner * held, held), held)
        lanes = pl.ds(pl.multiple_of(owner * LANES, LANES), LANES)
        for b in range(slots // held):
            x_ref[b * held : (b + 1) * held, lanes] = piece[:, b * LANES : (b + 1) * LANES]
        w_ref[rows, :] = piece[:, base : base + expand_end]
        scr[rows, :] = piece[:, base + expand_end : base + mid_end].astype(F32)
        block = piece[:, base + mid_end : base + end].astype(F32)
        out_ref[0:1, lanes] = block[0:1, :] + block[1:2, :]
        out_ref[1:2, lanes] = block[2:3, :] + block[3:4, :]
    flat = scr[...].T
    for q in range(4):
        mid_ref[q : q + 1, :] = flat[2 * q : 2 * q + 1, :] + flat[2 * q + 1 : 2 * q + 2, :]


def sigmoid(value):
    return 0.5 * jnp.tanh(0.5 * value) + 0.5


def silu(value):
    return value * sigmoid(value)


def silu_slope(value):
    gate = sigmoid(value)
    return gate * (1.0 + value * (1.0 - gate))


def unit_of(values):
    inverse = 1.0 / values.shape[-1]
    center = jnp.sum(values, axis=-1, keepdims=True) * inverse
    spread = jnp.sum(values * values, axis=-1, keepdims=True) * inverse - center * center
    factor = lax.rsqrt(spread + EPSILON)
    return (values - center) * factor, factor


def chunked(slots, step, body, carry=None):
    def wrapped(i, c):
        return body(pl.ds(pl.multiple_of(i * step, step), step), pl.multiple_of(i * step, step), c)

    return lax.fori_loop(0, slots // step, wrapped, carry)


def pad_of(side):
    return -(-(side + 1) // 16) * 16


def shift_columns(field, side, slots, aux_ref):
    pad = pad_of(side)
    field[0, pad : pad + slots, :] = field[1, pad - 1 : pad - 1 + slots, :] * aux_ref[:, 1:2]
    field[2, pad : pad + slots, :] = field[1, pad + 1 : pad + 1 + slots, :] * aux_ref[:, 2:3]


def clear_edges(field, side, slots):
    pad = pad_of(side)
    for k in range(3):
        field[k, 0:pad, :] = jnp.zeros((pad, field.shape[2]), F32)
        field[k, pad + slots : pad + slots + pad, :] = jnp.zeros((pad, field.shape[2]), F32)


def tap(field, side, slots, rise, step):
    at = pad_of(side) + rise * side
    return field[step + 1, at : at + slots, :].astype(BF16)


def forward_body(side, aux, x_ref, w_ref, mid_ref, out_ref, u1, u2, u3, fac, pat, field, act, finish):
    slots = x_ref.shape[0]
    chan, mid = out_ref.shape[1], w_ref.shape[0]
    reduce_end, conv_end, expand_end, _, _ = columns(chan, mid)
    pad = pad_of(side)
    clear_edges(field, side, slots)
    u1[...] = dot_nt(x_ref[...], w_ref[:, 0:reduce_end])

    def first(rows, start, carry):
        unit, factor = unit_of(u1[rows, :])
        u1[rows, :] = unit
        fac[0, rows, :] = jnp.broadcast_to(factor, (unit.shape[0], LANES))
        value = silu(unit * mid_ref[0:1, :] + mid_ref[1:2, :]) * aux[rows, 0:1]
        field[1, pl.ds(pad + start, unit.shape[0]), :] = value
        return carry

    chunked(slots, 48, first)
    shift_columns(field, side, slots, aux)
    for j, (rise, step) in enumerate(OFFSETS):
        pat[:, j * mid : (j + 1) * mid] = tap(field, side, slots, rise, step)
    u2[...] = dot_nt(pat[...], w_ref[:, reduce_end:conv_end])

    def second(rows, start, carry):
        unit, factor = unit_of(u2[rows, :])
        u2[rows, :] = unit
        fac[1, rows, :] = jnp.broadcast_to(factor, (unit.shape[0], LANES))
        act[rows, :] = silu(unit * mid_ref[2:3, :] + mid_ref[3:4, :]).astype(BF16)
        return carry

    chunked(slots, 48, second)
    u3[...] = dot_nn(act[...], w_ref[:, conv_end:expand_end])

    def third(rows, start, carry):
        unit, factor = unit_of(u3[rows, :])
        u3[rows, :] = unit
        fac[2, rows, :] = jnp.broadcast_to(factor, (unit.shape[0], LANES))
        summed = unit * out_ref[0:1, :] + out_ref[1:2, :] + x_ref[rows, :].astype(F32)
        finish[rows, :] = (silu(summed) * aux[rows, 0:1]).astype(BF16)
        return carry

    chunked(slots, 16, third)


def forward_kernel(side, pooling, assembled, count, *refs):
    refs = list(refs)
    me_ref, aux = refs.pop(0), refs.pop(0)
    spread = refs.pop(0) if pooling else None
    if assembled:
        x_ref, w_ref, mid_ref, out_ref = refs[:4]
        result, u1, u2, u3, fac, pat = refs[4:10]
        scratch = refs[10:]
    else:
        if not pooling:
            x_ref = refs.pop(0)
        pieces, refs = refs[:count], refs[count:]
        if pooling:
            x_ref = refs.pop(0)
        w_ref, mid_ref, out_ref, result, u1, u2, u3, fac, pat = refs[:9]
        scratch = refs[9:]
    field, act, scr, *rest = scratch
    slots = x_ref.shape[0]
    if not assembled:
        assemble(me_ref[0], slots if pooling else 0, pieces, x_ref, w_ref, mid_ref, out_ref, scr)
    finish = rest[0] if pooling else result
    forward_body(side, aux, x_ref, w_ref, mid_ref, out_ref, u1, u2, u3, fac, pat, field, act, finish)
    if pooling:
        result[...] = dot_nn(spread[...], finish[...]).astype(BF16)


def block_forward(side, chan, mid, me, aux, spread, x, pieces, assembled):
    slots = side * side
    pooling = spread is not None
    width = columns(chan, mid)[2]
    given = [me, aux] + ([spread] if pooling else [])
    kept = [
        sds((spread.shape[0] if pooling else slots, chan), BF16),
        sds((slots, mid), F32),
        sds((slots, mid), F32),
        sds((slots, chan), F32),
        sds((3, slots, LANES), F32),
        sds((slots, TAPS * mid), BF16),
    ]
    whole = [sds((mid, width), BF16), sds((8, mid), F32), sds((8, chan), F32)]
    if assembled is not None:
        args = given + list(assembled)
        outs = kept
    elif pooling:
        args = given + list(pieces)
        outs = [sds((slots, chan), BF16)] + whole + kept
    else:
        args = given + [x] + list(pieces)
        outs = whole + kept
    scratch = [
        pltpu.VMEM((3, slots + 2 * pad_of(side), mid), F32),
        pltpu.VMEM((slots, mid), BF16),
        pltpu.VMEM((mid, LANES), F32),
    ]
    if pooling:
        scratch.append(pltpu.VMEM((slots, chan), BF16))
    got = call(
        functools.partial(
            forward_kernel, side, pooling, assembled is not None, 0 if pieces is None else len(pieces)
        ),
        outs,
        [SMEM] + [VMEM] * (len(args) - 1),
        scratch,
        flops=2 * slots * mid * (2 * chan + TAPS * mid),
        moved=30 * slots * chan,
        vmem=40,
    )(*args)
    if assembled is not None:
        source = list(assembled)
    elif pooling:
        source, got = list(got[:4]), got[4:]
    else:
        source, got = [x] + list(got[:3]), got[3:]
    return got[0], source + list(got[1:])


def fold(value):
    return jnp.sum(value.reshape(value.shape[0] // 8, 8, value.shape[1]), axis=0)


def norm_back(upstream, unit, factor, gain):
    inverse = 1.0 / unit.shape[-1]
    scaled = upstream * gain
    first = jnp.sum(scaled, axis=-1, keepdims=True) * inverse
    second = jnp.sum(scaled * unit, axis=-1, keepdims=True) * inverse
    return factor * (scaled - first - unit * second)


def backward_kernel(side, halves, own_lanes, *refs):
    refs = list(refs)
    me_ref, aux = refs.pop(0), refs.pop(0)
    up_a, up_b = refs.pop(0), refs.pop(0)
    x_ref, w_ref, mid_ref, out_ref, u1, u2, u3, fac, pat = refs[:9]
    x_grad, grads, grads_low, out_grads = refs[9:13]
    up, sg, eg, turned, field, dense, accum = refs[13:]
    slots = x_ref.shape[0]
    chan, mid = out_ref.shape[1], w_ref.shape[0]
    held = grads.shape[0]
    reduce_end, conv_end, expand_end, mid_end, end = columns(chan, mid)
    pad = pad_of(side)
    me = me_ref[0]
    own_rows = pl.ds(pl.multiple_of(me * held, held), held)

    if halves:
        core = me & 1
        half = up_a.shape[1]
        up[:, pl.ds(pl.multiple_of(core * half, half), half)] = up_a[...].astype(F32)
        up[:, pl.ds(pl.multiple_of((1 - core) * half, half), half)] = up_b[...].astype(F32)
    else:
        up[...] = dot_nn(up_a[...], up_b[...])
    clear_edges(field, side, slots)

    def third(rows, start, carry):
        gain_acc, bias_acc = carry
        unit = u3[rows, :]
        summed = unit * out_ref[0:1, :] + out_ref[1:2, :] + x_ref[rows, :].astype(F32)
        grad = silu_slope(summed) * (up[rows, :] * aux[rows, 0:1])
        sg[rows, :] = grad
        eg[rows, :] = norm_back(grad, unit, fac[2, rows, 0:1], out_ref[0:1, :]).astype(BF16)
        return gain_acc + fold(grad * unit), bias_acc + fold(grad)

    zero = jnp.zeros((8, chan), F32)
    gain_acc, bias_acc = chunked(slots, 16, third, (zero, zero))
    out_grads[...] = jnp.zeros_like(out_grads)
    out_grads[0:1, :] = jnp.sum(gain_acc, axis=0, keepdims=True)
    out_grads[1:2, :] = jnp.sum(bias_acc, axis=0, keepdims=True)

    dense[...] = silu(u2[...] * mid_ref[2:3, :] + mid_ref[3:4, :])
    turned[...] = dense[...].T
    grads[:, conv_end:expand_end] = dot_nn(turned[own_rows, :].astype(BF16), eg[...])
    dense[...] = dot_nt(eg[...], w_ref[:, conv_end:expand_end])
    small = jnp.zeros((8, mid), F32)

    def second(rows, start, carry):
        gain_sum, bias_sum = carry
        unit = u2[rows, :]
        grad = silu_slope(unit * mid_ref[2:3, :] + mid_ref[3:4, :]) * dense[rows, :]
        back = norm_back(grad, unit, fac[1, rows, 0:1], mid_ref[2:3, :])
        field[1, pl.ds(pad + start, unit.shape[0]), :] = back
        return gain_sum + fold(grad * unit), bias_sum + fold(grad)

    gain_two, bias_two = chunked(slots, 48, second, (small, small))
    shift_columns(field, side, slots, aux)
    turned[...] = field[1, pad : pad + slots, :].T
    grads[:, reduce_end:conv_end] = dot_nn(turned[own_rows, :].astype(BF16), pat[...])
    for j, (rise, step) in enumerate(OFFSETS):
        at = reduce_end + j * mid
        term = dot_nn(tap(field, side, slots, -rise, -step), w_ref[:, at : at + mid])
        dense[...] = term if j == 0 else dense[...] + term

    def first(rows, start, carry):
        gain_sum, bias_sum = carry
        unit = u1[rows, :]
        grad = silu_slope(unit * mid_ref[0:1, :] + mid_ref[1:2, :]) * (dense[rows, :] * aux[rows, 0:1])
        dense[rows, :] = norm_back(grad, unit, fac[0, rows, 0:1], mid_ref[0:1, :])
        return gain_sum + fold(grad * unit), bias_sum + fold(grad)

    gain_one, bias_one = chunked(slots, 48, first, (small, small))
    turned[...] = dense[...].T
    grads[:, 0:reduce_end] = dot_nn(turned[own_rows, :].astype(BF16), x_ref[...])
    low = dense[...].astype(BF16)
    if own_lanes:
        lanes = pl.ds(pl.multiple_of(me * own_lanes, own_lanes), own_lanes)
        x_grad[...] = (dot_nn(low, w_ref[:, lanes]) + sg[:, lanes]).astype(x_grad.dtype)
    else:
        x_grad[...] = (dot_nn(low, w_ref[:, 0:reduce_end]) + sg[...]).astype(x_grad.dtype)

    accum[...] = jnp.zeros_like(accum)
    for q, value in enumerate((gain_one, bias_one, gain_two, bias_two)):
        accum[q : q + 1, :] = jnp.sum(value, axis=0, keepdims=True)
    turned[:, 0:LANES] = accum[...].T
    grads[:, expand_end:mid_end] = turned[own_rows, 0:LANES]
    grads[:, mid_end:end] = jnp.zeros((held, LANES), F32)
    if chan // (mid // held) == LANES:
        lanes = pl.ds(pl.multiple_of(me * LANES, LANES), LANES)
        grads[0:8, mid_end:end] = out_grads[:, lanes]
    grads_low[...] = grads[...].astype(BF16)


def block_backward(side, held, me, aux, upstream, saved, own_lanes, x_dtype):
    slots, chan = saved[0].shape
    mid = saved[1].shape[0]
    halves = upstream[0].shape[0] == slots and upstream[0].shape[1] * 2 == chan
    end = columns(chan, mid)[-1]
    outs = [
        sds((slots, own_lanes or chan), x_dtype),
        sds((held, end), F32),
        sds((held, end), BF16),
        sds((8, chan), F32),
    ]
    scratch = [
        pltpu.VMEM((slots, chan), F32),
        pltpu.VMEM((slots, chan), F32),
        pltpu.VMEM((slots, chan), BF16),
        pltpu.VMEM((mid, slots), F32),
        pltpu.VMEM((3, slots + 2 * pad_of(side), mid), F32),
        pltpu.VMEM((slots, mid), F32),
        pltpu.VMEM((LANES, mid), F32),
    ]
    return call(
        functools.partial(backward_kernel, side, halves, own_lanes),
        outs,
        [SMEM] + [VMEM] * (3 + len(saved)),
        scratch,
        flops=3 * slots * mid * (2 * chan + TAPS * mid),
        moved=40 * slots * chan,
        vmem=40,
    )(me, aux, *upstream, *saved)


GELU_A = 0.7978845608028654
GELU_B = 0.044715


def gelu_both(value):
    square = value * value
    curve = jnp.tanh(GELU_A * (value + GELU_B * value * square))
    slope = 0.5 * (1.0 + curve) + 0.5 * value * (1.0 - curve * curve) * (
        GELU_A * (1.0 + 3.0 * GELU_B * square)
    )
    return 0.5 * value * (1.0 + curve), slope


def act_grad_kernel(count, me_ref, w2, *refs):
    pieces, out = refs[:count], refs[count]
    width = pieces[0].shape[1]
    for r, piece in enumerate(pieces):
        lanes = pl.ds(pl.multiple_of((me_ref[0] ^ r) * width, width), width)
        term = dot_nt(piece[...], w2[:, lanes])
        out[...] = term if r == 0 else out[...] + term


def act_grad(me, w2, pieces):
    rows, width = pieces[0].shape
    hidden = w2.shape[0]
    return call(
        functools.partial(act_grad_kernel, len(pieces)),
        sds((rows, hidden), F32),
        [SMEM] + [VMEM] * (1 + len(pieces)),
        vmem=24,
        flops=2 * rows * hidden * w2.shape[1],
        moved=2 * hidden * w2.shape[1],
    )(me, w2, *pieces)


def readout_kernel(me_ref, readin, w1, b1, grad, act, mine, theirs, full):
    hidden = dot_nn(readin[...], w1[...]) + b1[...]
    value, slope = gelu_both(hidden)
    act[...] = value.astype(BF16)
    full[...] = dot_nt((slope * grad[...]).astype(BF16), w1[...])
    half = mine.shape[1]
    core = me_ref[0] & 1
    mine[...] = full[:, pl.ds(pl.multiple_of(core * half, half), half)]
    theirs[...] = full[:, pl.ds(pl.multiple_of((1 - core) * half, half), half)].astype(BF16)


def readout(me, readin, w1, b1, grad):
    rows, chan = readin.shape
    hidden = w1.shape[1]
    return call(
        readout_kernel,
        [
            sds((rows, hidden), BF16),
            sds((rows, chan // 2), F32),
            sds((rows, chan // 2), BF16),
        ],
        [SMEM] + [VMEM] * 4,
        [pltpu.VMEM((rows, chan), F32)],
        vmem=16,
        flops=4 * rows * hidden * chan,
        moved=2 * hidden * chan,
    )(me, readin, w1, b1, grad)


def tokens_kernel(me_ref, act, w2, keep, send):
    width = keep.shape[2]
    for q in range(keep.shape[0]):
        for odd, out in ((0, keep), (1, send)):
            lanes = pl.ds(pl.multiple_of((me_ref[0] ^ (2 * q + odd)) * width, width), width)
            out[q] = dot_nn(act[...], w2[:, lanes]).astype(out.dtype)


def tokens_share(me, act, w2, n):
    rows, hidden = act.shape
    width = w2.shape[1] // n
    return call(
        tokens_kernel,
        [sds((n // 2, rows, width), F32), sds((n // 2, rows, width), BF16)],
        [SMEM] + [VMEM] * 2,
        vmem=24,
        flops=2 * rows * hidden * w2.shape[1],
        moved=2 * hidden * w2.shape[1],
    )(me, act, w2)


def hidden_kernel(count, b1, w1, grad, grad_rest, *refs):
    readins = refs[:count]
    act, w1_grad, b1_grad, stacked, low = refs[count:]
    rows = readins[0].shape[0]
    for m, readin in enumerate(readins):
        stacked[m * rows : (m + 1) * rows, :] = readin[...]
    hidden = dot_nn(stacked[...], w1[...]) + b1[...]
    value, slope = gelu_both(hidden)
    act[...] = value.astype(BF16)
    low[0:rows, :] = (slope[0:rows] * grad[...]).astype(BF16)
    low[rows:, :] = (slope[rows:] * grad_rest[...]).astype(BF16)
    b1_grad[...] = jnp.sum(low[...].astype(F32), axis=0, keepdims=True)
    w1_grad[...] = dot_tn(stacked[...], low[...])


def hidden_all(b1, w1, grad, grad_rest, readins):
    rows, chan = readins[0].shape
    total = rows * len(readins)
    hidden = w1.shape[1]
    return call(
        functools.partial(hidden_kernel, len(readins)),
        [sds((total, hidden), BF16), sds((chan, hidden), F32), sds((1, hidden), F32)],
        [VMEM] * (4 + len(readins)),
        [pltpu.VMEM((total, chan), BF16), pltpu.VMEM((total, hidden), BF16)],
        vmem=24,
        flops=4 * total * hidden * chan,
        moved=8 * hidden * chan,
    )(b1, w1, grad, grad_rest, *readins)


def w2_kernel(count, me_ref, act, *refs):
    own, rest = refs[:count], refs[count : 2 * count]
    out, b2_grad, buffer, both, sems = refs[2 * count :]
    rows, width = own[0].shape
    turned = act[...].astype(F32).T.astype(BF16)
    copies = []
    for r in range(count):
        slot = r % 2
        if r >= 2:
            copies[r - 2].wait()
        both[0:rows, :] = own[r][...]
        both[rows:, :] = rest[r][...]
        if r == 0:
            b2_grad[...] = jnp.sum(both[...].astype(F32), axis=0, keepdims=True)
        buffer[slot] = dot_nn(turned, both[...])
        lanes = pl.ds(pl.multiple_of((me_ref[0] ^ r) * width, width), width)
        copy = pltpu.make_async_copy(buffer.at[slot], out.at[:, lanes], sems.at[slot])
        copy.start()
        copies.append(copy)
    for copy in copies[-2:]:
        copy.wait()


def w2_gradient(me, act, own, rest):
    total, hidden = act.shape
    rows, width = own[0].shape
    n = len(own)
    return call(
        functools.partial(w2_kernel, n),
        [sds((hidden, width * n), F32), sds((1, width), F32)],
        [SMEM] + [VMEM] * (1 + 2 * n),
        [
            pltpu.VMEM((2, hidden, width), F32),
            pltpu.VMEM((total, width), BF16),
            pltpu.SemaphoreType.DMA((2,)),
        ],
        [HBM, VMEM],
        vmem=24,
        flops=2 * total * hidden * width * n,
        moved=4 * hidden * width * n,
    )(me, act, *own, *rest)


def finish_kernel(count, *refs):
    early, late = refs[:count], refs[count : 2 * count]
    red, conv, exp, mid_gain, mid_bias, out_gain, out_bias, scr = refs[2 * count :]
    chan, mid = red.shape[2], conv.shape[3]
    held = red.shape[1]
    reduce_end, conv_end, expand_end, mid_end, end = columns(chan, mid)
    for k, parts in enumerate((early, late)):

        def summed(start, stop):
            value = parts[0][:, start:stop]
            for part in parts[1:]:
                value = value + part[:, start:stop].astype(F32)
            return value

        red[k] = summed(0, reduce_end)
        for j in range(TAPS):
            conv[k, j] = summed(reduce_end + j * mid, reduce_end + (j + 1) * mid)
        exp[k] = summed(conv_end, expand_end)
        scr[...] = jnp.zeros_like(scr)
        scr[0:held, :] = summed(expand_end, mid_end)
        flat = scr[...].T
        for which in range(2):
            mid_gain[k, which : which + 1, :] = flat[2 * which : 2 * which + 1, 0:held]
            mid_bias[k, which : which + 1, :] = flat[2 * which + 1 : 2 * which + 2, 0:held]
        block = summed(mid_end, end)
        out_gain[k : k + 1, :] = block[0:1, 0 : out_gain.shape[1]]
        out_bias[k : k + 1, :] = block[1:2, 0 : out_bias.shape[1]]


def finish(early, late, chan, mid, share):
    held = early[0].shape[0]
    outs = [
        sds((2, held, chan), F32),
        sds((2, TAPS, held, mid), F32),
        sds((2, held, chan), F32),
        sds((2, 2, held), F32),
        sds((2, 2, held), F32),
        sds((2, share), F32),
        sds((2, share), F32),
    ]
    return call(
        functools.partial(finish_kernel, len(early)),
        outs,
        [VMEM] * (2 * len(early)),
        [pltpu.VMEM((LANES, LANES), F32)],
        vmem=16,
        flops=8 * held * chan,
        moved=40 * held * chan,
    )(*early, *late)


def pool_table(grid):
    target = jnp.arange(POOLED, dtype=jnp.int32)
    place = jnp.arange(GRID, dtype=jnp.int32)
    begin = target * grid // POOLED
    ending = ((target + 1) * grid + POOLED - 1) // POOLED
    inside = (place[None, :] >= begin[:, None]) & (place[None, :] < ending[:, None])
    return inside.astype(F32) / (ending - begin)[:, None].astype(F32)


def slot_facts(valid, side):
    place = jnp.arange(side * side, dtype=jnp.int32)
    left = (place % side > 0).astype(F32)
    right = (place % side < side - 1).astype(F32)
    zero = jnp.zeros_like(left)
    return jnp.stack([valid, left, right] + [zero] * 5, axis=1)


def per_device(
    features,
    grid,
    reduce_w,
    conv_w,
    expand_w,
    mid_gain,
    mid_bias,
    out_gain,
    out_bias,
    read_w1,
    read_b1,
    read_w2,
    read_b2,
    cotangent,
):
    n = lax.axis_size("ch")
    chan, mid = reduce_w.shape[1], conv_w.shape[2]
    held, share = reduce_w.shape[2], features.shape[0]
    aligned = share == LANES and held % 16 == 0
    index = lax.axis_index("ch").astype(jnp.int32)
    me = index[None]

    feat = jnp.transpose(features[:, 0, :])
    cot = jnp.transpose(cotangent[:, 0, :])
    red = jnp.transpose(reduce_w, (0, 2, 1))
    conv = jnp.transpose(conv_w, (0, 1, 3, 2))

    if aligned:
        packed = [
            pack(k, feat if k == 0 else None, red, conv, expand_w, mid_gain, mid_bias, out_gain, out_bias)
            for k in range(2)
        ]
        pieces = [gather_pieces(p) for p in packed]
        whole = [None, None]
        x_whole = None
    else:
        rows = jnp.concatenate(
            [red, jnp.transpose(conv, (0, 2, 1, 3)).reshape(2, held, TAPS * mid), expand_w], axis=2
        )
        rows = lax.all_gather(rows, "ch", axis=1, tiled=True)
        mids = jnp.stack([mid_gain, mid_bias], axis=2).reshape(2, 4, held)
        mids = jnp.pad(lax.all_gather(mids, "ch", axis=2, tiled=True), ((0, 0), (0, 4), (0, 0)))
        outs = jnp.stack([out_gain, out_bias], axis=1)
        outs = jnp.pad(lax.all_gather(outs, "ch", axis=2, tiled=True), ((0, 0), (0, 6), (0, 0)))
        whole = [(rows[k], mids[k], outs[k]) for k in range(2)]
        x_whole = lax.all_gather(feat, "ch", axis=1, tiled=True)
        pieces = [None, None]

    side = jnp.arange(GRID, dtype=jnp.int32)
    inside = (side < grid[0]).astype(F32)
    facts = slot_facts((inside[:, None] * inside[None, :]).reshape(-1), GRID)
    facts_low = slot_facts(jnp.ones((POOLED * POOLED,), F32), POOLED)
    table = pool_table(grid[0])
    spread = jnp.einsum("ir,jq->ijrq", table, table).reshape(POOLED * POOLED, GRID * GRID)
    spread_back = jnp.transpose(spread).astype(BF16)
    spread = spread.astype(BF16)

    pooled, saved_first = block_forward(
        GRID, chan, mid, me, facts, spread, None, pieces[0], None if aligned else (x_whole,) + whole[0]
    )
    readin, saved_second = block_forward(
        POOLED, chan, mid, me, facts_low, None, pooled, pieces[1], None if aligned else (pooled,) + whole[1]
    )

    cot_own = gather_pieces(cot)
    own_grad = act_grad(me, read_w2, cot_own)
    bias_one = read_b1[None, :]
    act, mine, theirs = readout(me, readin, read_w1, bias_one, own_grad)

    half = (mine + ppermute_xor(theirs, "ch", 1).astype(F32)).astype(BF16)
    total = half.astype(F32)
    for r in range(2, n, 2):
        total = total + ppermute_xor(half, "ch", r).astype(F32)
    total = total.astype(BF16)
    second_grad = (total, ppermute_xor(total, "ch", 1))

    pooled_grad, late_grads, late_low, late_out = block_backward(
        POOLED, held, me, facts_low, second_grad, saved_second, 0, BF16
    )
    feat_grad, early_grads, early_low, early_out = block_backward(
        GRID, held, me, facts, (spread_back, pooled_grad), saved_first, share if aligned else 0, F32
    )

    early = [early_grads] + along_images(early_low)
    late = [late_grads] + along_images(late_low)
    red_grad, conv_grad, exp_grad, mid_gain_grad, mid_bias_grad, out_gain_grad, out_bias_grad = finish(
        early, late, chan, mid, share
    )
    if not aligned:
        feat_grad = lax.dynamic_slice_in_dim(feat_grad, index * share, share, 1)
        both = jnp.stack([early_out, late_out])
        both = lax.dynamic_slice_in_dim(both, index * share, share, 2)
        both = lax.psum(both.astype(BF16), "img").astype(F32)
        out_gain_grad, out_bias_grad = both[:, 0], both[:, 1]

    keep, send = tokens_share(me, act, read_w2, n)
    got = ppermute_xor(send, "ch", 1)
    parts = [keep[q] + got[q].astype(F32) for q in range(n // 2)]
    tokens = parts[0]
    for q in range(1, n // 2):
        tokens = tokens + ppermute_xor(parts[q].astype(BF16), "ch", 2 * q).astype(F32)
    tokens = (tokens + read_b2[None, :]).astype(BF16)

    cot_rest = gather_pieces(jnp.concatenate(along_images(cot), axis=0))
    rest_grad = act_grad(me, read_w2, cot_rest)
    readins = [readin] + along_images(readin)
    act_all, w1_grad, b1_grad = hidden_all(bias_one, read_w1, own_grad, rest_grad, readins)
    w2_grad, b2_grad = w2_gradient(me, act_all, cot_own, cot_rest)

    return (
        jnp.transpose(tokens)[:, None, :],
        jnp.transpose(feat_grad)[:, None, :],
        jnp.transpose(red_grad, (0, 2, 1)),
        jnp.transpose(conv_grad, (0, 1, 3, 2)),
        exp_grad,
        mid_gain_grad,
        mid_bias_grad,
        out_gain_grad,
        out_bias_grad,
        w1_grad,
        b1_grad[0],
        w2_grad,
        b2_grad[0],
    )


def solution(mesh):
    return jax.shard_map(
        per_device,
        mesh=mesh,
        in_specs=(
            P("ch", "img", None),
            P("img"),
            P(None, None, "ch"),
            P(None, None, None, "ch"),
            P(None, "ch", None),
            P(None, None, "ch"),
            P(None, None, "ch"),
            P(None, "ch"),
            P(None, "ch"),
            P(None, "ch"),
            P("ch"),
            P("ch", None),
            P("ch"),
            P("ch", "img", None),
        ),
        out_specs=(
            P("ch", "img", None),
            P("ch", "img", None),
            P(None, None, "ch"),
            P(None, None, None, "ch"),
            P(None, "ch", None),
            P(None, None, "ch"),
            P(None, None, "ch"),
            P(None, "ch"),
            P(None, "ch"),
            P(None, "ch"),
            P("ch"),
            P("ch", None),
            P("ch"),
        ),
        check_vma=False,
    )
```

```python
import functools

import jax
import jax.numpy as jnp
from jax import lax
from jax.experimental import pallas as pl
from jax.experimental.pallas import tpu as pltpu
from jax.sharding import PartitionSpec as P

GRID = 24
POOLED = 12
EPSILON = 1e-06
OFFSETS = [(-1, -1), (-1, 0), (-1, 1), (0, -1), (0, 0), (0, 1), (1, -1), (1, 0), (1, 1)]
TAPS = len(OFFSETS)
LANES = 128
BF16 = jnp.bfloat16
F32 = jnp.float32
SMEM = pl.BlockSpec(memory_space=pltpu.SMEM)
ANY = pl.BlockSpec(memory_space=pl.ANY)


def dot_nn(left, right):
    return lax.dot_general(left, right, (((1,), (0,)), ((), ())), preferred_element_type=F32)


def dot_nt(left, right):
    return lax.dot_general(left, right, (((1,), (1,)), ((), ())), preferred_element_type=F32)


def dot_tn(left, right):
    return lax.dot_general(left, right, (((0,), (0,)), ((), ())), preferred_element_type=F32)


def sds(shape, dtype):
    return jax.ShapeDtypeStruct(tuple(shape), dtype)


class Inward:
    def __init__(self, source, buffer, sem):
        self.copy = pltpu.make_async_copy(source, buffer, sem)
        self.buffer, self.waited = buffer, False
        self.copy.start()

    def __call__(self):
        if not self.waited:
            self.copy.wait()
            self.waited = True
        return self.buffer


class Outward:
    def __init__(self, target, buffer, sem):
        self.copy = pltpu.make_async_copy(buffer, target, sem)
        self.buffer, self.sent = buffer, False

    def __call__(self):
        return self.buffer

    def send(self):
        if not self.sent:
            self.copy.start()
            self.sent = True


def call(body, outs, scalars, args, scratch=(), vmem=60, flops=0, moved=0, plain=(), after=()):
    count = (len(scalars), len(args), len(plain), len(after), len(outs))

    def kernel(*refs):
        refs = list(refs)

        def take(k):
            got = refs[:k]
            del refs[:k]
            return got

        scalar_refs, sources, plain_refs, _, targets = [take(k) for k in count]
        in_buffers, out_buffers = take(len(args)), take(len(outs))
        in_sems = refs.pop(0) if args else None
        out_sems = refs.pop(0)
        inward = [Inward(s, b, in_sems.at[i]) for i, (s, b) in enumerate(zip(sources, in_buffers))]
        outward = [Outward(t, b, out_sems.at[i]) for i, (t, b) in enumerate(zip(targets, out_buffers))]
        body(scalar_refs, inward, outward, plain_refs, *refs)
        for item in inward:
            item()
        for item in outward:
            item.send()
        for item in outward:
            item.copy.wait()

    shapes = [pltpu.VMEM(x.shape, x.dtype) for x in list(args) + list(outs)]
    sems = ([pltpu.SemaphoreType.DMA((len(args),))] if args else []) + [
        pltpu.SemaphoreType.DMA((len(outs),))
    ]
    return pl.pallas_call(
        kernel,
        out_shape=list(outs),
        in_specs=[SMEM] * len(scalars) + [ANY] * (len(args) + len(plain) + len(after)),
        out_specs=[ANY] * len(outs),
        scratch_shapes=shapes + sems + list(scratch),
        compiler_params=pltpu.CompilerParams(vmem_limit_bytes=vmem << 20),
        cost_estimate=pl.CostEstimate(flops=flops, bytes_accessed=moved, transcendentals=0),
    )(*scalars, *args, *plain, *after)


def gate(values, *after):
    def nothing(*refs):
        pass

    return pl.pallas_call(
        nothing,
        out_shape=[sds(v.shape, v.dtype) for v in values],
        in_specs=[ANY] * (len(values) + len(after)),
        out_specs=[ANY] * len(values),
        input_output_aliases={i: i for i in range(len(values))},
    )(*values, *after)


def join_body(scalars, ins, outs, plain):
    at = 0
    for item in ins:
        rows = item.buffer.shape[0]
        outs[0]()[at : at + rows, :] = item()[...]
        at += rows


def join(*parts, after=()):
    rows = sum(x.shape[0] for x in parts)
    shape = sds((rows, parts[0].shape[1]), parts[0].dtype)
    return call(join_body, [shape], [], list(parts), after=after)[0]


def add_body(scalars, ins, outs, plain):
    outs[0]()[...] = (ins[0]()[...].astype(F32) + ins[1]()[...].astype(F32)).astype(BF16)


def add(left, right, after=()):
    return call(add_body, [sds(left.shape, BF16)], [], [left, right], after=after)[0]


def ppermute_xor(x, axis, mask):
    return lax.ppermute(x, axis, [(i, i ^ mask) for i in range(lax.axis_size(axis))])


def neighbours(x):
    n = lax.axis_size("ch")
    return {r: ppermute_xor(x, "ch", r) for r in range(n - 2, 0, -2)}


def with_cores(x, far):
    n = lax.axis_size("ch")
    pieces = [None] * n
    for r in range(0, n, 2):
        pieces[r] = far[r] if r else x
        pieces[r + 1] = ppermute_xor(pieces[r], "ch", 1)
    return pieces


def along_images(x):
    return [ppermute_xor(x, "img", m) for m in range(1, lax.axis_size("img"))]


def rows_of(value, index, count):
    return value[pl.ds(pl.multiple_of(index * count, count), count), :]


def half_of(value, second, count):
    return jnp.where(second == 1, value[count : 2 * count, :], value[0:count, :])


def columns(chan, mid):
    reduce_end = chan
    conv_end = reduce_end + TAPS * mid
    expand_end = conv_end + chan
    return reduce_end, conv_end, expand_end, expand_end + LANES, expand_end + 2 * LANES


def split_low(value):
    high = value.astype(BF16).astype(F32)
    return high, value - high


def pack_body(layer, scalars, ins, outs, plain, scr, *bufs):
    feat, mid_gain, mid_bias, out_gain, out_bias = ins
    red, conv, exp = plain
    red_buf, conv_buf, exp_buf, sems = bufs
    copies = [
        pltpu.make_async_copy(source.at[layer], buffer, sems.at[i])
        for i, (source, buffer) in enumerate(((red, red_buf), (conv, conv_buf), (exp, exp_buf)))
    ]
    for copy in copies:
        copy.start()
    packet = outs[0]()
    held, chan, mid = red_buf.shape[0], red_buf.shape[1], conv_buf.shape[2]
    reduce_end, conv_end, expand_end, mid_end, end = columns(chan, mid)
    scr[...] = jnp.zeros_like(scr)
    for which in range(2):
        for kind, ref in enumerate((mid_gain(), mid_bias())):
            high, low = split_low(ref[layer, which : which + 1, :])
            at = 4 * which + 2 * kind
            scr[at : at + 1, 0:held] = high
            scr[at + 1 : at + 2, 0:held] = low
    packet[:, expand_end:mid_end] = scr[...].T[0:held, :].astype(BF16)
    scr[...] = jnp.zeros_like(scr)
    for kind, ref in enumerate((out_gain(), out_bias())):
        high, low = split_low(ref[layer : layer + 1, :])
        scr[2 * kind : 2 * kind + 1, :] = high
        scr[2 * kind + 1 : 2 * kind + 2, :] = low
    packet[:, mid_end:end] = scr[0:held, :].astype(BF16)
    feat = feat()
    if layer == 0:
        for b in range(feat.shape[0] // held):
            packet[:, end + b * LANES : end + (b + 1) * LANES] = feat[b * held : (b + 1) * held, :]
    else:
        outs[1]()[...] = feat[...]
    for copy in copies:
        copy.wait()
    packet[:, 0:reduce_end] = red_buf[...]
    for j in range(TAPS):
        packet[:, reduce_end + j * mid : reduce_end + (j + 1) * mid] = conv_buf[j]
    packet[:, conv_end:expand_end] = exp_buf[...]


def pack(layer, extra, red, conv, exp, mid_gain, mid_bias, out_gain, out_bias, after=()):
    held, chan = red.shape[1:]
    mid = conv.shape[3]
    width = columns(chan, mid)[-1]
    if layer:
        outs = [sds((held, width), BF16), sds(extra.shape, BF16)]
    else:
        width += extra.shape[0] * extra.shape[1] // held
        outs = [sds((held, width), BF16)]
    return call(
        functools.partial(pack_body, layer),
        outs,
        [],
        [extra, mid_gain, mid_bias, out_gain, out_bias],
        [
            pltpu.VMEM((LANES, LANES), F32),
            pltpu.VMEM(red.shape[1:], BF16),
            pltpu.VMEM(conv.shape[1:], BF16),
            pltpu.VMEM(exp.shape[1:], BF16),
            pltpu.SemaphoreType.DMA((3,)),
        ],
        moved=2 * held * width * 2,
        plain=[red, conv, exp],
        after=after,
    )


def assemble(me, pieces, x_ref, w_ref, mid_ref, out_ref, stage, scr, sems):
    held = pieces[0].shape[0]
    chan, mid = out_ref.shape[1], w_ref.shape[0]
    reduce_end, conv_end, expand_end, mid_end, end = columns(chan, mid)
    width = stage.shape[2]
    copies, weights = [], []
    for r, piece in enumerate(pieces):
        copies.append(
            pltpu.make_async_copy(piece.at[:, expand_end : expand_end + width], stage.at[r], sems.at[0, r])
        )
        copies[-1].start()
    for r, piece in enumerate(pieces):
        rows = pl.ds(pl.multiple_of((me ^ r) * held, held), held)
        weights.append(pltpu.make_async_copy(piece.at[:, 0:expand_end], w_ref.at[rows, :], sems.at[1, r]))
        weights[-1].start()
    for r in range(len(pieces)):
        copies[r].wait()
        rows = pl.ds(pl.multiple_of((me ^ r) * held, held), held)
        lanes = pl.ds(pl.multiple_of((me ^ r) * LANES, LANES), LANES)
        scr[rows, :] = stage[r, :, 0:LANES].astype(F32)
        block = stage[r, :, LANES : 2 * LANES].astype(F32)
        out_ref[0:1, lanes] = block[0:1, :] + block[1:2, :]
        out_ref[1:2, lanes] = block[2:3, :] + block[3:4, :]
        for b in range(width // LANES - 2):
            at = (b + 2) * LANES
            x_ref[b * held : (b + 1) * held, lanes] = stage[r, :, at : at + LANES]
    flat = scr[...].T
    for q in range(4):
        mid_ref[q : q + 1, :] = flat[2 * q : 2 * q + 1, :] + flat[2 * q + 1 : 2 * q + 2, :]
    for copy in weights:
        copy.wait()


def sigmoid(value):
    return 0.5 * jnp.tanh(0.5 * value) + 0.5


def silu(value):
    return value * sigmoid(value)


def silu_slope(value):
    gate = sigmoid(value)
    return gate * (1.0 + value * (1.0 - gate))


def unit_of(values):
    inverse = 1.0 / values.shape[-1]
    center = jnp.sum(values, axis=-1, keepdims=True) * inverse
    spread = jnp.sum(values * values, axis=-1, keepdims=True) * inverse - center * center
    factor = lax.rsqrt(spread + EPSILON)
    return (values - center) * factor, factor


def chunked(slots, body, carry=None):
    return body(slice(0, slots), 0, carry)


def pad_of(side):
    return -(-(side + 1) // 16) * 16


def shift_columns(field, side, slots, aux_ref):
    pad = pad_of(side)
    field[0, pad : pad + slots, :] = field[1, pad - 1 : pad - 1 + slots, :] * aux_ref[:, 1:2]
    field[2, pad : pad + slots, :] = field[1, pad + 1 : pad + 1 + slots, :] * aux_ref[:, 2:3]


def clear_edges(field, side, slots):
    pad = pad_of(side)
    for k in range(3):
        field[k, 0:pad, :] = jnp.zeros((pad, field.shape[2]), F32)
        field[k, pad + slots : pad + slots + pad, :] = jnp.zeros((pad, field.shape[2]), F32)


def tap(field, side, slots, rise, step):
    at = pad_of(side) + rise * side
    return field[step + 1, at : at + slots, :].astype(BF16)


def forward_body(side, aux, x_ref, w_ref, mid_ref, out_ref, keep, field, act, finish):
    u1, u2, u3, fac, pat = [item() for item in keep]
    slots = x_ref.shape[0]
    chan, mid = out_ref.shape[1], w_ref.shape[0]
    reduce_end, conv_end, expand_end, _, _ = columns(chan, mid)
    pad = pad_of(side)
    clear_edges(field, side, slots)
    u1[...] = dot_nt(x_ref[...], w_ref[:, 0:reduce_end])

    def first(rows, start, carry):
        unit, factor = unit_of(u1[rows, :])
        u1[rows, :] = unit
        fac[rows, 0:1] = factor
        value = silu(unit * mid_ref[0:1, :] + mid_ref[1:2, :]) * aux[rows, 0:1]
        field[1, pl.ds(pad + start, unit.shape[0]), :] = value
        return carry

    chunked(slots, first)
    keep[0].send()
    shift_columns(field, side, slots, aux)
    for j, (rise, step) in enumerate(OFFSETS):
        pat[:, j * mid : (j + 1) * mid] = tap(field, side, slots, rise, step)
    keep[4].send()
    u2[...] = dot_nt(pat[...], w_ref[:, reduce_end:conv_end])

    def second(rows, start, carry):
        unit, factor = unit_of(u2[rows, :])
        u2[rows, :] = unit
        fac[rows, 1:2] = factor
        act[rows, :] = silu(unit * mid_ref[2:3, :] + mid_ref[3:4, :]).astype(BF16)
        return carry

    chunked(slots, second)
    keep[1].send()
    u3[...] = dot_nn(act[...], w_ref[:, conv_end:expand_end])

    def third(rows, start, carry):
        unit, factor = unit_of(u3[rows, :])
        u3[rows, :] = unit
        fac[rows, 2:3] = factor
        summed = unit * out_ref[0:1, :] + out_ref[1:2, :] + x_ref[rows, :].astype(F32)
        finish[rows, :] = (silu(summed) * aux[rows, 0:1]).astype(BF16)
        return carry

    chunked(slots, third)
    keep[2].send()
    keep[3].send()


def forward_kernel(side, pooling, assembled, scalars, ins, outs, plain, *scratch):
    field, act, *rest = scratch
    ins, outs = list(ins), list(outs)
    aux = ins.pop(0)()
    if pooling:
        spread, finish = ins.pop(0), rest.pop(0)
    if assembled:
        sources = [item() for item in ins]
    else:
        if pooling:
            sources = [outs.pop(0)]
        else:
            sources = [ins.pop(0)]
        sources += outs[:3]
        outs = outs[3:]
        refs = [item() for item in sources]
        assemble(scalars[0][0], plain, *refs, *rest)
        for item in sources:
            if isinstance(item, Outward):
                item.send()
        sources = refs
    result = outs[0]
    if not pooling:
        finish = result()
    forward_body(side, aux, *sources, outs[1:], field, act, finish)
    if pooling:
        result()[...] = dot_nn(spread()[...], finish[...]).astype(BF16)


def block_forward(side, chan, mid, me, aux, spread, x, pieces, assembled):
    slots = side * side
    pooling = spread is not None
    width = columns(chan, mid)[2]
    given = [aux] + ([spread] if pooling else [])
    kept = [
        sds((spread.shape[0] if pooling else slots, chan), BF16),
        sds((slots, mid), F32),
        sds((slots, mid), F32),
        sds((slots, chan), F32),
        sds((slots, LANES), F32),
        sds((slots, TAPS * mid), BF16),
    ]
    whole = [sds((mid, width), BF16), sds((8, mid), F32), sds((8, chan), F32)]
    scratch = [
        pltpu.VMEM((3, slots + 2 * pad_of(side), mid), F32),
        pltpu.VMEM((slots, mid), BF16),
    ]
    if pooling:
        scratch.append(pltpu.VMEM((slots, chan), BF16))
    plain = []
    if assembled is not None:
        args, outs = given + list(assembled), kept
    else:
        args, outs = (given, [sds((slots, chan), BF16)]) if pooling else (given + [x], [])
        outs = outs + whole + kept
        plain = list(pieces)
        held = mid // len(pieces)
        extra = 2 * LANES + (slots * LANES // held if pooling else 0)
        scratch += [
            pltpu.VMEM((len(pieces), held, extra), BF16),
            pltpu.VMEM((mid, LANES), F32),
            pltpu.SemaphoreType.DMA((2, len(pieces))),
        ]
    got = call(
        functools.partial(forward_kernel, side, pooling, assembled is not None),
        outs,
        [me],
        args,
        scratch,
        flops=2 * slots * mid * (2 * chan + TAPS * mid),
        moved=30 * slots * chan,
        plain=plain,
    )
    got = list(got)
    if assembled is not None:
        source = list(assembled)
    elif pooling:
        source, got = got[:4], got[4:]
    else:
        source, got = [x] + got[:3], got[3:]
    return got[0], source + got[1:]


def fold(value):
    return jnp.sum(value.reshape(value.shape[0] // 8, 8, value.shape[1]), axis=0)


def norm_back(upstream, unit, factor, gain):
    inverse = 1.0 / unit.shape[-1]
    scaled = upstream * gain
    first = jnp.sum(scaled, axis=-1, keepdims=True) * inverse
    second = jnp.sum(scaled * unit, axis=-1, keepdims=True) * inverse
    return factor * (scaled - first - unit * second)


def back_upper(side, me, aux, up, x_ref, w_in, mid_in, out_ref, u2_in, u3, fac, pat_in, sg, eg, turned, field, dense, accum, out_rows, grads):
    slots, chan = eg.shape
    mid = dense.shape[1]
    held = grads.shape[0]
    reduce_end, conv_end, expand_end, _, _ = columns(chan, mid)
    pad = pad_of(side)
    clear_edges(field, side, slots)

    def third(rows, start, carry):
        gain_acc, bias_acc = carry
        unit = u3[rows, :]
        summed = unit * out_ref[0:1, :] + out_ref[1:2, :] + x_ref[rows, :].astype(F32)
        grad = silu_slope(summed) * (up[rows, :] * aux[rows, 0:1])
        sg[rows, :] = grad
        eg[rows, :] = norm_back(grad, unit, fac[rows, 2:3], out_ref[0:1, :]).astype(BF16)
        return gain_acc + fold(grad * unit), bias_acc + fold(grad)

    zero = jnp.zeros((8, chan), F32)
    gain_acc, bias_acc = chunked(slots, third, (zero, zero))
    out_rows[...] = jnp.zeros_like(out_rows)
    out_rows[0:1, :] = jnp.sum(gain_acc, axis=0, keepdims=True)
    out_rows[1:2, :] = jnp.sum(bias_acc, axis=0, keepdims=True)

    u2, mid_ref, w_ref = u2_in(), mid_in(), w_in()
    dense[...] = silu(u2[...] * mid_ref[2:3, :] + mid_ref[3:4, :])
    turned[...] = dense[...].T
    grads[:, conv_end:expand_end] = dot_nn(rows_of(turned, me, held).astype(BF16), eg[...])
    dense[...] = dot_nt(eg[...], w_ref[:, conv_end:expand_end])
    small = jnp.zeros((8, mid), F32)

    def second(rows, start, carry):
        gain_sum, bias_sum = carry
        unit = u2[rows, :]
        grad = silu_slope(unit * mid_ref[2:3, :] + mid_ref[3:4, :]) * dense[rows, :]
        back = norm_back(grad, unit, fac[rows, 1:2], mid_ref[2:3, :])
        field[1, pl.ds(pad + start, unit.shape[0]), :] = back
        return gain_sum + fold(grad * unit), bias_sum + fold(grad)

    gain_two, bias_two = chunked(slots, second, (small, small))
    accum[2:3, :] = jnp.sum(gain_two, axis=0, keepdims=True)
    accum[3:4, :] = jnp.sum(bias_two, axis=0, keepdims=True)
    turned[...] = field[1, pad : pad + slots, :].T
    pat = pat_in()
    grads[:, reduce_end:conv_end] = dot_nn(rows_of(turned, me, held).astype(BF16), pat[...])


def back_lower(side, me, aux, x_ref, w_ref, mid_ref, u1_in, fac, turned, field, dense, accum, out_rows, grads, tail):
    slots, mid = dense.shape
    chan = x_ref.shape[1]
    held = grads.shape[0]
    reduce_end = columns(chan, mid)[0]
    shift_columns(field, side, slots, aux)
    for j, (rise, step) in enumerate(OFFSETS):
        at = reduce_end + j * mid
        term = dot_nn(tap(field, side, slots, -rise, -step), w_ref[:, at : at + mid])
        dense[...] = term if j == 0 else dense[...] + term
    u1 = u1_in()
    small = jnp.zeros((8, mid), F32)

    def first(rows, start, carry):
        gain_sum, bias_sum = carry
        unit = u1[rows, :]
        grad = silu_slope(unit * mid_ref[0:1, :] + mid_ref[1:2, :]) * (dense[rows, :] * aux[rows, 0:1])
        dense[rows, :] = norm_back(grad, unit, fac[rows, 0:1], mid_ref[0:1, :])
        return gain_sum + fold(grad * unit), bias_sum + fold(grad)

    gain_one, bias_one = chunked(slots, first, (small, small))
    accum[0:1, :] = jnp.sum(gain_one, axis=0, keepdims=True)
    accum[1:2, :] = jnp.sum(bias_one, axis=0, keepdims=True)
    turned[...] = dense[...].T
    grads[:, 0:reduce_end] = dot_nn(rows_of(turned, me, held).astype(BF16), x_ref[...])
    turned[:, 0:LANES] = accum[...].T
    grads[:, tail : tail + LANES] = rows_of(turned, me, held)[:, 0:LANES]
    grads[:, tail + LANES : tail + 2 * LANES] = jnp.zeros((held, LANES), F32)
    if chan // (mid // held) == LANES:
        lanes = pl.ds(pl.multiple_of(me * LANES, LANES), LANES)
        grads[0:8, tail + LANES : tail + 2 * LANES] = out_rows[:, lanes]


def split_rows(grads, plane, mine, theirs):
    count = mine.buffer.shape[0]
    theirs()[...] = half_of(grads, 1 - plane, count).astype(BF16)
    theirs.send()
    mine()[...] = half_of(grads, plane, count)
    mine.send()


def back_scratch(side, slots, chan, mid):
    return [
        pltpu.VMEM((slots, chan), F32),
        pltpu.VMEM((slots, chan), BF16),
        pltpu.VMEM((mid, slots), F32),
        pltpu.VMEM((3, slots + 2 * pad_of(side), mid), F32),
        pltpu.VMEM((slots, mid), F32),
        pltpu.VMEM((LANES, mid), F32),
    ]


def late_kernel(side, scalars, ins, outs, plain, up, grads, sg, eg, turned, field, dense, accum):
    aux, x_in, w_in, mid_in, out_in, u1_in, u2_in, u3_in, fac_in, pat_in, *pieces = ins
    x_grad, mine, theirs, out_rows = outs
    me, plane = scalars[0][0], scalars[0][1] & 1
    half = pieces[0].buffer.shape[1]
    for odd in range(2):
        core = (me & 1) ^ odd
        total = pieces[odd]()[...].astype(F32)
        for piece in pieces[odd + 2 :: 2]:
            total = total + piece()[...].astype(F32)
        up[:, pl.ds(pl.multiple_of(core * half, half), half)] = total
    aux, x_ref, out_ref, u3, fac = aux(), x_in(), out_in(), u3_in(), fac_in()
    chan, mid = eg.shape[1], dense.shape[1]
    reduce_end, _, expand_end, _, _ = columns(chan, mid)
    accum[...] = jnp.zeros_like(accum)
    back_upper(
        side, me, aux, up, x_ref, w_in, mid_in, out_ref, u2_in, u3, fac, pat_in,
        sg, eg, turned, field, dense, accum, out_rows(), grads,
    )
    back_lower(
        side, me, aux, x_ref, w_in(), mid_in(), u1_in, fac, turned, field, dense, accum, out_rows(), grads, expand_end,
    )
    split_rows(grads, plane, mine, theirs)
    x_grad()[...] = (dot_nn(dense[...].astype(BF16), w_in()[:, 0:reduce_end]) + sg[...]).astype(BF16)


def late_backward(side, held, me, aux, pieces, saved):
    slots, chan = saved[0].shape
    mid = saved[1].shape[0]
    end = columns(chan, mid)[-1]
    return call(
        functools.partial(late_kernel, side),
        [
            sds((slots, chan), BF16),
            sds((held // 2, end), F32),
            sds((held // 2, end), BF16),
            sds((8, chan), F32),
        ],
        [me],
        [aux, *saved, *pieces],
        [pltpu.VMEM((slots, chan), F32), pltpu.VMEM((held, end), F32)] + back_scratch(side, slots, chan, mid),
        flops=3 * slots * mid * (2 * chan + TAPS * mid),
        moved=40 * slots * chan,
    )


def upper_kernel(side, own_lanes, scalars, ins, outs, plain, up, grads, sg, eg, turned, field, dense, accum):
    aux, spread, pooled_grad, x_in, out_in, u3_in, fac_in, mid_in, u2_in, w_in, pat_in = ins
    mine, theirs, conv_grad, sg_own, accum_out, out_rows = outs
    me, plane = scalars[0][0], scalars[0][1] & 1
    slots = eg.shape[0]
    up[...] = dot_tn(spread()[...], pooled_grad()[...])
    aux, x_ref, out_ref, u3, fac = aux(), x_in(), out_in(), u3_in(), fac_in()
    accum[...] = jnp.zeros_like(accum)
    back_upper(
        side, me, aux, up, x_ref, w_in, mid_in, out_ref, u2_in, u3, fac, pat_in,
        sg, eg, turned, field, dense, accum, out_rows(), grads,
    )
    start = columns(eg.shape[1], dense.shape[1])[0]
    count = mine.buffer.shape[0]
    width = mine.buffer.shape[1]
    theirs()[...] = half_of(grads, 1 - plane, count)[:, start : start + width].astype(BF16)
    theirs.send()
    mine()[...] = half_of(grads, plane, count)[:, start : start + width]
    mine.send()
    pad = pad_of(side)
    conv_grad()[...] = field[1, pad : pad + slots, :]
    accum_out()[...] = accum[0:8, :]
    if own_lanes:
        sg_own()[...] = sg[:, pl.ds(pl.multiple_of(me * own_lanes, own_lanes), own_lanes)]
    else:
        sg_own()[...] = sg[...]


def upper_backward(side, held, me, aux, spread, pooled_grad, saved, own_lanes):
    x, w, mids, outs, u1, u2, u3, fac, pat = saved
    slots, chan = x.shape
    mid = w.shape[0]
    reduce_end, _, expand_end, _, end = columns(chan, mid)
    return call(
        functools.partial(upper_kernel, side, own_lanes),
        [
            sds((held // 2, expand_end - reduce_end), F32),
            sds((held // 2, expand_end - reduce_end), BF16),
            sds((slots, mid), F32),
            sds((slots, own_lanes or chan), F32),
            sds((8, mid), F32),
            sds((8, chan), F32),
        ],
        [me],
        [aux, spread, pooled_grad, x, outs, u3, fac, mids, u2, w, pat],
        [pltpu.VMEM((slots, chan), F32), pltpu.VMEM((held, end), F32)] + back_scratch(side, slots, chan, mid),
        flops=2 * slots * mid * (2 * chan + TAPS * mid),
        moved=40 * slots * chan,
    )


def lower_kernel(side, own_lanes, scalars, ins, outs, plain, turned, field, dense, accum):
    aux, conv_grad, w_in, u1_in, fac, mid_in, x_in, sg_own, accum_in, out_rows = ins
    x_grad, grads, grads_low = outs
    me = scalars[0][0]
    slots, mid = dense.shape
    pad = pad_of(side)
    clear_edges(field, side, slots)
    field[1, pad : pad + slots, :] = conv_grad()[...]
    accum[...] = jnp.zeros_like(accum)
    accum[0:8, :] = accum_in()[...]
    w_ref, x_ref = w_in(), x_in()
    reduce_end = x_ref.shape[1]
    back_lower(
        side, me, aux(), x_ref, w_ref, mid_in(), u1_in, fac(), turned, field, dense, accum, out_rows(), grads(), reduce_end,
    )
    grads_low()[...] = grads()[...].astype(BF16)
    grads_low.send()
    grads.send()
    low = dense[...].astype(BF16)
    if own_lanes:
        lanes = pl.ds(pl.multiple_of(me * own_lanes, own_lanes), own_lanes)
        x_grad()[...] = dot_nn(low, w_ref[:, lanes]) + sg_own()[...]
    else:
        x_grad()[...] = dot_nn(low, w_ref[:, 0:reduce_end]) + sg_own()[...]


def lower_backward(side, held, me, aux, upper, saved, own_lanes):
    x, w, mids, outs, u1, u2, u3, fac, pat = saved
    slots, chan = x.shape
    mid = w.shape[0]
    conv_grad, sg_own, accum, out_rows = upper
    return call(
        functools.partial(lower_kernel, side, own_lanes),
        [
            sds((slots, own_lanes or chan), F32),
            sds((held, chan + 2 * LANES), F32),
            sds((held, chan + 2 * LANES), BF16),
        ],
        [me],
        [aux, conv_grad, w, u1, fac, mids, x, sg_own, accum, out_rows],
        back_scratch(side, slots, chan, mid)[2:],
        flops=slots * mid * (2 * chan + TAPS * mid),
        moved=20 * slots * chan,
    )


GELU_A = 0.7978845608028654
GELU_B = 0.044715


def gelu_both(value):
    square = value * value
    curve = jnp.tanh(GELU_A * (value + GELU_B * value * square))
    slope = 0.5 * (1.0 + curve) + 0.5 * value * (1.0 - curve * curve) * (
        GELU_A * (1.0 + 3.0 * GELU_B * square)
    )
    return 0.5 * value * (1.0 + curve), slope


def place_pieces(me, plain, natural, sems):
    copies = []
    for r, piece in enumerate(plain):
        share = piece.shape[1]
        lanes = pl.ds(pl.multiple_of((me ^ r) * share, share), share)
        copies.append(pltpu.make_async_copy(piece, natural.at[:, lanes], sems.at[r]))
        copies[-1].start()
    return copies


def readout_kernel(placed, scalars, ins, outs, plain, full, *sems):
    readin, w1, b1, w2, *rest = ins
    act, mine, theirs, grad, half_in, *more = outs
    me = scalars[0][0]
    if placed:
        cot = more[0]()
        copies = place_pieces(me, plain, cot, sems[0])
    else:
        cot, copies = rest[0](), []
    half = full.shape[1] // 2
    core = me & 1
    lanes = pl.ds(pl.multiple_of(core * half, half), half)
    half_in()[...] = readin()[:, lanes]
    half_in.send()
    hidden = dot_nn(readin()[...], w1()[...]) + b1()[...]
    value, slope = gelu_both(hidden)
    act()[...] = value.astype(BF16)
    act.send()
    for copy in copies:
        copy.wait()
    for item in more:
        item.send()
    grad()[...] = dot_nt(cot[...], w2()[...])
    grad.send()
    full[...] = dot_nt((slope * grad()[...]).astype(BF16), w1()[...])
    theirs()[...] = full[:, pl.ds(pl.multiple_of((1 - core) * half, half), half)].astype(BF16)
    theirs.send()
    mine()[...] = full[:, lanes]


def readout(me, readin, w1, b1, w2, pieces, whole):
    rows, chan = readin.shape
    hidden, width = w2.shape
    outs = [
        sds((rows, hidden), BF16),
        sds((rows, chan // 2), F32),
        sds((rows, chan // 2), BF16),
        sds((rows, hidden), F32),
        sds((rows, chan // 2), BF16),
    ]
    args, scratch = [readin, w1, b1, w2], [pltpu.VMEM((rows, chan), F32)]
    if pieces is None:
        args.append(whole)
    else:
        outs.append(sds((rows, width), BF16))
        scratch.append(pltpu.SemaphoreType.DMA((len(pieces),)))
    got = call(
        functools.partial(readout_kernel, pieces is not None),
        outs,
        [me],
        args,
        scratch,
        flops=2 * rows * hidden * (2 * chan + width),
        moved=2 * hidden * (chan + width),
        plain=pieces or [],
    )
    return list(got) + ([whole] if pieces is None else [])


def tokens_kernel(scalars, ins, outs, plain):
    act, w2 = [item() for item in ins]
    keep, send = [item() for item in outs]
    width = keep.shape[2]
    for odd, out in ((1, send), (0, keep)):
        for q in range(keep.shape[0]):
            lanes = pl.ds(pl.multiple_of((scalars[0][0] ^ (2 * q + odd)) * width, width), width)
            out[q] = dot_nn(act[...], w2[:, lanes]).astype(out.dtype)
        outs[odd].send()


def tokens_share(me, act, w2, n):
    rows, hidden = act.shape
    width = w2.shape[1] // n
    return call(
        tokens_kernel,
        [sds((n // 2, rows, width), F32), sds((n // 2, rows, width), BF16)],
        [me],
        [act, w2],
        flops=2 * rows * hidden * w2.shape[1],
        moved=2 * hidden * w2.shape[1],
    )


def hidden_kernel(placed, scalars, ins, outs, plain, stacked, low, *sems):
    w1, b1, w2, grad, readin, *parts = ins
    act, w1_grad, b1_grad, *more = outs
    me = scalars[0][0]
    if placed:
        cot = more[0]()
        copies = place_pieces(me, plain, cot, sems[0])
    else:
        cot, copies = parts.pop()(), []
    other = parts.pop()
    half = other.buffer.shape[1]
    rows = readin.buffer.shape[0]
    lanes = [pl.ds(pl.multiple_of(((me & 1) ^ odd) * half, half), half) for odd in range(2)]
    stacked[0:rows, :] = readin()[...]
    at = rows
    for part in parts:
        count = part.buffer.shape[0]
        stacked[at : at + count, lanes[0]] = part()[...]
        at += count
    stacked[rows:, lanes[1]] = other()[...]
    hidden = dot_nn(stacked[...], w1()[...]) + b1()[...]
    value, slope = gelu_both(hidden)
    act()[...] = value.astype(BF16)
    act.send()
    low[0:rows, :] = (slope[0:rows] * grad()[...]).astype(BF16)
    for copy in copies:
        copy.wait()
    for item in more:
        item.send()
    low[rows:, :] = (slope[rows:] * dot_nt(cot[...], w2()[...])).astype(BF16)
    b1_grad()[...] = jnp.sum(low[...].astype(F32), axis=0, keepdims=True)
    w1_grad()[...] = dot_tn(stacked[...], low[...])


def hidden_all(me, b1, w1, w2, grad, readin, parts, other, pieces, whole):
    rows, chan = readin.shape
    total = rows + other.shape[0]
    hidden, width = w2.shape
    outs = [sds((total, hidden), BF16), sds((chan, hidden), F32), sds((1, hidden), F32)]
    args = [w1, b1, w2, grad, readin, *parts, other]
    scratch = [pltpu.VMEM((total, chan), BF16), pltpu.VMEM((total, hidden), BF16)]
    if pieces is None:
        args.append(whole)
    else:
        outs.append(sds((total - rows, width), BF16))
        scratch.append(pltpu.SemaphoreType.DMA((len(pieces),)))
    got = call(
        functools.partial(hidden_kernel, pieces is not None),
        outs,
        [me],
        args,
        scratch,
        flops=2 * total * hidden * (2 * chan + width),
        moved=2 * hidden * (3 * chan + width),
        plain=pieces or [],
    )
    return list(got) + ([whole] if pieces is None else [])


def w2_kernel(n, scalars, ins, outs, plain, both, buffer, sems):
    act, own, rest = [item() for item in ins]
    b2_grad = outs[0]()
    (out,) = plain[1:] if len(plain) > 1 else plain
    rows = own.shape[0]
    width = own.shape[1] // n
    turned = act[...].astype(F32).T.astype(BF16)
    lanes = pl.ds(pl.multiple_of(scalars[0][0] * width, width), width)
    b2_grad[...] = jnp.sum(own[:, lanes].astype(F32), axis=0, keepdims=True) + jnp.sum(
        rest[:, lanes].astype(F32), axis=0, keepdims=True
    )
    copies = []
    for r in range(n):
        slot = r % 2
        if r >= 2:
            copies[r - 2].wait()
        both[0:rows, :] = own[:, r * width : (r + 1) * width]
        both[rows:, :] = rest[:, r * width : (r + 1) * width]
        buffer[slot] = dot_nn(turned, both[...])
        copy = pltpu.make_async_copy(
            buffer.at[slot], out.at[:, r * width : (r + 1) * width], sems.at[slot]
        )
        copy.start()
        copies.append(copy)
    for copy in copies[-2:]:
        copy.wait()


def w2_gradient(me, act, own, rest, n):
    total, hidden = act.shape
    chan = own.shape[1]
    width = chan // n

    def kernel(me_ref, act_ref, own_ref, rest_ref, out, b2_out, *scratch):
        act_buf, own_buf, rest_buf, b2_buf, sems, out_sem, *more = scratch
        ins = [
            Inward(a, b, sems.at[i])
            for i, (a, b) in enumerate(((act_ref, act_buf), (own_ref, own_buf), (rest_ref, rest_buf)))
        ]
        b2_grad = Outward(b2_out, b2_buf, out_sem)
        w2_kernel(n, [me_ref], ins, [b2_grad], [out], *more)
        b2_grad.send()
        b2_grad.copy.wait()

    return pl.pallas_call(
        kernel,
        out_shape=[sds((hidden, chan), F32), sds((1, width), F32)],
        in_specs=[SMEM] + [ANY] * 3,
        out_specs=[ANY] * 2,
        scratch_shapes=[
            pltpu.VMEM(act.shape, BF16),
            pltpu.VMEM(own.shape, BF16),
            pltpu.VMEM(rest.shape, BF16),
            pltpu.VMEM((1, width), F32),
            pltpu.SemaphoreType.DMA((3,)),
            pltpu.SemaphoreType.DMA,
            pltpu.VMEM((total, width), BF16),
            pltpu.VMEM((2, hidden, width), F32),
            pltpu.SemaphoreType.DMA((2,)),
        ],
        compiler_params=pltpu.CompilerParams(vmem_limit_bytes=60 << 20),
        cost_estimate=pl.CostEstimate(
            flops=2 * total * hidden * chan, bytes_accessed=4 * hidden * chan, transcendentals=0
        ),
    )(me, act, own, rest)


def finish_kernel(count, scalars, ins, outs, plain, scr):
    red, conv, exp, mid_gain, mid_bias, out_gain, out_bias = [item() for item in outs]
    late, middle, parts = ins[0:2], ins[2:4], ins[4:]
    chan, mid = red.shape[2], conv.shape[3]
    held = red.shape[1]
    reduce_end, conv_end, expand_end, mid_end, end = columns(chan, mid)
    plane = scalars[0][1] & 1
    few = held // 2

    def from_pair(pair, base, k):
        mine, other = [item()[...] for item in pair]
        for odd in range(2):
            value = jnp.where(plane == odd, mine, other)
            rows = slice(odd * few, odd * few + few)
            for j in range(TAPS):
                at = reduce_end + j * mid - base
                conv[k, j, rows, :] = value[:, at : at + mid].astype(F32)
            exp[k, rows, :] = value[:, conv_end - base : expand_end - base].astype(F32)
            if base == 0:
                red[k, rows, :] = value[:, 0:reduce_end].astype(F32)
                scr[k, rows, :] = value[:, expand_end:end].astype(F32)

    scr[...] = jnp.zeros_like(scr)
    from_pair(late, 0, 1)
    from_pair(middle, reduce_end, 0)
    total = parts[0]()[...]
    for part in parts[1:]:
        total = total + part()[...].astype(F32)
    red[0] = total[:, 0:reduce_end]
    scr[0, 0:held, :] = total[:, reduce_end:]
    for k in range(2):
        flat = scr[k, :, 0:LANES].T
        for which in range(2):
            mid_gain[k, which : which + 1, :] = flat[2 * which : 2 * which + 1, 0:held]
            mid_bias[k, which : which + 1, :] = flat[2 * which + 1 : 2 * which + 2, 0:held]
        out_gain[k : k + 1, :] = scr[k, 0:1, LANES : LANES + out_gain.shape[1]]
        out_bias[k : k + 1, :] = scr[k, 1:2, LANES : LANES + out_bias.shape[1]]


def finish(me, late, middle, parts, chan, mid, share):
    held = parts[0].shape[0]
    outs = [
        sds((2, held, chan), F32),
        sds((2, TAPS, held, mid), F32),
        sds((2, held, chan), F32),
        sds((2, 2, held), F32),
        sds((2, 2, held), F32),
        sds((2, share), F32),
        sds((2, share), F32),
    ]
    return call(
        functools.partial(finish_kernel, len(parts)),
        outs,
        [me],
        [*late, *middle, *parts],
        [pltpu.VMEM((2, LANES, 2 * LANES), F32)],
        flops=8 * held * chan,
        moved=40 * held * chan,
    )


def iota(shape, dim):
    return lax.broadcasted_iota(jnp.int32, shape, dim).astype(F32)


def whole_part(value, divisor):
    return jnp.floor((value + 0.5) * (1.0 / divisor))


def table_at(target, place, extent):
    begin = whole_part(target * extent, POOLED)
    ending = whole_part((target + 1.0) * extent + (POOLED - 1), POOLED)
    inside = jnp.where((place >= begin) & (place < ending), 1.0, 0.0)
    return inside / (ending - begin)


def facts_kernel(scalars, ins, outs, plain):
    extent = scalars[0][0].astype(F32)
    for side, out in ((GRID, outs[0]), (POOLED, outs[1])):
        slots = side * side
        place = iota((slots, 1), 0)
        row = whole_part(place, side)
        column = place - row * side
        out()[:, 1:2] = jnp.where(column > 0.5, 1.0, 0.0)
        out()[:, 2:3] = jnp.where(column < side - 1.5, 1.0, 0.0)
        if side == GRID:
            out()[:, 0:1] = jnp.where((row < extent) & (column < extent), 1.0, 0.0)
        else:
            out()[:, 0:1] = jnp.ones((slots, 1), F32)
    shape = outs[2]().shape
    target, place = iota((shape[0], 1), 0), iota((1, shape[1]), 1)
    up, across = whole_part(target, POOLED), whole_part(place, GRID)
    rows = table_at(up, across, extent)
    lanes = table_at(target - up * POOLED, place - across * GRID, extent)
    outs[2]()[...] = (rows * lanes).astype(BF16)


def facts(grid):
    slots, few = GRID * GRID, POOLED * POOLED
    return call(
        facts_kernel,
        [sds((slots, LANES), F32), sds((few, LANES), F32), sds((few, slots), BF16)],
        [grid],
        [],
    )


def per_device(
    features,
    grid,
    reduce_w,
    conv_w,
    expand_w,
    mid_gain,
    mid_bias,
    out_gain,
    out_bias,
    read_w1,
    read_b1,
    read_w2,
    read_b2,
    cotangent,
):
    n = lax.axis_size("ch")
    chan, mid = reduce_w.shape[1], conv_w.shape[2]
    held, share = reduce_w.shape[2], features.shape[0]
    aligned = share == LANES and held % 16 == 0
    index = lax.axis_index("ch").astype(jnp.int32)
    planes = lax.axis_size("img")
    me = jnp.stack([index, lax.axis_index("img").astype(jnp.int32)])

    feat = jnp.transpose(features[:, 0, :])
    cot = jnp.transpose(cotangent[:, 0, :])
    red = jnp.transpose(reduce_w, (0, 2, 1))
    conv = jnp.transpose(conv_w, (0, 1, 3, 2))
    norms = (mid_gain, mid_bias, out_gain, out_bias)
    few = cot.shape[0]
    slot_facts, few_facts, spread = facts(grid)

    if aligned:
        (first_packet,) = pack(0, feat, red, conv, expand_w, *norms)
        far = neighbours(first_packet)
        second_packet, cot = pack(1, cot, red, conv, expand_w, *norms, after=[first_packet])
        first_pieces = with_cores(first_packet, far)
        (second_packet,) = gate([second_packet], *far.values())
        far = neighbours(second_packet)
        first_whole = second_whole = None
    else:
        rows = jnp.concatenate(
            [red, jnp.transpose(conv, (0, 2, 1, 3)).reshape(2, held, TAPS * mid), expand_w], axis=2
        )
        rows = lax.all_gather(rows, "ch", axis=1, tiled=True)
        mids = jnp.stack([mid_gain, mid_bias], axis=2).reshape(2, 4, held)
        mids = jnp.pad(lax.all_gather(mids, "ch", axis=2, tiled=True), ((0, 0), (0, 4), (0, 0)))
        outs = jnp.stack([out_gain, out_bias], axis=1)
        outs = jnp.pad(lax.all_gather(outs, "ch", axis=2, tiled=True), ((0, 0), (0, 6), (0, 0)))
        x_whole = lax.all_gather(feat, "ch", axis=1, tiled=True)
        first_whole = (x_whole, rows[0], mids[0], outs[0])
        second_whole = (rows[1], mids[1], outs[1])
        first_pieces = second_pieces = None

    cot_rest, held_cot = [], cot
    for mask in (1 << k for k in range(planes.bit_length() - 1)):
        cot_rest.append(ppermute_xor(held_cot, "img", mask))
        if 2 * mask < planes:
            held_cot = join(held_cot, cot_rest[-1])
    cot_rest = join(*cot_rest)

    pooled, saved_first = block_forward(
        GRID, chan, mid, me, slot_facts, spread, None, first_pieces, first_whole
    )
    if aligned:
        far = dict(zip(far, gate(list(far.values()), pooled)))
        second_pieces = with_cores(second_packet, far)
        (cot,) = gate([cot], *far.values())
        far = neighbours(cot)
    else:
        second_whole = (pooled,) + second_whole
    readin, saved_second = block_forward(
        POOLED, chan, mid, me, few_facts, None, pooled, second_pieces, second_whole
    )

    bias_one = read_b1[None, :]
    if aligned:
        far = dict(zip(far, gate(list(far.values()), readin)))
        cot_pieces, cot_own = with_cores(cot, far), None
    else:
        cot_pieces, cot_own = None, lax.all_gather(cot, "ch", axis=1, tiled=True)
    act, mine, theirs, own_grad, half_in, cot_own = readout(
        me, readin, read_w1, bias_one, read_w2, cot_pieces, cot_own
    )

    half = add(mine, ppermute_xor(theirs, "ch", 1))
    far = neighbours(half)
    keep, send = tokens_share(me, act, read_w2, n)
    far = dict(zip(far, gate(list(far.values()), send)))
    grad_pieces = with_cores(half, far)

    parts, held_in = [], half_in
    for mask in (1 << k for k in range(planes.bit_length() - 1)):
        parts.append(ppermute_xor(held_in, "img", mask))
        if 2 * mask < planes:
            held_in = join(held_in, parts[-1])

    (cot_rest,) = gate([cot_rest], *far.values())
    if aligned:
        far = neighbours(cot_rest)

    pooled_grad, late_mine, late_theirs, late_out = late_backward(
        POOLED, held, me, few_facts, grad_pieces, saved_second
    )
    late_got = ppermute_xor(late_theirs, "img", 1)
    own_lanes = share if aligned else 0
    middle_mine, middle_theirs, *upper = upper_backward(
        GRID, held, me, slot_facts, spread, pooled_grad, saved_first, own_lanes
    )
    middle_got = ppermute_xor(middle_theirs, "img", 1)
    late_half = add(late_mine, late_got, after=[upper[0]])
    late_more = [ppermute_xor(late_half, "img", 2)]
    feat_grad, last_grads, last_low = lower_backward(
        GRID, held, me, slot_facts, upper, saved_first, own_lanes
    )
    last = [last_grads] + along_images(last_low)
    middle_half = add(middle_mine, middle_got, after=[last_grads])
    middle_more = [ppermute_xor(middle_half, "img", 2)]
    late_half = add(late_half, late_more[-1], after=[last_grads])
    for mask in (1 << k for k in range(2, planes.bit_length() - 1)):
        late_half = add(late_half, ppermute_xor(late_half, "img", mask))
    late = (late_half, ppermute_xor(late_half, "img", 1))

    other = ppermute_xor(join(*parts, after=[upper[0]]), "ch", 1)
    if aligned:
        far = dict(zip(far, gate(list(far.values()), last_grads)))
        rest_pieces, cot_rest = with_cores(cot_rest, far), None
    else:
        rest_pieces, cot_rest = None, lax.all_gather(cot_rest, "ch", axis=1, tiled=True)
    act_all, w1_grad, b1_grad, cot_rest = hidden_all(
        me, bias_one, read_w1, read_w2, own_grad, readin, parts, other, rest_pieces, cot_rest
    )
    middle_half = add(middle_half, middle_more[-1], after=[act_all])
    for mask in (1 << k for k in range(2, planes.bit_length() - 1)):
        middle_half = add(middle_half, ppermute_xor(middle_half, "img", mask))
    middle = (middle_half, ppermute_xor(middle_half, "img", 1))

    got = ppermute_xor(send, "ch", 1)
    parts = [keep[q] + got[q].astype(F32) for q in range(n // 2)]
    tokens = parts[0]
    for q in range(1, n // 2):
        tokens = tokens + ppermute_xor(parts[q].astype(BF16), "ch", 2 * q).astype(F32)
    tokens = (tokens + read_b2[None, :]).astype(BF16)

    w2_grad, b2_grad = w2_gradient(me, act_all, cot_own, cot_rest, n)
    red_grad, conv_grad, exp_grad, mid_gain_grad, mid_bias_grad, out_gain_grad, out_bias_grad = finish(
        me, late, middle, last, chan, mid, share
    )
    if not aligned:
        feat_grad = lax.dynamic_slice_in_dim(feat_grad, index * share, share, 1)
        both = jnp.stack([upper[3], late_out])
        both = lax.dynamic_slice_in_dim(both, index * share, share, 2)
        both = lax.psum(both.astype(BF16), "img").astype(F32)
        out_gain_grad, out_bias_grad = both[:, 0], both[:, 1]

    return (
        jnp.transpose(tokens)[:, None, :],
        jnp.transpose(feat_grad)[:, None, :],
        jnp.transpose(red_grad, (0, 2, 1)),
        jnp.transpose(conv_grad, (0, 1, 3, 2)),
        exp_grad,
        mid_gain_grad,
        mid_bias_grad,
        out_gain_grad,
        out_bias_grad,
        w1_grad,
        b1_grad[0],
        w2_grad,
        b2_grad[0],
    )


def solution(mesh):
    return jax.shard_map(
        per_device,
        mesh=mesh,
        in_specs=(
            P("ch", "img", None),
            P("img"),
            P(None, None, "ch"),
            P(None, None, None, "ch"),
            P(None, "ch", None),
            P(None, None, "ch"),
            P(None, None, "ch"),
            P(None, "ch"),
            P(None, "ch"),
            P(None, "ch"),
            P("ch"),
            P("ch", None),
            P("ch"),
            P("ch", "img", None),
        ),
        out_specs=(
            P("ch", "img", None),
            P("ch", "img", None),
            P(None, None, "ch"),
            P(None, None, None, "ch"),
            P(None, "ch", None),
            P(None, None, "ch"),
            P(None, None, "ch"),
            P(None, "ch"),
            P(None, "ch"),
            P(None, "ch"),
            P("ch"),
            P("ch", None),
            P("ch"),
        ),
        check_vma=False,
    )
```

```python
import functools

import jax
import jax.numpy as jnp
from jax import lax
from jax.experimental import pallas as pl
from jax.experimental.pallas import tpu as pltpu
from jax.sharding import PartitionSpec as P

GRID = 24
POOLED = 12
EPSILON = 1e-06
OFFSETS = [(-1, -1), (-1, 0), (-1, 1), (0, -1), (0, 0), (0, 1), (1, -1), (1, 0), (1, 1)]
TAPS = len(OFFSETS)
LANES = 128
BF16 = jnp.bfloat16
F32 = jnp.float32
SMEM = pl.BlockSpec(memory_space=pltpu.SMEM)
ANY = pl.BlockSpec(memory_space=pl.ANY)


def dot_nn(left, right):
    return lax.dot_general(left, right, (((1,), (0,)), ((), ())), preferred_element_type=F32)


def dot_nt(left, right):
    return lax.dot_general(left, right, (((1,), (1,)), ((), ())), preferred_element_type=F32)


def dot_tn(left, right):
    return lax.dot_general(left, right, (((0,), (0,)), ((), ())), preferred_element_type=F32)


def sds(shape, dtype):
    return jax.ShapeDtypeStruct(tuple(shape), dtype)


class Inward:
    def __init__(self, source, buffer, sem):
        self.copy = pltpu.make_async_copy(source, buffer, sem)
        self.buffer, self.waited = buffer, False
        self.copy.start()

    def __call__(self):
        if not self.waited:
            self.copy.wait()
            self.waited = True
        return self.buffer


class Outward:
    def __init__(self, target, buffer, sem):
        self.copy = None if buffer is None else pltpu.make_async_copy(buffer, target, sem)
        self.target, self.buffer, self.sent = target, buffer, False

    def __call__(self):
        return self.buffer

    def send(self):
        if not self.sent:
            self.copy.start()
            self.sent = True


def call(body, outs, scalars, args, scratch=(), vmem=60, flops=0, moved=0, plain=(), after=(), direct=()):
    count = (len(scalars), len(args), len(plain), len(after), len(outs))

    def kernel(*refs):
        refs = list(refs)

        def take(k):
            got = refs[:k]
            del refs[:k]
            return got

        scalar_refs, sources, plain_refs, _, targets = [take(k) for k in count]
        in_buffers = take(len(args))
        out_buffers = [None if i in direct else refs.pop(0) for i in range(len(outs))]
        in_sems = refs.pop(0) if args else None
        out_sems = refs.pop(0)
        inward = [Inward(s, b, in_sems.at[i]) for i, (s, b) in enumerate(zip(sources, in_buffers))]
        outward = [Outward(t, b, out_sems.at[i]) for i, (t, b) in enumerate(zip(targets, out_buffers))]
        made = [item for item in outward if item.buffer is not None]
        body(scalar_refs, inward, outward, plain_refs, *refs)
        for item in inward:
            item()
        for item in made:
            item.send()
        for item in made:
            item.copy.wait()

    results = [x for i, x in enumerate(outs) if i not in direct]
    shapes = [pltpu.VMEM(x.shape, x.dtype) for x in list(args) + results]
    sems = ([pltpu.SemaphoreType.DMA((len(args),))] if args else []) + [
        pltpu.SemaphoreType.DMA((len(outs),))
    ]
    return pl.pallas_call(
        kernel,
        out_shape=list(outs),
        in_specs=[SMEM] * len(scalars) + [ANY] * (len(args) + len(plain) + len(after)),
        out_specs=[ANY] * len(outs),
        scratch_shapes=shapes + sems + list(scratch),
        compiler_params=pltpu.CompilerParams(vmem_limit_bytes=vmem << 20),
        cost_estimate=pl.CostEstimate(flops=flops, bytes_accessed=moved, transcendentals=0),
    )(*scalars, *args, *plain, *after)


def gate(values, *after):
    def nothing(*refs):
        pass

    return pl.pallas_call(
        nothing,
        out_shape=[sds(v.shape, v.dtype) for v in values],
        in_specs=[ANY] * (len(values) + len(after)),
        out_specs=[ANY] * len(values),
        input_output_aliases={i: i for i in range(len(values))},
    )(*values, *after)


def join_body(scalars, ins, outs, plain):
    at = 0
    for item in ins:
        rows = item.buffer.shape[0]
        outs[0]()[at : at + rows, :] = item()[...]
        at += rows


def join(*parts, after=()):
    rows = sum(x.shape[0] for x in parts)
    shape = sds((rows, parts[0].shape[1]), parts[0].dtype)
    return call(join_body, [shape], [], list(parts), after=after)[0]


def ppermute_xor(x, axis, mask):
    return lax.ppermute(x, axis, [(i, i ^ mask) for i in range(lax.axis_size(axis))])


def neighbours(x):
    n = lax.axis_size("ch")
    return {r: ppermute_xor(x, "ch", r) for r in range(n - 2, 0, -2)}


def with_cores(x, far):
    n = lax.axis_size("ch")
    pieces = [None] * n
    for r in range(0, n, 2):
        pieces[r] = far[r] if r else x
        pieces[r + 1] = ppermute_xor(pieces[r], "ch", 1)
    return pieces


def along_images(x):
    return [ppermute_xor(x, "img", m) for m in range(1, lax.axis_size("img"))]


def pair_sum(mine, low, after):
    masks = [1 << k for k in range(lax.axis_size("img").bit_length() - 1)]
    total, got = mine, ppermute_xor(low, "img", masks[0])
    for mask in masks[1:]:
        (got,) = gate([got], after)
        total = (total.astype(F32) + got.astype(F32)).astype(BF16)
        got = ppermute_xor(total, "img", mask)
    return total, got


def summed(left, right):
    return (left.astype(F32) + right.astype(F32)).astype(BF16)


def rows_of(value, index, count):
    return value[pl.ds(pl.multiple_of(index * count, count), count), :]


def half_of(value, second, count):
    return jnp.where(second == 1, value[count : 2 * count, :], value[0:count, :])


def columns(chan, mid):
    reduce_end = chan
    conv_end = reduce_end + TAPS * mid
    expand_end = conv_end + chan
    return reduce_end, conv_end, expand_end, expand_end + LANES, expand_end + 2 * LANES


def split_low(value):
    high = value.astype(BF16).astype(F32)
    return high, value - high


def cot_block(index, width):
    per = width // LANES
    return (index // per * 16, index % per * LANES), (index % 2 * 16, index // 2 * LANES)


def pack_body(layer, scalars, ins, outs, plain, scr, *bufs):
    feat, mid_gain, mid_bias, out_gain, out_bias = ins
    red, conv, exp = plain
    red_buf, conv_buf, exp_buf, sems = bufs
    copies = [
        pltpu.make_async_copy(source.at[layer], buffer, sems.at[i])
        for i, (source, buffer) in enumerate(((red, red_buf), (conv, conv_buf), (exp, exp_buf)))
    ]
    for copy in copies:
        copy.start()
    packet = outs[0]()
    held, chan, mid = red_buf.shape[0], red_buf.shape[1], conv_buf.shape[2]
    reduce_end, conv_end, expand_end, mid_end, end = columns(chan, mid)
    scr[...] = jnp.zeros_like(scr)
    for which in range(2):
        for kind, ref in enumerate((mid_gain(), mid_bias())):
            high, low = split_low(ref[layer, which : which + 1, :])
            at = 4 * which + 2 * kind
            scr[at : at + 1, 0:held] = high
            scr[at + 1 : at + 2, 0:held] = low
    packet[:, expand_end:mid_end] = scr[...].T[0:held, :].astype(BF16)
    scr[...] = jnp.zeros_like(scr)
    for kind, ref in enumerate((out_gain(), out_bias())):
        high, low = split_low(ref[layer : layer + 1, :])
        scr[2 * kind : 2 * kind + 1, :] = high
        scr[2 * kind + 1 : 2 * kind + 2, :] = low
    packet[:, mid_end:end] = scr[0:held, :].astype(BF16)
    feat = feat()
    if layer == 0:
        for b in range(feat.shape[0] // held):
            packet[:, end + b * LANES : end + (b + 1) * LANES] = feat[b * held : (b + 1) * held, :]
    else:
        for index in range(feat.shape[0] // 16 * (feat.shape[1] // LANES)):
            (row, lane), (low_row, low_lane) = cot_block(index, feat.shape[1])
            packet[low_row : low_row + 16, end + low_lane : end + low_lane + LANES] = feat[
                row : row + 16, lane : lane + LANES
            ]
        outs[1]()[...] = feat[...]
    for copy in copies:
        copy.wait()
    packet[:, 0:reduce_end] = red_buf[...]
    for j in range(TAPS):
        packet[:, reduce_end + j * mid : reduce_end + (j + 1) * mid] = conv_buf[j]
    packet[:, conv_end:expand_end] = exp_buf[...]


def pack(layer, extra, red, conv, exp, mid_gain, mid_bias, out_gain, out_bias, after=()):
    held, chan = red.shape[1:]
    mid = conv.shape[3]
    width = columns(chan, mid)[-1] + extra.shape[0] * extra.shape[1] // held
    outs = [sds((held, width), BF16)]
    if layer:
        outs.append(sds(extra.shape, BF16))
    return call(
        functools.partial(pack_body, layer),
        outs,
        [],
        [extra, mid_gain, mid_bias, out_gain, out_bias],
        [
            pltpu.VMEM((LANES, LANES), F32),
            pltpu.VMEM(red.shape[1:], BF16),
            pltpu.VMEM(conv.shape[1:], BF16),
            pltpu.VMEM(exp.shape[1:], BF16),
            pltpu.SemaphoreType.DMA((3,)),
        ],
        moved=2 * held * width * 2,
        plain=[red, conv, exp],
        after=after,
    )


def assemble(me, pieces, x_ref, w_ref, mid_ref, out_ref, stage, scr, sems, then=()):
    held = pieces[0].shape[0]
    chan, mid = out_ref.shape[1], w_ref.shape[0]
    reduce_end, conv_end, expand_end, mid_end, end = columns(chan, mid)
    width = stage.shape[2]
    copies, weights = [], []
    for r, piece in enumerate(pieces):
        copies.append(
            pltpu.make_async_copy(piece.at[:, expand_end : expand_end + width], stage.at[r], sems.at[0, r])
        )
        copies[-1].start()
    for r, piece in enumerate(pieces):
        rows = pl.ds(pl.multiple_of((me ^ r) * held, held), held)
        weights.append(pltpu.make_async_copy(piece.at[:, 0:expand_end], w_ref.at[rows, :], sems.at[1, r]))
        weights[-1].start()
    for copy in then:
        copy.start()
    for r in range(len(pieces)):
        copies[r].wait()
        rows = pl.ds(pl.multiple_of((me ^ r) * held, held), held)
        lanes = pl.ds(pl.multiple_of((me ^ r) * LANES, LANES), LANES)
        scr[rows, :] = stage[r, :, 0:LANES].astype(F32)
        block = stage[r, :, LANES : 2 * LANES].astype(F32)
        out_ref[0:1, lanes] = block[0:1, :] + block[1:2, :]
        out_ref[1:2, lanes] = block[2:3, :] + block[3:4, :]
        for b in range(width // LANES - 2 if x_ref is not None else 0):
            at = (b + 2) * LANES
            x_ref[b * held : (b + 1) * held, lanes] = stage[r, :, at : at + LANES]
    flat = scr[...].T
    for q in range(4):
        mid_ref[q : q + 1, :] = flat[2 * q : 2 * q + 1, :] + flat[2 * q + 1 : 2 * q + 2, :]
    for copy in weights:
        copy.wait()


def sigmoid(value):
    return 0.5 * jnp.tanh(0.5 * value) + 0.5


def silu(value):
    return value * sigmoid(value)


def silu_slope(value):
    gate = sigmoid(value)
    return gate * (1.0 + value * (1.0 - gate))


def unit_of(values):
    inverse = 1.0 / values.shape[-1]
    center = jnp.sum(values, axis=-1, keepdims=True) * inverse
    spread = jnp.sum(values * values, axis=-1, keepdims=True) * inverse - center * center
    factor = lax.rsqrt(spread + EPSILON)
    return (values - center) * factor, factor


def chunked(slots, body, carry=None):
    return body(slice(0, slots), 0, carry)


def pad_of(side):
    return -(-(side + 1) // 16) * 16


def shift_columns(field, side, slots, aux_ref):
    pad = pad_of(side)
    field[0, pad : pad + slots, :] = field[1, pad - 1 : pad - 1 + slots, :] * aux_ref[:, 1:2]
    field[2, pad : pad + slots, :] = field[1, pad + 1 : pad + 1 + slots, :] * aux_ref[:, 2:3]


def clear_edges(field, side, slots):
    pad = pad_of(side)
    for k in range(3):
        field[k, 0:pad, :] = jnp.zeros((pad, field.shape[2]), F32)
        field[k, pad + slots : pad + slots + pad, :] = jnp.zeros((pad, field.shape[2]), F32)


def tap(field, side, slots, rise, step):
    at = pad_of(side) + rise * side
    return field[step + 1, at : at + slots, :].astype(BF16)


def forward_body(side, aux, x_ref, w_ref, mid_ref, out_ref, keep, field, act, finish):
    u1, u2, u3, fac, pat = [item() for item in keep]
    slots = x_ref.shape[0]
    chan, mid = out_ref.shape[1], w_ref.shape[0]
    reduce_end, conv_end, expand_end, _, _ = columns(chan, mid)
    pad = pad_of(side)
    clear_edges(field, side, slots)
    u1[...] = dot_nt(x_ref[...], w_ref[:, 0:reduce_end])

    def first(rows, start, carry):
        unit, factor = unit_of(u1[rows, :])
        u1[rows, :] = unit
        fac[rows, 0:1] = factor
        value = silu(unit * mid_ref[0:1, :] + mid_ref[1:2, :]) * aux[rows, 0:1]
        field[1, pl.ds(pad + start, unit.shape[0]), :] = value
        return carry

    chunked(slots, first)
    keep[0].send()
    shift_columns(field, side, slots, aux)
    for j, (rise, step) in enumerate(OFFSETS):
        pat[:, j * mid : (j + 1) * mid] = tap(field, side, slots, rise, step)
    keep[4].send()
    u2[...] = dot_nt(pat[...], w_ref[:, reduce_end:conv_end])

    def second(rows, start, carry):
        unit, factor = unit_of(u2[rows, :])
        u2[rows, :] = unit
        fac[rows, 1:2] = factor
        act[rows, :] = silu(unit * mid_ref[2:3, :] + mid_ref[3:4, :]).astype(BF16)
        return carry

    chunked(slots, second)
    keep[1].send()
    u3[...] = dot_nn(act[...], w_ref[:, conv_end:expand_end])

    def third(rows, start, carry):
        unit, factor = unit_of(u3[rows, :])
        u3[rows, :] = unit
        fac[rows, 2:3] = factor
        summed = unit * out_ref[0:1, :] + out_ref[1:2, :] + x_ref[rows, :].astype(F32)
        finish[rows, :] = (silu(summed) * aux[rows, 0:1]).astype(BF16)
        return carry

    chunked(slots, third)
    keep[2].send()
    keep[3].send()


def forward_kernel(side, pooling, assembled, scalars, ins, outs, plain, *scratch):
    field, act, *rest = scratch
    ins, outs = list(ins), list(outs)
    aux = ins.pop(0)()
    if pooling:
        spread, finish = ins.pop(0), rest.pop(0)
    if assembled:
        sources = [item() for item in ins]
    else:
        sources, outs = [item() for item in outs[:4]], outs[4:]
        assemble(scalars[0][0], plain, *sources, *rest)
    result = outs[0]
    if not pooling:
        finish = result()
    forward_body(side, aux, *sources, outs[1:], field, act, finish)
    if pooling:
        result()[...] = dot_nn(spread()[...], finish[...]).astype(BF16)


def kept_shapes(slots, chan, mid):
    return [
        sds((slots, mid), F32),
        sds((slots, mid), F32),
        sds((slots, chan), F32),
        sds((slots, LANES), F32),
        sds((slots, TAPS * mid), BF16),
    ]


def whole_shapes(chan, mid):
    return [sds((mid, columns(chan, mid)[2]), BF16), sds((8, mid), F32), sds((8, chan), F32)]


def forward_scratch(side, mid):
    slots = side * side
    return [
        pltpu.VMEM((3, slots + 2 * pad_of(side), mid), F32),
        pltpu.VMEM((slots, mid), BF16),
    ]


def assemble_scratch(pieces, mid, extra):
    held = mid // len(pieces)
    return [
        pltpu.VMEM((len(pieces), held, 2 * LANES + extra), BF16),
        pltpu.VMEM((mid, LANES), F32),
        pltpu.SemaphoreType.DMA((2, len(pieces))),
    ]


def block_forward(side, chan, mid, me, aux, spread, pieces, assembled):
    slots = side * side
    pooling = spread is not None
    args = [aux] + ([spread] if pooling else [])
    outs = [sds((spread.shape[0] if pooling else slots, chan), BF16)] + kept_shapes(slots, chan, mid)
    scratch = forward_scratch(side, mid)
    if pooling:
        scratch.append(pltpu.VMEM((slots, chan), BF16))
    if assembled is not None:
        args += list(assembled)
    else:
        outs = [sds((slots, chan), BF16)] + whole_shapes(chan, mid) + outs
        scratch += assemble_scratch(pieces, mid, slots * LANES * len(pieces) // mid)
    got = call(
        functools.partial(forward_kernel, side, pooling, assembled is not None),
        outs,
        [me],
        args,
        scratch,
        flops=2 * slots * mid * (2 * chan + TAPS * mid),
        moved=30 * slots * chan,
        plain=list(pieces or []),
    )
    got = list(got)
    source, got = (list(assembled), got) if assembled is not None else (got[:4], got[4:])
    return got[0], source + got[1:]


def fold(value):
    return jnp.sum(value.reshape(value.shape[0] // 8, 8, value.shape[1]), axis=0)


def norm_back(upstream, unit, factor, gain):
    inverse = 1.0 / unit.shape[-1]
    scaled = upstream * gain
    first = jnp.sum(scaled, axis=-1, keepdims=True) * inverse
    second = jnp.sum(scaled * unit, axis=-1, keepdims=True) * inverse
    return factor * (scaled - first - unit * second)


def back_upper(side, me, aux, up, x_ref, w_in, mid_in, out_ref, u2_in, u3, fac, pat_in, sg, eg, turned, field, dense, accum, out_rows, grads):
    slots, chan = eg.shape
    mid = dense.shape[1]
    held = grads.shape[0]
    reduce_end, conv_end, expand_end, _, _ = columns(chan, mid)
    pad = pad_of(side)
    clear_edges(field, side, slots)

    def third(rows, start, carry):
        gain_acc, bias_acc = carry
        unit = u3[rows, :]
        summed = unit * out_ref[0:1, :] + out_ref[1:2, :] + x_ref[rows, :].astype(F32)
        grad = silu_slope(summed) * (up[rows, :] * aux[rows, 0:1])
        sg[rows, :] = grad
        eg[rows, :] = norm_back(grad, unit, fac[rows, 2:3], out_ref[0:1, :]).astype(BF16)
        return gain_acc + fold(grad * unit), bias_acc + fold(grad)

    zero = jnp.zeros((8, chan), F32)
    gain_acc, bias_acc = chunked(slots, third, (zero, zero))
    out_rows[...] = jnp.zeros_like(out_rows)
    out_rows[0:1, :] = jnp.sum(gain_acc, axis=0, keepdims=True)
    out_rows[1:2, :] = jnp.sum(bias_acc, axis=0, keepdims=True)

    u2, mid_ref, w_ref = u2_in(), mid_in(), w_in()
    dense[...] = silu(u2[...] * mid_ref[2:3, :] + mid_ref[3:4, :])
    turned[...] = dense[...].T
    grads[:, conv_end:expand_end] = dot_nn(rows_of(turned, me, held).astype(BF16), eg[...])
    dense[...] = dot_nt(eg[...], w_ref[:, conv_end:expand_end])
    small = jnp.zeros((8, mid), F32)

    def second(rows, start, carry):
        gain_sum, bias_sum = carry
        unit = u2[rows, :]
        grad = silu_slope(unit * mid_ref[2:3, :] + mid_ref[3:4, :]) * dense[rows, :]
        back = norm_back(grad, unit, fac[rows, 1:2], mid_ref[2:3, :])
        field[1, pl.ds(pad + start, unit.shape[0]), :] = back
        return gain_sum + fold(grad * unit), bias_sum + fold(grad)

    gain_two, bias_two = chunked(slots, second, (small, small))
    accum[2:3, :] = jnp.sum(gain_two, axis=0, keepdims=True)
    accum[3:4, :] = jnp.sum(bias_two, axis=0, keepdims=True)
    turned[...] = field[1, pad : pad + slots, :].T
    pat = pat_in()
    grads[:, reduce_end:conv_end] = dot_nn(rows_of(turned, me, held).astype(BF16), pat[...])


def back_lower(side, me, aux, x_ref, w_ref, mid_ref, u1_in, fac, turned, field, dense, accum, out_rows, grads, tail):
    slots, mid = dense.shape
    chan = x_ref.shape[1]
    held = grads.shape[0]
    reduce_end = columns(chan, mid)[0]
    shift_columns(field, side, slots, aux)
    for j, (rise, step) in enumerate(OFFSETS):
        at = reduce_end + j * mid
        term = dot_nn(tap(field, side, slots, -rise, -step), w_ref[:, at : at + mid])
        dense[...] = term if j == 0 else dense[...] + term
    u1 = u1_in()
    small = jnp.zeros((8, mid), F32)

    def first(rows, start, carry):
        gain_sum, bias_sum = carry
        unit = u1[rows, :]
        grad = silu_slope(unit * mid_ref[0:1, :] + mid_ref[1:2, :]) * (dense[rows, :] * aux[rows, 0:1])
        dense[rows, :] = norm_back(grad, unit, fac[rows, 0:1], mid_ref[0:1, :])
        return gain_sum + fold(grad * unit), bias_sum + fold(grad)

    gain_one, bias_one = chunked(slots, first, (small, small))
    accum[0:1, :] = jnp.sum(gain_one, axis=0, keepdims=True)
    accum[1:2, :] = jnp.sum(bias_one, axis=0, keepdims=True)
    turned[...] = dense[...].T
    grads[:, 0:reduce_end] = dot_nn(rows_of(turned, me, held).astype(BF16), x_ref[...])
    turned[:, 0:LANES] = accum[...].T
    grads[:, tail : tail + LANES] = rows_of(turned, me, held)[:, 0:LANES]
    grads[:, tail + LANES : tail + 2 * LANES] = jnp.zeros((held, LANES), F32)
    if chan // (mid // held) == LANES:
        lanes = pl.ds(pl.multiple_of(me * LANES, LANES), LANES)
        grads[0:8, tail + LANES : tail + 2 * LANES] = out_rows[:, lanes]


def split_rows(grads, plane, mine, theirs, start):
    count, width = mine.buffer.shape
    theirs()[...] = half_of(grads, 1 - plane, count)[:, start : start + width].astype(BF16)
    theirs.send()
    mine()[...] = half_of(grads, plane, count)[:, start : start + width]
    mine.send()


def back_scratch(side, slots, chan, mid):
    return [
        pltpu.VMEM((slots, chan), F32),
        pltpu.VMEM((slots, chan), BF16),
        pltpu.VMEM((mid, slots), F32),
        pltpu.VMEM((3, slots + 2 * pad_of(side), mid), F32),
        pltpu.VMEM((slots, mid), F32),
        pltpu.VMEM((LANES, mid), F32),
    ]


def late_kernel(side, scalars, ins, outs, plain, up, grads, sg, eg, turned, field, dense, accum):
    aux, x_in, w_in, mid_in, out_in, u1_in, u2_in, u3_in, fac_in, pat_in, *pieces = ins
    x_grad, mine, theirs, out_rows = outs
    me, plane = scalars[0][0], scalars[0][1] & 1
    half = pieces[0].buffer.shape[1]
    for odd in range(2):
        core = (me & 1) ^ odd
        total = pieces[odd]()[...].astype(F32)
        for piece in pieces[odd + 2 :: 2]:
            total = total + piece()[...].astype(F32)
        up[:, pl.ds(pl.multiple_of(core * half, half), half)] = total
    aux, x_ref, out_ref, u3, fac = aux(), x_in(), out_in(), u3_in(), fac_in()
    chan, mid = eg.shape[1], dense.shape[1]
    reduce_end, _, expand_end, _, _ = columns(chan, mid)
    accum[...] = jnp.zeros_like(accum)
    back_upper(
        side, me, aux, up, x_ref, w_in, mid_in, out_ref, u2_in, u3, fac, pat_in,
        sg, eg, turned, field, dense, accum, out_rows(), grads,
    )
    back_lower(
        side, me, aux, x_ref, w_in(), mid_in(), u1_in, fac, turned, field, dense, accum, out_rows(), grads, expand_end,
    )
    split_rows(grads, plane, mine, theirs, 0)
    x_grad()[...] = (dot_nn(dense[...].astype(BF16), w_in()[:, 0:reduce_end]) + sg[...]).astype(BF16)


def late_backward(side, held, me, aux, pieces, saved):
    slots, chan = saved[0].shape
    mid = saved[1].shape[0]
    end = columns(chan, mid)[-1]
    return call(
        functools.partial(late_kernel, side),
        [
            sds((slots, chan), BF16),
            sds((held // 2, end), F32),
            sds((held // 2, end), BF16),
            sds((8, chan), F32),
        ],
        [me],
        [aux, *saved, *pieces],
        [pltpu.VMEM((slots, chan), F32), pltpu.VMEM((held, end), F32)] + back_scratch(side, slots, chan, mid),
        flops=3 * slots * mid * (2 * chan + TAPS * mid),
        moved=40 * slots * chan,
    )


def upper_kernel(side, own_lanes, scalars, ins, outs, plain, up, grads, sg, eg, turned, field, dense, accum):
    aux, spread, pooled_grad, x_in, out_in, u3_in, fac_in, mid_in, u2_in, w_in, pat_in = ins
    mine, theirs, conv_grad, sg_own, accum_out, out_rows = outs
    me, plane = scalars[0][0], scalars[0][1] & 1
    slots = eg.shape[0]
    up[...] = dot_tn(spread()[...], pooled_grad()[...])
    aux, x_ref, out_ref, u3, fac = aux(), x_in(), out_in(), u3_in(), fac_in()
    accum[...] = jnp.zeros_like(accum)
    back_upper(
        side, me, aux, up, x_ref, w_in, mid_in, out_ref, u2_in, u3, fac, pat_in,
        sg, eg, turned, field, dense, accum, out_rows(), grads,
    )
    split_rows(grads, plane, mine, theirs, columns(eg.shape[1], dense.shape[1])[0])
    pad = pad_of(side)
    conv_grad()[...] = field[1, pad : pad + slots, :]
    accum_out()[...] = accum[0:8, :]
    if own_lanes:
        sg_own()[...] = sg[:, pl.ds(pl.multiple_of(me * own_lanes, own_lanes), own_lanes)]
    else:
        sg_own()[...] = sg[...]


def upper_backward(side, held, me, aux, spread, pooled_grad, saved, own_lanes):
    x, w, mids, outs, u1, u2, u3, fac, pat = saved
    slots, chan = x.shape
    mid = w.shape[0]
    reduce_end, _, expand_end, _, end = columns(chan, mid)
    return call(
        functools.partial(upper_kernel, side, own_lanes),
        [
            sds((held // 2, expand_end - reduce_end), F32),
            sds((held // 2, expand_end - reduce_end), BF16),
            sds((slots, mid), F32),
            sds((slots, own_lanes or chan), F32),
            sds((8, mid), F32),
            sds((8, chan), F32),
        ],
        [me],
        [aux, spread, pooled_grad, x, outs, u3, fac, mids, u2, w, pat],
        [pltpu.VMEM((slots, chan), F32), pltpu.VMEM((held, end), F32)] + back_scratch(side, slots, chan, mid),
        flops=2 * slots * mid * (2 * chan + TAPS * mid),
        moved=40 * slots * chan,
    )


def lower_kernel(side, own_lanes, scalars, ins, outs, plain, turned, field, dense, accum):
    aux, conv_grad, w_in, u1_in, fac, mid_in, x_in, sg_own, accum_in, out_rows = ins
    x_grad, grads, grads_low = outs
    me = scalars[0][0]
    slots, mid = dense.shape
    pad = pad_of(side)
    clear_edges(field, side, slots)
    field[1, pad : pad + slots, :] = conv_grad()[...]
    accum[...] = jnp.zeros_like(accum)
    accum[0:8, :] = accum_in()[...]
    w_ref, x_ref = w_in(), x_in()
    reduce_end = x_ref.shape[1]
    back_lower(
        side, me, aux(), x_ref, w_ref, mid_in(), u1_in, fac(), turned, field, dense, accum, out_rows(), grads(), reduce_end,
    )
    grads_low()[...] = grads()[...].astype(BF16)
    grads_low.send()
    grads.send()
    low = dense[...].astype(BF16)
    if own_lanes:
        lanes = pl.ds(pl.multiple_of(me * own_lanes, own_lanes), own_lanes)
        x_grad()[...] = dot_nn(low, w_ref[:, lanes]) + sg_own()[...]
    else:
        x_grad()[...] = dot_nn(low, w_ref[:, 0:reduce_end]) + sg_own()[...]


def lower_backward(side, held, me, aux, upper, saved, own_lanes):
    x, w, mids, outs, u1, u2, u3, fac, pat = saved
    slots, chan = x.shape
    mid = w.shape[0]
    conv_grad, sg_own, accum, out_rows = upper
    return call(
        functools.partial(lower_kernel, side, own_lanes),
        [
            sds((slots, own_lanes or chan), F32),
            sds((held, chan + 2 * LANES), F32),
            sds((held, chan + 2 * LANES), BF16),
        ],
        [me],
        [aux, conv_grad, w, u1, fac, mids, x, sg_own, accum, out_rows],
        back_scratch(side, slots, chan, mid)[2:],
        flops=slots * mid * (2 * chan + TAPS * mid),
        moved=20 * slots * chan,
    )


GELU_A = 0.7978845608028654
GELU_B = 0.044715


def gelu_both(value):
    square = value * value
    curve = jnp.tanh(GELU_A * (value + GELU_B * value * square))
    slope = 0.5 * (1.0 + curve) + 0.5 * value * (1.0 - curve * curve) * (
        GELU_A * (1.0 + 3.0 * GELU_B * square)
    )
    return 0.5 * value * (1.0 + curve), slope


def readout_body(me, readin, w1, b1, w2, cot, outs, full):
    act, mine, theirs, grad, half_in, keep, send = outs
    half = full.shape[1] // 2
    core = me & 1
    lanes = pl.ds(pl.multiple_of(core * half, half), half)
    half_in()[...] = readin[:, lanes]
    half_in.send()
    hidden = dot_nn(readin[...], w1()[...]) + b1[...]
    value, slope = gelu_both(hidden)
    act[...] = value.astype(BF16)
    grad()[...] = dot_nt(cot()[...], w2()[...])
    grad.send()
    full[...] = dot_nt((slope * grad()[...]).astype(BF16), w1()[...])
    theirs()[...] = full[:, pl.ds(pl.multiple_of((1 - core) * half, half), half)].astype(BF16)
    theirs.send()
    mine()[...] = full[:, lanes]
    mine.send()
    width = keep.buffer.shape[2]
    for odd, out in ((1, send), (0, keep)):
        for q in range(out.buffer.shape[0]):
            lanes = pl.ds(pl.multiple_of((me ^ (2 * q + odd)) * width, width), width)
            out()[q] = dot_nn(act[...], w2()[:, lanes]).astype(BF16)
        out.send()


def readout_shapes(rows, chan, hidden, width, n):
    return [
        sds((rows, chan // 2), F32),
        sds((rows, chan // 2), BF16),
        sds((rows, hidden), F32),
        sds((rows, chan // 2), BF16),
        sds((n // 2, rows, width // n), BF16),
        sds((n // 2, rows, width // n), BF16),
    ]


def readout_kernel(scalars, ins, outs, plain, full, act):
    readin, w1, b1, w2, cot = ins
    readout_body(scalars[0][0], readin(), w1, b1(), w2, cot, [act, *outs], full)


def readout(me, readin, w1, b1, w2, cot, n):
    rows, chan = readin.shape
    return call(
        readout_kernel,
        readout_shapes(rows, chan, *w2.shape, n),
        [me],
        [readin, w1, b1, w2, cot],
        [pltpu.VMEM((rows, chan), F32), pltpu.VMEM((rows, w2.shape[0]), BF16)],
    )


class Later:
    def __init__(self, source, buffer, sem):
        self.copy, self.buffer, self.waited = pltpu.make_async_copy(source, buffer, sem), buffer, False

    def start(self):
        self.copy.start()

    def __call__(self):
        if not self.waited:
            self.copy.wait()
            self.waited = True
        return self.buffer


def second_kernel(side, count, scalars, ins, outs, plain, field, act, stage, scr, sems, full, hid, w1_buf, w2_buf, wsems):
    aux, x, b1 = [item() for item in ins]
    pieces, (w1, w2) = plain[:count], plain[count:]
    w1, w2 = Later(w1, w1_buf, wsems.at[0]), Later(w2, w2_buf, wsems.at[1])
    me = scalars[0][0]
    sources = [item() for item in outs[:3]]
    assemble(me, pieces, None, *sources, stage, scr, sems, (w1, w2))
    for item in outs[:3]:
        item.send()
    readin, keep, rest, cot_out = outs[3], outs[4:9], outs[9:15], outs[15]
    cot = cot_out()
    share = cot.shape[1] // count
    for r in range(count):
        start = (me ^ r) * share
        for index in range((stage.shape[2] - 2 * LANES) // LANES * 2):
            (row, lane), (low_row, low_lane) = cot_block(index, share)
            lanes = pl.ds(pl.multiple_of(start + lane, LANES), LANES)
            low_lane = 2 * LANES + low_lane
            cot[row : row + 16, lanes] = stage[r, low_row : low_row + 16, low_lane : low_lane + LANES]
    cot_out.send()
    forward_body(side, aux, x, *sources, keep, field, act, readin())
    readin.send()
    readout_body(me, readin(), w1, b1, w2, cot_out, [hid, *rest], full)


def second_forward(side, chan, mid, me, aux, x, pieces, w1, b1, w2):
    slots = side * side
    hidden, width = w2.shape
    got = call(
        functools.partial(second_kernel, side, len(pieces)),
        whole_shapes(chan, mid)
        + [sds((slots, chan), BF16)]
        + kept_shapes(slots, chan, mid)
        + readout_shapes(slots, chan, hidden, width, len(pieces))
        + [sds((slots, width), BF16)],
        [me],
        [aux, x, b1],
        forward_scratch(side, mid)
        + assemble_scratch(pieces, mid, slots * width // mid)
        + [
            pltpu.VMEM((slots, chan), F32),
            pltpu.VMEM((slots, hidden), BF16),
            pltpu.VMEM(w1.shape, BF16),
            pltpu.VMEM(w2.shape, BF16),
            pltpu.SemaphoreType.DMA((2,)),
        ],
        flops=2 * slots * (mid * (2 * chan + TAPS * mid) + hidden * (2 * chan + width)),
        moved=30 * slots * chan + 2 * hidden * (chan + width),
        plain=[*pieces, w1, w2],
    )
    got = list(got)
    return got[3], [x] + got[:3] + got[4:9], got[9:]


def tail_kernel(placed, scalars, ins, outs, plain, stacked, low, cot, w2_buf, buffer, sems, out_sems):
    readin, w1, b1, *parts, grad = ins
    w1_grad, b1_grad, b2_grad, w2_out = outs
    me = scalars[0][0]
    rows = readin.buffer.shape[0]
    own, w2, *rest = plain
    w2 = Later(w2, w2_buf, sems.at[1 + len(rest)])
    copies = [pltpu.make_async_copy(own, cot.at[0:rows, :], sems.at[0])]
    for r, piece in enumerate(rest):
        share = piece.shape[1]
        lanes = pl.ds(pl.multiple_of((me ^ r) * share, share), share) if placed else slice(0, share)
        copies.append(pltpu.make_async_copy(piece, cot.at[rows:, lanes], sems.at[1 + r]))
    for copy in copies:
        copy.start()
    w2.start()
    split = len(parts) // 2
    half = parts[0].buffer.shape[1]
    lanes = [pl.ds(pl.multiple_of(((me & 1) ^ odd) * half, half), half) for odd in range(2)]
    stacked[0:rows, :] = readin()[...]
    for odd, group in enumerate((parts[:split], parts[split:])):
        at = rows
        for part in group:
            count = part.buffer.shape[0]
            stacked[at : at + count, lanes[odd]] = part()[...]
            at += count
    hidden = dot_nn(stacked[...], w1()[...]) + b1()[...]
    value, slope = gelu_both(hidden)
    turned = value.T.astype(BF16)
    for copy in copies:
        copy.wait()
    width = buffer.shape[2]
    flights = []
    for r in range(cot.shape[1] // width):
        if r >= 2:
            flights[r - 2].wait()
        lanes = slice(r * width, (r + 1) * width)
        buffer[r % 2] = dot_nn(turned, cot[:, lanes])
        flights.append(pltpu.make_async_copy(buffer.at[r % 2], w2_out.target.at[:, lanes], out_sems.at[r % 2]))
        flights[-1].start()
    low[0:rows, :] = (slope[0:rows] * grad()[...]).astype(BF16)
    low[rows:, :] = (slope[rows:] * dot_nt(cot[rows:, :], w2()[...])).astype(BF16)
    w1_grad()[...] = dot_tn(stacked[...], low[...])
    w1_grad.send()
    b1_grad()[...] = jnp.sum(low[...].astype(F32), axis=0, keepdims=True)
    share = b2_grad.buffer.shape[1]
    lanes = pl.ds(pl.multiple_of(me * share, share), share)
    b2_grad()[...] = jnp.sum(cot[:, lanes].astype(F32), axis=0, keepdims=True)
    for flight in flights[-2:]:
        flight.wait()


def tail(me, b1, w1, w2, grad, readin, parts, own, rest, placed, n):
    rows, chan = readin.shape
    total = rows + sum(x.shape[0] for x in parts) // 2
    hidden, width = w2.shape
    chunk = min(width, 1024)
    return call(
        functools.partial(tail_kernel, placed),
        [sds((chan, hidden), F32), sds((1, hidden), F32), sds((1, width // n), F32), sds((hidden, width), F32)],
        [me],
        [readin, w1, b1, *parts, grad],
        [
            pltpu.VMEM((total, chan), BF16),
            pltpu.VMEM((total, hidden), BF16),
            pltpu.VMEM((total, width), BF16),
            pltpu.VMEM(w2.shape, BF16),
            pltpu.VMEM((2, hidden, chunk), F32),
            pltpu.SemaphoreType.DMA((2 + len(rest),)),
            pltpu.SemaphoreType.DMA((2,)),
        ],
        flops=4 * total * hidden * (chan + width),
        moved=2 * hidden * (3 * chan + 3 * width),
        plain=[own, w2, *rest],
        direct=(3,),
    )


def finish_kernel(count, scalars, ins, outs, plain, scr):
    red, conv, exp, mid_gain, mid_bias, out_gain, out_bias = [item() for item in outs]
    late, middle, parts = ins[0:2], ins[2:4], ins[4:]
    chan, mid = red.shape[2], conv.shape[3]
    held = red.shape[1]
    reduce_end, conv_end, expand_end, mid_end, end = columns(chan, mid)
    plane = scalars[0][1] & 1
    few = held // 2

    def from_pair(pair, base, k):
        mine, other = [item()[...] for item in pair]
        for odd in range(2):
            value = jnp.where(plane == odd, mine, other)
            rows = slice(odd * few, odd * few + few)
            for j in range(TAPS):
                at = reduce_end + j * mid - base
                conv[k, j, rows, :] = value[:, at : at + mid].astype(F32)
            exp[k, rows, :] = value[:, conv_end - base : expand_end - base].astype(F32)
            if base == 0:
                red[k, rows, :] = value[:, 0:reduce_end].astype(F32)
                scr[k, rows, :] = value[:, expand_end:end].astype(F32)

    scr[...] = jnp.zeros_like(scr)
    from_pair(late, 0, 1)
    from_pair(middle, reduce_end, 0)
    total = parts[0]()[...]
    for part in parts[1:]:
        total = total + part()[...].astype(F32)
    red[0] = total[:, 0:reduce_end]
    scr[0, 0:held, :] = total[:, reduce_end:]
    for k in range(2):
        flat = scr[k, :, 0:LANES].T
        for which in range(2):
            mid_gain[k, which : which + 1, :] = flat[2 * which : 2 * which + 1, 0:held]
            mid_bias[k, which : which + 1, :] = flat[2 * which + 1 : 2 * which + 2, 0:held]
        out_gain[k : k + 1, :] = scr[k, 0:1, LANES : LANES + out_gain.shape[1]]
        out_bias[k : k + 1, :] = scr[k, 1:2, LANES : LANES + out_bias.shape[1]]


def finish(me, late, middle, parts, chan, mid, share):
    held = parts[0].shape[0]
    outs = [
        sds((2, held, chan), F32),
        sds((2, TAPS, held, mid), F32),
        sds((2, held, chan), F32),
        sds((2, 2, held), F32),
        sds((2, 2, held), F32),
        sds((2, share), F32),
        sds((2, share), F32),
    ]
    return call(
        functools.partial(finish_kernel, len(parts)),
        outs,
        [me],
        [*late, *middle, *parts],
        [pltpu.VMEM((2, LANES, 2 * LANES), F32)],
        flops=8 * held * chan,
        moved=40 * held * chan,
    )


def iota(shape, dim):
    return lax.broadcasted_iota(jnp.int32, shape, dim).astype(F32)


def whole_part(value, divisor):
    return jnp.floor((value + 0.5) * (1.0 / divisor))


def table_at(target, place, extent):
    begin = whole_part(target * extent, POOLED)
    ending = whole_part((target + 1.0) * extent + (POOLED - 1), POOLED)
    inside = jnp.where((place >= begin) & (place < ending), 1.0, 0.0)
    return inside / (ending - begin)


def facts_kernel(scalars, ins, outs, plain):
    extent = scalars[0][0].astype(F32)
    for side, out in ((GRID, outs[0]), (POOLED, outs[1])):
        slots = side * side
        place = iota((slots, 1), 0)
        row = whole_part(place, side)
        column = place - row * side
        out()[:, 1:2] = jnp.where(column > 0.5, 1.0, 0.0)
        out()[:, 2:3] = jnp.where(column < side - 1.5, 1.0, 0.0)
        if side == GRID:
            out()[:, 0:1] = jnp.where((row < extent) & (column < extent), 1.0, 0.0)
        else:
            out()[:, 0:1] = jnp.ones((slots, 1), F32)
    shape = outs[2]().shape
    target, place = iota((shape[0], 1), 0), iota((1, shape[1]), 1)
    up, across = whole_part(target, POOLED), whole_part(place, GRID)
    rows = table_at(up, across, extent)
    lanes = table_at(target - up * POOLED, place - across * GRID, extent)
    outs[2]()[...] = (rows * lanes).astype(BF16)


def facts(grid):
    slots, few = GRID * GRID, POOLED * POOLED
    return call(
        facts_kernel,
        [sds((slots, LANES), F32), sds((few, LANES), F32), sds((few, slots), BF16)],
        [grid],
        [],
    )


def per_device(
    features,
    grid,
    reduce_w,
    conv_w,
    expand_w,
    mid_gain,
    mid_bias,
    out_gain,
    out_bias,
    read_w1,
    read_b1,
    read_w2,
    read_b2,
    cotangent,
):
    n = lax.axis_size("ch")
    chan, mid = reduce_w.shape[1], conv_w.shape[2]
    held, share = reduce_w.shape[2], features.shape[0]
    aligned = share == LANES and held % 16 == 0
    index = lax.axis_index("ch").astype(jnp.int32)
    planes = lax.axis_size("img")
    me = jnp.stack([index, lax.axis_index("img").astype(jnp.int32)])

    feat = jnp.transpose(features[:, 0, :])
    cot = jnp.transpose(cotangent[:, 0, :])
    red = jnp.transpose(reduce_w, (0, 2, 1))
    conv = jnp.transpose(conv_w, (0, 1, 3, 2))
    norms = (mid_gain, mid_bias, out_gain, out_bias)
    few = cot.shape[0]
    slot_facts, few_facts, spread = facts(grid)

    bias_one = read_b1[None, :]

    if aligned:
        (first_packet,) = pack(0, feat, red, conv, expand_w, *norms)
        far = neighbours(first_packet)
        second_packet, cot = pack(1, cot, red, conv, expand_w, *norms, after=[first_packet])

    cot_rest = join(*along_images(cot))

    if aligned:
        far = dict(zip(far, gate(list(far.values()), second_packet, cot_rest, spread)))
        first_pieces = with_cores(first_packet, far)
        (second_packet,) = gate([second_packet], *far.values())
        far = neighbours(second_packet)
        pooled, saved_first = block_forward(GRID, chan, mid, me, slot_facts, spread, first_pieces, None)
        far = dict(zip(far, gate(list(far.values()), pooled)))
        second_pieces = with_cores(second_packet, far)
        readin, saved_second, got = second_forward(
            POOLED, chan, mid, me, few_facts, pooled, second_pieces, read_w1, bias_one, read_w2
        )
        mine, theirs, own_grad, half_in, keep, send, cot_own = got
    else:
        rows = jnp.concatenate(
            [red, jnp.transpose(conv, (0, 2, 1, 3)).reshape(2, held, TAPS * mid), expand_w], axis=2
        )
        rows = lax.all_gather(rows, "ch", axis=1, tiled=True)
        mids = jnp.stack([mid_gain, mid_bias], axis=2).reshape(2, 4, held)
        mids = jnp.pad(lax.all_gather(mids, "ch", axis=2, tiled=True), ((0, 0), (0, 4), (0, 0)))
        outs = jnp.stack([out_gain, out_bias], axis=1)
        outs = jnp.pad(lax.all_gather(outs, "ch", axis=2, tiled=True), ((0, 0), (0, 6), (0, 0)))
        x_whole = lax.all_gather(feat, "ch", axis=1, tiled=True)
        pooled, saved_first = block_forward(
            GRID, chan, mid, me, slot_facts, spread, None, (x_whole, rows[0], mids[0], outs[0])
        )
        readin, saved_second = block_forward(
            POOLED, chan, mid, me, few_facts, None, None, (pooled, rows[1], mids[1], outs[1])
        )
        cot_own = lax.all_gather(cot, "ch", axis=1, tiled=True)
        mine, theirs, own_grad, half_in, keep, send = readout(me, readin, read_w1, bias_one, read_w2, cot_own, n)

    half = summed(mine, ppermute_xor(theirs, "ch", 1))
    far = neighbours(half)
    if aligned:
        (cot_rest,) = gate([cot_rest], half)
        cot_far = neighbours(cot_rest)
    grad_pieces = with_cores(half, far)
    (half_in,) = gate([half_in], *far.values())
    parts = [ppermute_xor(half_in, "img", m) for m in (1, 2) if m < planes]

    pooled_grad, late_mine, late_theirs, late_out = late_backward(
        POOLED, held, me, few_facts, grad_pieces, saved_second
    )
    late_got = ppermute_xor(late_theirs, "img", 1)
    (half_in,) = gate([half_in], pooled_grad)
    parts += [ppermute_xor(half_in, "img", m) for m in range(3, planes)]
    own_lanes = share if aligned else 0
    middle_mine, middle_theirs, *upper = upper_backward(
        GRID, held, me, slot_facts, spread, pooled_grad, saved_first, own_lanes
    )
    middle_got = ppermute_xor(middle_theirs, "img", 1)
    (late_got,) = gate([late_got], upper[0])
    late_half = summed(late_mine, late_got)
    late_got = ppermute_xor(late_half, "img", 2)
    parts = gate(parts, upper[0])
    parts = [*parts, *[ppermute_xor(x, "ch", 1) for x in parts]]
    if aligned:
        cot_far = dict(zip(cot_far, gate(list(cot_far.values()), upper[0])))
        rest_pieces = with_cores(cot_rest, cot_far)
    else:
        rest_pieces = [lax.all_gather(cot_rest, "ch", axis=1, tiled=True)]
    feat_grad, last_grads, last_low = lower_backward(
        GRID, held, me, slot_facts, upper, saved_first, own_lanes
    )
    last = [last_grads] + along_images(last_low)
    late_got, middle_got = gate([late_got, middle_got], last_grads)
    middle_half = summed(middle_mine, middle_got)
    middle_got = ppermute_xor(middle_half, "img", 2)
    late_half = summed(late_half, late_got)
    for mask in (1 << k for k in range(2, planes.bit_length() - 1)):
        late_half = summed(late_half, ppermute_xor(late_half, "img", mask))
    late = (late_half, ppermute_xor(late_half, "img", 1))
    w1_grad, b1_grad, b2_grad, w2_grad = tail(
        me, bias_one, read_w1, read_w2, own_grad, readin, parts, cot_own, rest_pieces, aligned, n
    )
    (middle_got,) = gate([middle_got], b1_grad)
    middle_half = summed(middle_half, middle_got)
    for mask in (1 << k for k in range(2, planes.bit_length() - 1)):
        middle_half = summed(middle_half, ppermute_xor(middle_half, "img", mask))
    middle = (middle_half, ppermute_xor(middle_half, "img", 1))

    got = ppermute_xor(send, "ch", 1)
    (got,) = gate([got], b1_grad)
    shares = [summed(keep[q], got[q]) for q in range(n // 2)]
    tokens = shares[0].astype(F32)
    for q in range(1, n // 2):
        tokens = tokens + ppermute_xor(shares[q], "ch", 2 * q).astype(F32)
    tokens = (tokens + read_b2[None, :]).astype(BF16)

    red_grad, conv_grad, exp_grad, mid_gain_grad, mid_bias_grad, out_gain_grad, out_bias_grad = finish(
        me, late, middle, last, chan, mid, share
    )
    if not aligned:
        feat_grad = lax.dynamic_slice_in_dim(feat_grad, index * share, share, 1)
        both = jnp.stack([upper[3], late_out])
        both = lax.dynamic_slice_in_dim(both, index * share, share, 2)
        both = lax.psum(both.astype(BF16), "img").astype(F32)
        out_gain_grad, out_bias_grad = both[:, 0], both[:, 1]

    return (
        jnp.transpose(tokens)[:, None, :],
        jnp.transpose(feat_grad)[:, None, :],
        jnp.transpose(red_grad, (0, 2, 1)),
        jnp.transpose(conv_grad, (0, 1, 3, 2)),
        exp_grad,
        mid_gain_grad,
        mid_bias_grad,
        out_gain_grad,
        out_bias_grad,
        w1_grad,
        b1_grad[0],
        w2_grad,
        b2_grad[0],
    )


def solution(mesh):
    return jax.shard_map(
        per_device,
        mesh=mesh,
        in_specs=(
            P("ch", "img", None),
            P("img"),
            P(None, None, "ch"),
            P(None, None, None, "ch"),
            P(None, "ch", None),
            P(None, None, "ch"),
            P(None, None, "ch"),
            P(None, "ch"),
            P(None, "ch"),
            P(None, "ch"),
            P("ch"),
            P("ch", None),
            P("ch"),
            P("ch", "img", None),
        ),
        out_specs=(
            P("ch", "img", None),
            P("ch", "img", None),
            P(None, None, "ch"),
            P(None, None, None, "ch"),
            P(None, "ch", None),
            P(None, None, "ch"),
            P(None, None, "ch"),
            P(None, "ch"),
            P(None, "ch"),
            P(None, "ch"),
            P("ch"),
            P("ch", None),
            P("ch"),
        ),
        check_vma=False,
    )
```

```python
import functools

import jax
import jax.numpy as jnp
from jax import lax
from jax.experimental import pallas as pl
from jax.experimental.pallas import tpu as pltpu
from jax.sharding import PartitionSpec as P

GRID = 24
POOLED = 12
EPSILON = 1e-06
OFFSETS = [(-1, -1), (-1, 0), (-1, 1), (0, -1), (0, 0), (0, 1), (1, -1), (1, 0), (1, 1)]
TAPS = len(OFFSETS)
LANES = 128
BF16 = jnp.bfloat16
F32 = jnp.float32
SMEM = pl.BlockSpec(memory_space=pltpu.SMEM)
ANY = pl.BlockSpec(memory_space=pl.ANY)


def dot_nn(left, right):
    return lax.dot_general(left, right, (((1,), (0,)), ((), ())), preferred_element_type=F32)


def dot_nt(left, right):
    return lax.dot_general(left, right, (((1,), (1,)), ((), ())), preferred_element_type=F32)


def dot_tn(left, right):
    return lax.dot_general(left, right, (((0,), (0,)), ((), ())), preferred_element_type=F32)


def sds(shape, dtype):
    return jax.ShapeDtypeStruct(tuple(shape), dtype)


class Inward:
    def __init__(self, source, buffer, sem):
        self.copy = pltpu.make_async_copy(source, buffer, sem)
        self.buffer, self.waited = buffer, False
        self.copy.start()

    def __call__(self):
        if not self.waited:
            self.copy.wait()
            self.waited = True
        return self.buffer


class Outward:
    def __init__(self, target, buffer, sem):
        self.copy = None if buffer is None else pltpu.make_async_copy(buffer, target, sem)
        self.target, self.buffer, self.sent = target, buffer, False

    def __call__(self):
        return self.buffer

    def send(self):
        if not self.sent:
            self.copy.start()
            self.sent = True


def call(body, outs, scalars, args, scratch=(), vmem=60, flops=0, moved=0, plain=(), after=(), direct=()):
    count = (len(scalars), len(args), len(plain), len(after), len(outs))

    def kernel(*refs):
        refs = list(refs)

        def take(k):
            got = refs[:k]
            del refs[:k]
            return got

        scalar_refs, sources, plain_refs, _, targets = [take(k) for k in count]
        in_buffers = take(len(args))
        out_buffers = [None if i in direct else refs.pop(0) for i in range(len(outs))]
        in_sems = refs.pop(0) if args else None
        out_sems = refs.pop(0)
        inward = [Inward(s, b, in_sems.at[i]) for i, (s, b) in enumerate(zip(sources, in_buffers))]
        outward = [Outward(t, b, out_sems.at[i]) for i, (t, b) in enumerate(zip(targets, out_buffers))]
        made = [item for item in outward if item.buffer is not None]
        body(scalar_refs, inward, outward, plain_refs, *refs)
        for item in inward:
            item()
        for item in made:
            item.send()
        for item in made:
            item.copy.wait()

    results = [x for i, x in enumerate(outs) if i not in direct]
    shapes = [pltpu.VMEM(x.shape, x.dtype) for x in list(args) + results]
    sems = ([pltpu.SemaphoreType.DMA((len(args),))] if args else []) + [
        pltpu.SemaphoreType.DMA((len(outs),))
    ]
    return pl.pallas_call(
        kernel,
        out_shape=list(outs),
        in_specs=[SMEM] * len(scalars) + [ANY] * (len(args) + len(plain) + len(after)),
        out_specs=[ANY] * len(outs),
        scratch_shapes=shapes + sems + list(scratch),
        compiler_params=pltpu.CompilerParams(vmem_limit_bytes=vmem << 20),
        cost_estimate=pl.CostEstimate(flops=0, bytes_accessed=0, transcendentals=0),
    )(*scalars, *args, *plain, *after)


def gate(values, *after):
    def nothing(*refs):
        pass

    return pl.pallas_call(
        nothing,
        out_shape=[sds(v.shape, v.dtype) for v in values],
        in_specs=[ANY] * (len(values) + len(after)),
        out_specs=[ANY] * len(values),
        input_output_aliases={i: i for i in range(len(values))},
    )(*values, *after)


def join_body(scalars, ins, outs, plain):
    at = 0
    for item in ins:
        rows = item.buffer.shape[0]
        outs[0]()[at : at + rows, :] = item()[...]
        at += rows


def join(*parts, after=()):
    rows = sum(x.shape[0] for x in parts)
    shape = sds((rows, parts[0].shape[1]), parts[0].dtype)
    return call(join_body, [shape], [], list(parts), after=after)[0]


def ppermute_xor(x, axis, mask):
    return lax.ppermute(x, axis, [(i, i ^ mask) for i in range(lax.axis_size(axis))])


def neighbours(x):
    n = lax.axis_size("ch")
    return {r: ppermute_xor(x, "ch", r) for r in range(n - 2, 0, -2)}


def with_cores(x, far):
    n = lax.axis_size("ch")
    pieces = [None] * n
    for r in range(0, n, 2):
        pieces[r] = far[r] if r else x
        pieces[r + 1] = ppermute_xor(pieces[r], "ch", 1)
    return pieces


def along_images(x):
    return [ppermute_xor(x, "img", m) for m in range(1, lax.axis_size("img"))]


def pair_sum(mine, low, after):
    masks = [1 << k for k in range(lax.axis_size("img").bit_length() - 1)]
    total, got = mine, ppermute_xor(low, "img", masks[0])
    for mask in masks[1:]:
        (got,) = gate([got], after)
        total = (total.astype(F32) + got.astype(F32)).astype(BF16)
        got = ppermute_xor(total, "img", mask)
    return total, got


def doubled(parts, held):
    planes = lax.axis_size("img")
    for mask in (1 << k for k in range(1, planes.bit_length() - 1)):
        parts.append(ppermute_xor(held, "img", mask))
        if 2 * mask < planes:
            held = join(held, parts[-1])
    return parts


def summed(left, right):
    return (left.astype(F32) + right.astype(F32)).astype(BF16)


def rows_of(value, index, count):
    return value[pl.ds(pl.multiple_of(index * count, count), count), :]


def half_of(value, second, count):
    return jnp.where(second == 1, value[count : 2 * count, :], value[0:count, :])


def columns(chan, mid):
    reduce_end = chan
    conv_end = reduce_end + TAPS * mid
    expand_end = conv_end + chan
    return reduce_end, conv_end, expand_end, expand_end + LANES, expand_end + 2 * LANES


def split_low(value):
    high = value.astype(BF16).astype(F32)
    return high, value - high


def cot_block(index, width):
    per = width // LANES
    return (index // per * 16, index % per * LANES), (index % 2 * 16, index // 2 * LANES)


def pack_body(layer, scalars, ins, outs, plain, scr, *bufs):
    feat, mid_gain, mid_bias, out_gain, out_bias = ins
    red, conv, exp = plain
    red_buf, conv_buf, exp_buf, sems = bufs
    copies = [
        pltpu.make_async_copy(source.at[layer], buffer, sems.at[i])
        for i, (source, buffer) in enumerate(((red, red_buf), (conv, conv_buf), (exp, exp_buf)))
    ]
    for copy in copies:
        copy.start()
    packet = outs[0]()
    held, chan, mid = red_buf.shape[0], red_buf.shape[1], conv_buf.shape[2]
    reduce_end, conv_end, expand_end, mid_end, end = columns(chan, mid)
    scr[...] = jnp.zeros_like(scr)
    for which in range(2):
        for kind, ref in enumerate((mid_gain(), mid_bias())):
            high, low = split_low(ref[layer, which : which + 1, :])
            at = 4 * which + 2 * kind
            scr[at : at + 1, 0:held] = high
            scr[at + 1 : at + 2, 0:held] = low
    packet[:, expand_end:mid_end] = scr[...].T[0:held, :].astype(BF16)
    scr[...] = jnp.zeros_like(scr)
    for kind, ref in enumerate((out_gain(), out_bias())):
        high, low = split_low(ref[layer : layer + 1, :])
        scr[2 * kind : 2 * kind + 1, :] = high
        scr[2 * kind + 1 : 2 * kind + 2, :] = low
    packet[:, mid_end:end] = scr[0:held, :].astype(BF16)
    feat = feat()
    if layer == 0:
        for b in range(feat.shape[0] // held):
            packet[:, end + b * LANES : end + (b + 1) * LANES] = feat[b * held : (b + 1) * held, :]
    else:
        for index in range(feat.shape[0] // 16 * (feat.shape[1] // LANES)):
            (row, lane), (low_row, low_lane) = cot_block(index, feat.shape[1])
            packet[low_row : low_row + 16, end + low_lane : end + low_lane + LANES] = feat[
                row : row + 16, lane : lane + LANES
            ]
        outs[1]()[...] = feat[...]
    for copy in copies:
        copy.wait()
    packet[:, 0:reduce_end] = red_buf[...]
    for j in range(TAPS):
        packet[:, reduce_end + j * mid : reduce_end + (j + 1) * mid] = conv_buf[j]
    packet[:, conv_end:expand_end] = exp_buf[...]


def pack(layer, extra, red, conv, exp, mid_gain, mid_bias, out_gain, out_bias, after=()):
    held, chan = red.shape[1:]
    mid = conv.shape[3]
    width = columns(chan, mid)[-1] + extra.shape[0] * extra.shape[1] // held
    outs = [sds((held, width), BF16)]
    if layer:
        outs.append(sds(extra.shape, BF16))
    return call(
        functools.partial(pack_body, layer),
        outs,
        [],
        [extra, mid_gain, mid_bias, out_gain, out_bias],
        [
            pltpu.VMEM((LANES, LANES), F32),
            pltpu.VMEM(red.shape[1:], BF16),
            pltpu.VMEM(conv.shape[1:], BF16),
            pltpu.VMEM(exp.shape[1:], BF16),
            pltpu.SemaphoreType.DMA((3,)),
        ],
        moved=2 * held * width * 2,
        plain=[red, conv, exp],
        after=after,
    )


def assemble(me, pieces, x_ref, w_ref, mid_ref, out_ref, stage, scr, sems, then=()):
    held = pieces[0].shape[0]
    chan, mid = out_ref.shape[1], w_ref.shape[0]
    reduce_end, conv_end, expand_end, mid_end, end = columns(chan, mid)
    width = stage.shape[2]
    parts, copies = [], []
    for r, piece in enumerate(pieces):
        parts.append(
            pltpu.make_async_copy(piece.at[:, expand_end : expand_end + width], stage.at[r], sems.at[2, r])
        )
        parts[-1].start()
    for k, (start, stop) in enumerate(((0, reduce_end), (reduce_end, expand_end))):
        for r, piece in enumerate(pieces):
            rows = pl.ds(pl.multiple_of((me ^ r) * held, held), held)
            copies.append(
                pltpu.make_async_copy(piece.at[:, start:stop], w_ref.at[rows, start:stop], sems.at[k, r])
            )
            copies[-1].start()
    for copy in then:
        copy.start()
    for r in range(len(pieces)):
        parts[r].wait()
        rows = pl.ds(pl.multiple_of((me ^ r) * held, held), held)
        lanes = pl.ds(pl.multiple_of((me ^ r) * LANES, LANES), LANES)
        scr[rows, :] = stage[r, :, 0:LANES].astype(F32)
        block = stage[r, :, LANES : 2 * LANES].astype(F32)
        out_ref[0:1, lanes] = block[0:1, :] + block[1:2, :]
        out_ref[1:2, lanes] = block[2:3, :] + block[3:4, :]
        for b in range(width // LANES - 2 if x_ref is not None else 0):
            at = (b + 2) * LANES
            x_ref[b * held : (b + 1) * held, lanes] = stage[r, :, at : at + LANES]
    flat = scr[...].T
    for q in range(4):
        mid_ref[q : q + 1, :] = flat[2 * q : 2 * q + 1, :] + flat[2 * q + 1 : 2 * q + 2, :]

    def wait(some):
        def waiting():
            for copy in some:
                copy.wait()

        return waiting

    return wait(copies[: len(pieces)]), wait(copies[len(pieces) :])


def at_once():
    pass


def sigmoid(value):
    return 0.5 * jnp.tanh(0.5 * value) + 0.5


def silu(value):
    return value * sigmoid(value)


def silu_slope(value):
    gate = sigmoid(value)
    return gate * (1.0 + value * (1.0 - gate))


def unit_of(values):
    inverse = 1.0 / values.shape[-1]
    center = jnp.sum(values, axis=-1, keepdims=True) * inverse
    spread = jnp.sum(values * values, axis=-1, keepdims=True) * inverse - center * center
    factor = lax.rsqrt(spread + EPSILON)
    return (values - center) * factor, factor


def chunked(slots, body, carry=None):
    return body(slice(0, slots), 0, carry)


def pad_of(side):
    return -(-(side + 1) // 16) * 16


def shift_columns(field, side, slots, aux_ref):
    pad = pad_of(side)
    field[0, pad : pad + slots, :] = field[1, pad - 1 : pad - 1 + slots, :] * aux_ref[:, 1:2]
    field[2, pad : pad + slots, :] = field[1, pad + 1 : pad + 1 + slots, :] * aux_ref[:, 2:3]


def clear_edges(field, side, slots):
    pad = pad_of(side)
    for k in range(3):
        field[k, 0:pad, :] = jnp.zeros((pad, field.shape[2]), F32)
        field[k, pad + slots : pad + slots + pad, :] = jnp.zeros((pad, field.shape[2]), F32)


def tap(field, side, slots, rise, step):
    at = pad_of(side) + rise * side
    return field[step + 1, at : at + slots, :].astype(BF16)


def forward_body(side, aux, x_ref, w_ref, mid_ref, out_ref, keep, field, act, finish, ready=(at_once, at_once)):
    u1, u2, u3, fac, pat = [item() for item in keep]
    slots = x_ref.shape[0]
    chan, mid = out_ref.shape[1], w_ref.shape[0]
    reduce_end, conv_end, expand_end, _, _ = columns(chan, mid)
    pad = pad_of(side)
    clear_edges(field, side, slots)
    ready[0]()
    u1[...] = dot_nt(x_ref[...], w_ref[:, 0:reduce_end])

    def first(rows, start, carry):
        unit, factor = unit_of(u1[rows, :])
        u1[rows, :] = unit
        fac[rows, 0:1] = factor
        value = silu(unit * mid_ref[0:1, :] + mid_ref[1:2, :]) * aux[rows, 0:1]
        field[1, pl.ds(pad + start, unit.shape[0]), :] = value
        return carry

    chunked(slots, first)
    keep[0].send()
    shift_columns(field, side, slots, aux)
    for j, (rise, step) in enumerate(OFFSETS):
        pat[:, j * mid : (j + 1) * mid] = tap(field, side, slots, rise, step)
    keep[4].send()
    ready[1]()
    u2[...] = dot_nt(pat[...], w_ref[:, reduce_end:conv_end])

    def second(rows, start, carry):
        unit, factor = unit_of(u2[rows, :])
        u2[rows, :] = unit
        fac[rows, 1:2] = factor
        act[rows, :] = silu(unit * mid_ref[2:3, :] + mid_ref[3:4, :]).astype(BF16)
        return carry

    chunked(slots, second)
    keep[1].send()
    u3[...] = dot_nn(act[...], w_ref[:, conv_end:expand_end])

    def third(rows, start, carry):
        unit, factor = unit_of(u3[rows, :])
        u3[rows, :] = unit
        fac[rows, 2:3] = factor
        summed = unit * out_ref[0:1, :] + out_ref[1:2, :] + x_ref[rows, :].astype(F32)
        finish[rows, :] = (silu(summed) * aux[rows, 0:1]).astype(BF16)
        return carry

    chunked(slots, third)
    keep[2].send()
    keep[3].send()


def forward_kernel(side, pooling, assembled, scalars, ins, outs, plain, *scratch):
    field, act, *rest = scratch
    ins, outs = list(ins), list(outs)
    aux = ins.pop(0)()
    if pooling:
        spread, finish = ins.pop(0), rest.pop(0)
    ready, made = (at_once, at_once), []
    if assembled:
        sources = [item() for item in ins]
    else:
        made, outs = outs[:4], outs[4:]
        sources = [item() for item in made]
        ready = assemble(scalars[0][0], plain, *sources, *rest)
    result = outs[0]
    if not pooling:
        finish = result()
    if made:
        made[0].send()
    forward_body(side, aux, *sources, outs[1:], field, act, finish, ready)
    for item in made:
        item.send()
    if pooling:
        result()[...] = dot_nn(spread()[...], finish[...]).astype(BF16)


def kept_shapes(slots, chan, mid):
    return [
        sds((slots, mid), F32),
        sds((slots, mid), F32),
        sds((slots, chan), F32),
        sds((slots, LANES), F32),
        sds((slots, TAPS * mid), BF16),
    ]


def whole_shapes(chan, mid):
    return [sds((mid, columns(chan, mid)[2]), BF16), sds((8, mid), F32), sds((8, chan), F32)]


def forward_scratch(side, mid):
    slots = side * side
    return [
        pltpu.VMEM((3, slots + 2 * pad_of(side), mid), F32),
        pltpu.VMEM((slots, mid), BF16),
    ]


def assemble_scratch(pieces, mid, extra):
    held = mid // len(pieces)
    return [
        pltpu.VMEM((len(pieces), held, 2 * LANES + extra), BF16),
        pltpu.VMEM((mid, LANES), F32),
        pltpu.SemaphoreType.DMA((3, len(pieces))),
    ]


def block_forward(side, chan, mid, me, aux, spread, pieces, assembled):
    slots = side * side
    pooling = spread is not None
    args = [aux] + ([spread] if pooling else [])
    outs = [sds((spread.shape[0] if pooling else slots, chan), BF16)] + kept_shapes(slots, chan, mid)
    scratch = forward_scratch(side, mid)
    if pooling:
        scratch.append(pltpu.VMEM((slots, chan), BF16))
    if assembled is not None:
        args += list(assembled)
    else:
        outs = [sds((slots, chan), BF16)] + whole_shapes(chan, mid) + outs
        scratch += assemble_scratch(pieces, mid, slots * LANES * len(pieces) // mid)
    got = call(
        functools.partial(forward_kernel, side, pooling, assembled is not None),
        outs,
        [me],
        args,
        scratch,
        flops=2 * slots * mid * (2 * chan + TAPS * mid),
        moved=30 * slots * chan,
        plain=list(pieces or []),
    )
    got = list(got)
    source, got = (list(assembled), got) if assembled is not None else (got[:4], got[4:])
    return got[0], source + got[1:]


def fold(value):
    return jnp.sum(value.reshape(value.shape[0] // 8, 8, value.shape[1]), axis=0)


def norm_back(upstream, unit, factor, gain):
    inverse = 1.0 / unit.shape[-1]
    scaled = upstream * gain
    first = jnp.sum(scaled, axis=-1, keepdims=True) * inverse
    second = jnp.sum(scaled * unit, axis=-1, keepdims=True) * inverse
    return factor * (scaled - first - unit * second)


def back_upper(side, me, aux, up, x_ref, w_in, mid_in, out_ref, u2_in, u3, fac, pat_in, sg, eg, turned, field, dense, accum, out_rows, grads):
    slots, chan = eg.shape
    mid = dense.shape[1]
    held = grads.shape[0]
    reduce_end, conv_end, expand_end, _, _ = columns(chan, mid)
    pad = pad_of(side)
    clear_edges(field, side, slots)

    def third(rows, start, carry):
        gain_acc, bias_acc = carry
        unit = u3[rows, :]
        summed = unit * out_ref[0:1, :] + out_ref[1:2, :] + x_ref[rows, :].astype(F32)
        grad = silu_slope(summed) * (up[rows, :] * aux[rows, 0:1])
        sg[rows, :] = grad
        eg[rows, :] = norm_back(grad, unit, fac[rows, 2:3], out_ref[0:1, :]).astype(BF16)
        return gain_acc + fold(grad * unit), bias_acc + fold(grad)

    zero = jnp.zeros((8, chan), F32)
    gain_acc, bias_acc = chunked(slots, third, (zero, zero))
    out_rows[...] = jnp.zeros_like(out_rows)
    out_rows[0:1, :] = jnp.sum(gain_acc, axis=0, keepdims=True)
    out_rows[1:2, :] = jnp.sum(bias_acc, axis=0, keepdims=True)

    u2, mid_ref, w_ref = u2_in(), mid_in(), w_in()
    dense[...] = silu(u2[...] * mid_ref[2:3, :] + mid_ref[3:4, :])
    turned[...] = dense[...].T
    grads[:, conv_end:expand_end] = dot_nn(rows_of(turned, me, held).astype(BF16), eg[...])
    dense[...] = dot_nt(eg[...], w_ref[:, conv_end:expand_end])
    small = jnp.zeros((8, mid), F32)

    def second(rows, start, carry):
        gain_sum, bias_sum = carry
        unit = u2[rows, :]
        grad = silu_slope(unit * mid_ref[2:3, :] + mid_ref[3:4, :]) * dense[rows, :]
        back = norm_back(grad, unit, fac[rows, 1:2], mid_ref[2:3, :])
        field[1, pl.ds(pad + start, unit.shape[0]), :] = back
        return gain_sum + fold(grad * unit), bias_sum + fold(grad)

    gain_two, bias_two = chunked(slots, second, (small, small))
    accum[2:3, :] = jnp.sum(gain_two, axis=0, keepdims=True)
    accum[3:4, :] = jnp.sum(bias_two, axis=0, keepdims=True)
    turned[...] = field[1, pad : pad + slots, :].T
    pat = pat_in()
    grads[:, reduce_end:conv_end] = dot_nn(rows_of(turned, me, held).astype(BF16), pat[...])


def back_lower(side, me, aux, x_ref, w_ref, mid_ref, u1_in, fac, turned, field, dense, accum, out_rows, grads, tail):
    slots, mid = dense.shape
    chan = x_ref.shape[1]
    held = grads.shape[0]
    reduce_end = columns(chan, mid)[0]
    shift_columns(field, side, slots, aux)
    for j, (rise, step) in enumerate(OFFSETS):
        at = reduce_end + j * mid
        term = dot_nn(tap(field, side, slots, -rise, -step), w_ref[:, at : at + mid])
        dense[...] = term if j == 0 else dense[...] + term
    u1 = u1_in()
    small = jnp.zeros((8, mid), F32)

    def first(rows, start, carry):
        gain_sum, bias_sum = carry
        unit = u1[rows, :]
        grad = silu_slope(unit * mid_ref[0:1, :] + mid_ref[1:2, :]) * (dense[rows, :] * aux[rows, 0:1])
        dense[rows, :] = norm_back(grad, unit, fac[rows, 0:1], mid_ref[0:1, :])
        return gain_sum + fold(grad * unit), bias_sum + fold(grad)

    gain_one, bias_one = chunked(slots, first, (small, small))
    accum[0:1, :] = jnp.sum(gain_one, axis=0, keepdims=True)
    accum[1:2, :] = jnp.sum(bias_one, axis=0, keepdims=True)
    turned[...] = dense[...].T
    grads[:, 0:reduce_end] = dot_nn(rows_of(turned, me, held).astype(BF16), x_ref[...])
    turned[:, 0:LANES] = accum[...].T
    grads[:, tail : tail + LANES] = rows_of(turned, me, held)[:, 0:LANES]
    grads[:, tail + LANES : tail + 2 * LANES] = jnp.zeros((held, LANES), F32)
    if chan // (mid // held) == LANES:
        lanes = pl.ds(pl.multiple_of(me * LANES, LANES), LANES)
        grads[0:8, tail + LANES : tail + 2 * LANES] = out_rows[:, lanes]


def split_rows(grads, plane, mine, theirs, start):
    count, width = mine.buffer.shape
    theirs()[...] = half_of(grads, 1 - plane, count)[:, start : start + width].astype(BF16)
    theirs.send()
    mine()[...] = half_of(grads, plane, count)[:, start : start + width]
    mine.send()


def back_scratch(side, slots, chan, mid):
    return [
        pltpu.VMEM((slots, chan), F32),
        pltpu.VMEM((slots, chan), BF16),
        pltpu.VMEM((mid, slots), F32),
        pltpu.VMEM((3, slots + 2 * pad_of(side), mid), F32),
        pltpu.VMEM((slots, mid), F32),
        pltpu.VMEM((LANES, mid), F32),
    ]


def late_kernel(side, scalars, ins, outs, plain, up, grads, sg, eg, turned, field, dense, accum):
    pieces = ins[:-10]
    aux, x_in, out_in, u3_in, fac_in, mid_in, u2_in, w_in, pat_in, u1_in = ins[-10:]
    x_grad, mine, theirs, out_rows = outs
    me, plane = scalars[0][0], scalars[1][0] & 1
    half = pieces[0].buffer.shape[1]
    for odd in range(2):
        core = (me & 1) ^ odd
        total = pieces[odd]()[...].astype(F32)
        for piece in pieces[odd + 2 :: 2]:
            total = total + piece()[...].astype(F32)
        up[:, pl.ds(pl.multiple_of(core * half, half), half)] = total
    aux, x_ref, out_ref, u3, fac = aux(), x_in(), out_in(), u3_in(), fac_in()
    chan, mid = eg.shape[1], dense.shape[1]
    reduce_end, _, expand_end, _, _ = columns(chan, mid)
    accum[...] = jnp.zeros_like(accum)
    back_upper(
        side, me, aux, up, x_ref, w_in, mid_in, out_ref, u2_in, u3, fac, pat_in,
        sg, eg, turned, field, dense, accum, out_rows(), grads,
    )
    back_lower(
        side, me, aux, x_ref, w_in(), mid_in(), u1_in, fac, turned, field, dense, accum, out_rows(), grads, expand_end,
    )
    split_rows(grads, plane, mine, theirs, 0)
    x_grad()[...] = (dot_nn(dense[...].astype(BF16), w_in()[:, 0:reduce_end]) + sg[...]).astype(BF16)


def late_backward(side, held, me, plane, aux, pieces, saved):
    x, w, mids, outs, u1, u2, u3, fac, pat = saved
    slots, chan = x.shape
    mid = w.shape[0]
    end = columns(chan, mid)[-1]
    return call(
        functools.partial(late_kernel, side),
        [
            sds((slots, chan), BF16),
            sds((held // 2, end), F32),
            sds((held // 2, end), BF16),
            sds((8, chan), F32),
        ],
        [me, plane],
        [*pieces, aux, x, outs, u3, fac, mids, u2, w, pat, u1],
        [pltpu.VMEM((slots, chan), F32), pltpu.VMEM((held, end), F32)] + back_scratch(side, slots, chan, mid),
        flops=3 * slots * mid * (2 * chan + TAPS * mid),
        moved=40 * slots * chan,
    )


def upper_kernel(side, own_lanes, scalars, ins, outs, plain, up, grads, sg, eg, turned, field, dense, accum):
    aux, spread, pooled_grad, x_in, out_in, u3_in, fac_in, mid_in, u2_in, w_in, pat_in = ins
    mine, theirs, conv_grad, sg_own, accum_out, out_rows = outs
    me, plane = scalars[0][0], scalars[1][0] & 1
    slots = eg.shape[0]
    up[...] = dot_tn(spread()[...], pooled_grad()[...])
    aux, x_ref, out_ref, u3, fac = aux(), x_in(), out_in(), u3_in(), fac_in()
    accum[...] = jnp.zeros_like(accum)
    back_upper(
        side, me, aux, up, x_ref, w_in, mid_in, out_ref, u2_in, u3, fac, pat_in,
        sg, eg, turned, field, dense, accum, out_rows(), grads,
    )
    split_rows(grads, plane, mine, theirs, columns(eg.shape[1], dense.shape[1])[0])
    pad = pad_of(side)
    conv_grad()[...] = field[1, pad : pad + slots, :]
    accum_out()[...] = accum[0:8, :]
    if own_lanes:
        sg_own()[...] = sg[:, pl.ds(pl.multiple_of(me * own_lanes, own_lanes), own_lanes)]
    else:
        sg_own()[...] = sg[...]


def upper_backward(side, held, me, plane, aux, spread, pooled_grad, saved, own_lanes):
    x, w, mids, outs, u1, u2, u3, fac, pat = saved
    slots, chan = x.shape
    mid = w.shape[0]
    reduce_end, _, expand_end, _, end = columns(chan, mid)
    return call(
        functools.partial(upper_kernel, side, own_lanes),
        [
            sds((held // 2, expand_end - reduce_end), F32),
            sds((held // 2, expand_end - reduce_end), BF16),
            sds((slots, mid), F32),
            sds((slots, own_lanes or chan), F32),
            sds((8, mid), F32),
            sds((8, chan), F32),
        ],
        [me, plane],
        [aux, spread, pooled_grad, x, outs, u3, fac, mids, u2, w, pat],
        [pltpu.VMEM((slots, chan), F32), pltpu.VMEM((held, end), F32)] + back_scratch(side, slots, chan, mid),
        flops=2 * slots * mid * (2 * chan + TAPS * mid),
        moved=40 * slots * chan,
    )


def lower_kernel(side, own_lanes, scalars, ins, outs, plain, turned, field, dense, accum):
    aux, conv_grad, w_in, u1_in, fac, mid_in, x_in, sg_own, accum_in, out_rows = ins
    x_grad, grads, grads_low = outs
    me = scalars[0][0]
    slots, mid = dense.shape
    pad = pad_of(side)
    clear_edges(field, side, slots)
    field[1, pad : pad + slots, :] = conv_grad()[...]
    accum[...] = jnp.zeros_like(accum)
    accum[0:8, :] = accum_in()[...]
    w_ref, x_ref = w_in(), x_in()
    reduce_end = x_ref.shape[1]
    back_lower(
        side, me, aux(), x_ref, w_ref, mid_in(), u1_in, fac(), turned, field, dense, accum, out_rows(), grads(), reduce_end,
    )
    grads_low()[...] = grads()[...].astype(BF16)
    grads_low.send()
    grads.send()
    low = dense[...].astype(BF16)
    if own_lanes:
        lanes = pl.ds(pl.multiple_of(me * own_lanes, own_lanes), own_lanes)
        x_grad()[...] = dot_nn(low, w_ref[:, lanes]) + sg_own()[...]
    else:
        x_grad()[...] = dot_nn(low, w_ref[:, 0:reduce_end]) + sg_own()[...]


def lower_backward(side, held, me, aux, upper, saved, own_lanes):
    x, w, mids, outs, u1, u2, u3, fac, pat = saved
    slots, chan = x.shape
    mid = w.shape[0]
    conv_grad, sg_own, accum, out_rows = upper
    return call(
        functools.partial(lower_kernel, side, own_lanes),
        [
            sds((slots, own_lanes or chan), F32),
            sds((held, chan + 2 * LANES), F32),
            sds((held, chan + 2 * LANES), BF16),
        ],
        [me],
        [aux, conv_grad, w, u1, fac, mids, x, sg_own, accum, out_rows],
        back_scratch(side, slots, chan, mid)[2:],
        flops=slots * mid * (2 * chan + TAPS * mid),
        moved=20 * slots * chan,
    )


GELU_A = 0.7978845608028654
GELU_B = 0.044715


def gelu_both(value):
    square = value * value
    curve = jnp.tanh(GELU_A * (value + GELU_B * value * square))
    slope = 0.5 * (1.0 + curve) + 0.5 * value * (1.0 - curve * curve) * (
        GELU_A * (1.0 + 3.0 * GELU_B * square)
    )
    return 0.5 * value * (1.0 + curve), slope


def readout_body(me, readin, w1, b1, w2, cot, outs, full):
    act, mine, theirs, grad, half_in, keep, send = outs
    half = full.shape[1] // 2
    core = me & 1
    lanes = pl.ds(pl.multiple_of(core * half, half), half)
    half_in()[...] = readin[:, lanes]
    half_in.send()
    hidden = dot_nn(readin[...], w1()[...]) + b1[...]
    value, slope = gelu_both(hidden)
    act[...] = value.astype(BF16)
    grad()[...] = dot_nt(cot()[...], w2()[...])
    grad.send()
    full[...] = dot_nt((slope * grad()[...]).astype(BF16), w1()[...])
    theirs()[...] = full[:, pl.ds(pl.multiple_of((1 - core) * half, half), half)].astype(BF16)
    theirs.send()
    mine()[...] = full[:, lanes]
    mine.send()
    width = keep.buffer.shape[2]
    for odd, out in ((1, send), (0, keep)):
        for q in range(out.buffer.shape[0]):
            lanes = pl.ds(pl.multiple_of((me ^ (2 * q + odd)) * width, width), width)
            out()[q] = dot_nn(act[...], w2()[:, lanes]).astype(BF16)
        out.send()


def readout_shapes(rows, chan, hidden, width, n):
    return [
        sds((rows, chan // 2), F32),
        sds((rows, chan // 2), BF16),
        sds((rows, hidden), F32),
        sds((rows, chan // 2), BF16),
        sds((n // 2, rows, width // n), BF16),
        sds((n // 2, rows, width // n), BF16),
    ]


def readout_kernel(scalars, ins, outs, plain, full, act):
    readin, w1, b1, w2, cot = ins
    readout_body(scalars[0][0], readin(), w1, b1(), w2, cot, [act, *outs], full)


def readout(me, readin, w1, b1, w2, cot, n):
    rows, chan = readin.shape
    return call(
        readout_kernel,
        readout_shapes(rows, chan, *w2.shape, n),
        [me],
        [readin, w1, b1, w2, cot],
        [pltpu.VMEM((rows, chan), F32), pltpu.VMEM((rows, w2.shape[0]), BF16)],
    )


class Later:
    def __init__(self, source, buffer, sem):
        self.copy, self.buffer, self.waited = pltpu.make_async_copy(source, buffer, sem), buffer, False

    def start(self):
        self.copy.start()

    def __call__(self):
        if not self.waited:
            self.copy.wait()
            self.waited = True
        return self.buffer


def second_kernel(side, count, scalars, ins, outs, plain, field, act, stage, scr, sems, full, hid, w1_buf, w2_buf, wsems):
    pieces, (w1, w2) = plain[:count], plain[count:]
    w1, w2 = Later(w1, w1_buf, wsems.at[0]), Later(w2, w2_buf, wsems.at[1])
    me = scalars[0][0]
    sources = [item() for item in outs[:3]]
    ready = assemble(me, pieces, None, *sources, stage, scr, sems, (w1, w2))
    aux, x, b1 = [item() for item in ins]
    readin, keep, rest, cot_out = outs[3], outs[4:9], outs[9:15], outs[15]
    cot = cot_out()
    share = cot.shape[1] // count
    for r in range(count):
        start = (me ^ r) * share
        for index in range((stage.shape[2] - 2 * LANES) // LANES * 2):
            (row, lane), (low_row, low_lane) = cot_block(index, share)
            lanes = pl.ds(pl.multiple_of(start + lane, LANES), LANES)
            low_lane = 2 * LANES + low_lane
            cot[row : row + 16, lanes] = stage[r, low_row : low_row + 16, low_lane : low_lane + LANES]
    cot_out.send()
    forward_body(side, aux, x, *sources, keep, field, act, readin(), ready)
    readin.send()
    for item in outs[:3]:
        item.send()
    readout_body(me, readin(), w1, b1, w2, cot_out, [hid, *rest], full)


def second_forward(side, chan, mid, me, aux, x, pieces, w1, b1, w2):
    slots = side * side
    hidden, width = w2.shape
    got = call(
        functools.partial(second_kernel, side, len(pieces)),
        whole_shapes(chan, mid)
        + [sds((slots, chan), BF16)]
        + kept_shapes(slots, chan, mid)
        + readout_shapes(slots, chan, hidden, width, len(pieces))
        + [sds((slots, width), BF16)],
        [me],
        [aux, x, b1],
        forward_scratch(side, mid)
        + assemble_scratch(pieces, mid, slots * width // mid)
        + [
            pltpu.VMEM((slots, chan), F32),
            pltpu.VMEM((slots, hidden), BF16),
            pltpu.VMEM(w1.shape, BF16),
            pltpu.VMEM(w2.shape, BF16),
            pltpu.SemaphoreType.DMA((2,)),
        ],
        flops=2 * slots * (mid * (2 * chan + TAPS * mid) + hidden * (2 * chan + width)),
        moved=30 * slots * chan + 2 * hidden * (chan + width),
        plain=[*pieces, w1, w2],
    )
    got = list(got)
    return got[3], [x] + got[:3] + got[4:9], got[9:]


def tail_kernel(placed, count, scalars, ins, outs, plain, stacked, low, cot, w2_buf, buffer, sems, out_sems):
    parts, (readin, w1, b1, grad) = ins[:count], ins[count:]
    w1_grad, b1_grad, b2_grad, w2_out = outs
    me = scalars[0][0]
    rows = readin.buffer.shape[0]
    own, w2, *rest = plain
    w2 = Later(w2, w2_buf, sems.at[1 + len(rest)])
    copies = [pltpu.make_async_copy(own, cot.at[0:rows, :], sems.at[0])]
    for r, piece in enumerate(rest):
        share = piece.shape[1]
        lanes = pl.ds(pl.multiple_of((me ^ r) * share, share), share) if placed else slice(0, share)
        copies.append(pltpu.make_async_copy(piece, cot.at[rows:, lanes], sems.at[1 + r]))
    for copy in copies:
        copy.start()
    w2.start()
    split = len(parts) // 2
    half = parts[0].buffer.shape[1]
    lanes = [pl.ds(pl.multiple_of(((me & 1) ^ odd) * half, half), half) for odd in range(2)]
    stacked[0:rows, :] = readin()[...]
    for odd, group in enumerate((parts[:split], parts[split:])):
        at = rows
        for part in group:
            count = part.buffer.shape[0]
            stacked[at : at + count, lanes[odd]] = part()[...]
            at += count
    hidden = dot_nn(stacked[...], w1()[...]) + b1()[...]
    value, slope = gelu_both(hidden)
    turned = value.T.astype(BF16)
    for copy in copies:
        copy.wait()
    width = buffer.shape[2]
    flights = []
    for r in range(cot.shape[1] // width):
        if r >= 2:
            flights[r - 2].wait()
        lanes = slice(r * width, (r + 1) * width)
        buffer[r % 2] = dot_nn(turned, cot[:, lanes])
        flights.append(pltpu.make_async_copy(buffer.at[r % 2], w2_out.target.at[:, lanes], out_sems.at[r % 2]))
        flights[-1].start()
    low[0:rows, :] = (slope[0:rows] * grad()[...]).astype(BF16)
    low[rows:, :] = (slope[rows:] * dot_nt(cot[rows:, :], w2()[...])).astype(BF16)
    w1_grad()[...] = dot_tn(stacked[...], low[...])
    w1_grad.send()
    b1_grad()[...] = jnp.sum(low[...].astype(F32), axis=0, keepdims=True)
    share = b2_grad.buffer.shape[1]
    lanes = pl.ds(pl.multiple_of(me * share, share), share)
    b2_grad()[...] = jnp.sum(cot[:, lanes].astype(F32), axis=0, keepdims=True)
    for flight in flights[-2:]:
        flight.wait()


def tail(me, b1, w1, w2, grad, readin, parts, own, rest, placed, n):
    rows, chan = readin.shape
    total = rows + sum(x.shape[0] for x in parts) // 2
    hidden, width = w2.shape
    chunk = min(width, 1024)
    return call(
        functools.partial(tail_kernel, placed, len(parts)),
        [sds((chan, hidden), F32), sds((1, hidden), F32), sds((1, width // n), F32), sds((hidden, width), F32)],
        [me],
        [*parts, readin, w1, b1, grad],
        [
            pltpu.VMEM((total, chan), BF16),
            pltpu.VMEM((total, hidden), BF16),
            pltpu.VMEM((total, width), BF16),
            pltpu.VMEM(w2.shape, BF16),
            pltpu.VMEM((2, hidden, chunk), F32),
            pltpu.SemaphoreType.DMA((2 + len(rest),)),
            pltpu.SemaphoreType.DMA((2,)),
        ],
        flops=4 * total * hidden * (chan + width),
        moved=2 * hidden * (3 * chan + 3 * width),
        plain=[own, w2, *rest],
        direct=(3,),
    )


def finish_kernel(count, scalars, ins, outs, plain, scr):
    red, conv, exp, mid_gain, mid_bias, out_gain, out_bias = [item() for item in outs]
    late, middle, parts = ins[0:2], ins[2:4], ins[4:]
    chan, mid = red.shape[2], conv.shape[3]
    held = red.shape[1]
    reduce_end, conv_end, expand_end, mid_end, end = columns(chan, mid)
    plane = scalars[1][0] & 1
    few = held // 2

    def from_pair(pair, base, k):
        mine, other = [item()[...] for item in pair]
        for odd in range(2):
            value = jnp.where(plane == odd, mine, other)
            rows = slice(odd * few, odd * few + few)
            for j in range(TAPS):
                at = reduce_end + j * mid - base
                conv[k, j, rows, :] = value[:, at : at + mid].astype(F32)
            exp[k, rows, :] = value[:, conv_end - base : expand_end - base].astype(F32)
            if base == 0:
                red[k, rows, :] = value[:, 0:reduce_end].astype(F32)
                scr[k, rows, :] = value[:, expand_end:end].astype(F32)

    scr[...] = jnp.zeros_like(scr)
    from_pair(late, 0, 1)
    from_pair(middle, reduce_end, 0)
    total = parts[0]()[...]
    for part in parts[1:]:
        total = total + part()[...].astype(F32)
    red[0] = total[:, 0:reduce_end]
    scr[0, 0:held, :] = total[:, reduce_end:]
    for k in range(2):
        flat = scr[k, :, 0:LANES].T
        for which in range(2):
            mid_gain[k, which : which + 1, :] = flat[2 * which : 2 * which + 1, 0:held]
            mid_bias[k, which : which + 1, :] = flat[2 * which + 1 : 2 * which + 2, 0:held]
        out_gain[k : k + 1, :] = scr[k, 0:1, LANES : LANES + out_gain.shape[1]]
        out_bias[k : k + 1, :] = scr[k, 1:2, LANES : LANES + out_bias.shape[1]]


def finish(me, plane, late, middle, parts, chan, mid, share):
    held = parts[0].shape[0]
    outs = [
        sds((2, held, chan), F32),
        sds((2, TAPS, held, mid), F32),
        sds((2, held, chan), F32),
        sds((2, 2, held), F32),
        sds((2, 2, held), F32),
        sds((2, share), F32),
        sds((2, share), F32),
    ]
    return call(
        functools.partial(finish_kernel, len(parts)),
        outs,
        [me, plane],
        [*late, *middle, *parts],
        [pltpu.VMEM((2, LANES, 2 * LANES), F32)],
        flops=8 * held * chan,
        moved=40 * held * chan,
    )


def iota(shape, dim):
    return lax.broadcasted_iota(jnp.int32, shape, dim).astype(F32)


def whole_part(value, divisor):
    return jnp.floor((value + 0.5) * (1.0 / divisor))


def table_at(target, place, extent):
    begin = whole_part(target * extent, POOLED)
    ending = whole_part((target + 1.0) * extent + (POOLED - 1), POOLED)
    inside = jnp.where((place >= begin) & (place < ending), 1.0, 0.0)
    return inside / (ending - begin)


def facts_kernel(scalars, ins, outs, plain):
    extent = scalars[0][0].astype(F32)
    for side, out in ((GRID, outs[0]), (POOLED, outs[1])):
        slots = side * side
        place = iota((slots, 1), 0)
        row = whole_part(place, side)
        column = place - row * side
        out()[:, 1:2] = jnp.where(column > 0.5, 1.0, 0.0)
        out()[:, 2:3] = jnp.where(column < side - 1.5, 1.0, 0.0)
        if side == GRID:
            out()[:, 0:1] = jnp.where((row < extent) & (column < extent), 1.0, 0.0)
        else:
            out()[:, 0:1] = jnp.ones((slots, 1), F32)
    shape = outs[2]().shape
    target, place = iota((shape[0], 1), 0), iota((1, shape[1]), 1)
    up, across = whole_part(target, POOLED), whole_part(place, GRID)
    rows = table_at(up, across, extent)
    lanes = table_at(target - up * POOLED, place - across * GRID, extent)
    outs[2]()[...] = (rows * lanes).astype(BF16)


def facts(grid):
    slots, few = GRID * GRID, POOLED * POOLED
    return call(
        facts_kernel,
        [sds((slots, LANES), F32), sds((few, LANES), F32), sds((few, slots), BF16)],
        [grid],
        [],
    )


def per_device(
    features,
    grid,
    reduce_w,
    conv_w,
    expand_w,
    mid_gain,
    mid_bias,
    out_gain,
    out_bias,
    read_w1,
    read_b1,
    read_w2,
    read_b2,
    cotangent,
):
    n = lax.axis_size("ch")
    chan, mid = reduce_w.shape[1], conv_w.shape[2]
    held, share = reduce_w.shape[2], features.shape[0]
    aligned = share == LANES and held % 16 == 0
    index = lax.axis_index("ch").astype(jnp.int32)
    planes = lax.axis_size("img")
    me = index[None]
    plane = lax.axis_index("img").astype(jnp.int32)[None]

    feat = jnp.transpose(features[:, 0, :])
    cot = jnp.transpose(cotangent[:, 0, :])
    red = jnp.transpose(reduce_w, (0, 2, 1))
    conv = jnp.transpose(conv_w, (0, 1, 3, 2))
    norms = (mid_gain, mid_bias, out_gain, out_bias)
    few = cot.shape[0]
    slot_facts, few_facts, spread = facts(grid)

    bias_one = read_b1[None, :]

    if aligned:
        (first_packet,) = pack(0, feat, red, conv, expand_w, *norms)
        far = neighbours(first_packet)
        second_packet, cot = pack(1, cot, red, conv, expand_w, *norms, after=[first_packet])

        (second_packet,) = gate([second_packet], far[2])

    cot_rest = [ppermute_xor(cot, "img", 1)]
    held_cot = join(cot, cot_rest[0])

    if aligned:
        second_far = neighbours(second_packet)
        far = dict(zip(far, gate(list(far.values()), held_cot, spread)))
        (held_cot,) = gate([held_cot], *far.values())
        cot_rest = doubled(cot_rest, held_cot)
        first_pieces = with_cores(first_packet, far)
        pooled, saved_first = block_forward(GRID, chan, mid, me, slot_facts, spread, first_pieces, None)
        far = dict(zip(second_far, gate(list(second_far.values()), pooled, *cot_rest)))
        second_pieces = with_cores(second_packet, far)
        readin, saved_second, got = second_forward(
            POOLED, chan, mid, me, few_facts, pooled, second_pieces, read_w1, bias_one, read_w2
        )
        mine, theirs, own_grad, half_in, keep, send, cot_own = got
    else:
        rows = jnp.concatenate(
            [red, jnp.transpose(conv, (0, 2, 1, 3)).reshape(2, held, TAPS * mid), expand_w], axis=2
        )
        rows = lax.all_gather(rows, "ch", axis=1, tiled=True)
        mids = jnp.stack([mid_gain, mid_bias], axis=2).reshape(2, 4, held)
        mids = jnp.pad(lax.all_gather(mids, "ch", axis=2, tiled=True), ((0, 0), (0, 4), (0, 0)))
        outs = jnp.stack([out_gain, out_bias], axis=1)
        outs = jnp.pad(lax.all_gather(outs, "ch", axis=2, tiled=True), ((0, 0), (0, 6), (0, 0)))
        x_whole = lax.all_gather(feat, "ch", axis=1, tiled=True)
        pooled, saved_first = block_forward(
            GRID, chan, mid, me, slot_facts, spread, None, (x_whole, rows[0], mids[0], outs[0])
        )
        readin, saved_second = block_forward(
            POOLED, chan, mid, me, few_facts, None, None, (pooled, rows[1], mids[1], outs[1])
        )
        cot_own = lax.all_gather(cot, "ch", axis=1, tiled=True)
        mine, theirs, own_grad, half_in, keep, send = readout(me, readin, read_w1, bias_one, read_w2, cot_own, n)

    if not aligned:
        cot_rest = doubled(cot_rest, held_cot)
    half = summed(mine, ppermute_xor(theirs, "ch", 1))
    far = neighbours(half)
    cot_rest = join(*cot_rest, after=[half])
    far = dict(zip(far, gate(list(far.values()), cot_rest)))
    if aligned:
        (cot_far,) = gate([cot_rest], *far.values())
        cot_far = neighbours(cot_far)
    grad_pieces = with_cores(half, far)
    (half_in,) = gate([half_in], half)
    parts = [ppermute_xor(half_in, "img", m) for m in (1, 2) if m < planes]

    pooled_grad, late_mine, late_theirs, late_out = late_backward(
        POOLED, held, me, plane, few_facts, grad_pieces, saved_second
    )
    late_got = ppermute_xor(late_theirs, "img", 1)
    (half_in,) = gate([half_in], pooled_grad)
    parts += [ppermute_xor(half_in, "img", m) for m in range(3, planes)]
    own_lanes = share if aligned else 0
    middle_mine, middle_theirs, *upper = upper_backward(
        GRID, held, me, plane, slot_facts, spread, pooled_grad, saved_first, own_lanes
    )
    middle_got = ppermute_xor(middle_theirs, "img", 1)
    (late_got,) = gate([late_got], upper[0])
    late_half = summed(late_mine, late_got)
    late_got = ppermute_xor(late_half, "img", 2)
    parts = gate(parts, upper[0])
    parts = [*parts, *[ppermute_xor(x, "ch", 1) for x in parts]]
    if aligned:
        cot_far = dict(zip(cot_far, gate(list(cot_far.values()), upper[0])))
        rest_pieces = with_cores(cot_rest, cot_far)
    else:
        rest_pieces = [lax.all_gather(cot_rest, "ch", axis=1, tiled=True)]
    feat_grad, last_grads, last_low = lower_backward(
        GRID, held, me, slot_facts, upper, saved_first, own_lanes
    )
    last = [last_grads] + along_images(last_low)
    late_got, middle_got = gate([late_got, middle_got], last_grads)
    middle_half = summed(middle_mine, middle_got)
    middle_got = ppermute_xor(middle_half, "img", 2)
    late_half = summed(late_half, late_got)
    for mask in (1 << k for k in range(2, planes.bit_length() - 1)):
        late_half = summed(late_half, ppermute_xor(late_half, "img", mask))
    late = (late_half, ppermute_xor(late_half, "img", 1))
    w1_grad, b1_grad, b2_grad, w2_grad = tail(
        me, bias_one, read_w1, read_w2, own_grad, readin, parts, cot_own, rest_pieces, aligned, n
    )
    (middle_got,) = gate([middle_got], b1_grad)
    middle_half = summed(middle_half, middle_got)
    for mask in (1 << k for k in range(2, planes.bit_length() - 1)):
        middle_half = summed(middle_half, ppermute_xor(middle_half, "img", mask))
    middle = (middle_half, ppermute_xor(middle_half, "img", 1))

    got = ppermute_xor(send, "ch", 1)
    (got,) = gate([got], b1_grad)
    shares = [summed(keep[q], got[q]) for q in range(n // 2)]
    shares = gate(shares, middle_half)
    tokens = shares[0].astype(F32)
    for q in range(1, n // 2):
        tokens = tokens + ppermute_xor(shares[q], "ch", 2 * q).astype(F32)
    tokens = (tokens + read_b2[None, :]).astype(BF16)

    red_grad, conv_grad, exp_grad, mid_gain_grad, mid_bias_grad, out_gain_grad, out_bias_grad = finish(
        me, plane, late, middle, last, chan, mid, share
    )
    if not aligned:
        feat_grad = lax.dynamic_slice_in_dim(feat_grad, index * share, share, 1)
        both = jnp.stack([upper[3], late_out])
        both = lax.dynamic_slice_in_dim(both, index * share, share, 2)
        both = lax.psum(both.astype(BF16), "img").astype(F32)
        out_gain_grad, out_bias_grad = both[:, 0], both[:, 1]

    return (
        jnp.transpose(tokens)[:, None, :],
        jnp.transpose(feat_grad)[:, None, :],
        jnp.transpose(red_grad, (0, 2, 1)),
        jnp.transpose(conv_grad, (0, 1, 3, 2)),
        exp_grad,
        mid_gain_grad,
        mid_bias_grad,
        out_gain_grad,
        out_bias_grad,
        w1_grad,
        b1_grad[0],
        w2_grad,
        b2_grad[0],
    )


def solution(mesh):
    return jax.shard_map(
        per_device,
        mesh=mesh,
        in_specs=(
            P("ch", "img", None),
            P("img"),
            P(None, None, "ch"),
            P(None, None, None, "ch"),
            P(None, "ch", None),
            P(None, None, "ch"),
            P(None, None, "ch"),
            P(None, "ch"),
            P(None, "ch"),
            P(None, "ch"),
            P("ch"),
            P("ch", None),
            P("ch"),
            P("ch", "img", None),
        ),
        out_specs=(
            P("ch", "img", None),
            P("ch", "img", None),
            P(None, None, "ch"),
            P(None, None, None, "ch"),
            P(None, "ch", None),
            P(None, None, "ch"),
            P(None, None, "ch"),
            P(None, "ch"),
            P(None, "ch"),
            P(None, "ch"),
            P("ch"),
            P("ch", None),
            P("ch"),
        ),
        check_vma=False,
    )
```

```python
import functools

import jax
import jax.numpy as jnp
from jax import lax
from jax.experimental import pallas as pl
from jax.experimental.pallas import tpu as pltpu
from jax.sharding import PartitionSpec as P

GRID = 24
POOLED = 12
EPSILON = 1e-06
OFFSETS = [(-1, -1), (-1, 0), (-1, 1), (0, -1), (0, 0), (0, 1), (1, -1), (1, 0), (1, 1)]
TAPS = len(OFFSETS)
LANES = 128
VMEM_MIB = 64
BF16 = jnp.bfloat16
F32 = jnp.float32
SMEM = pl.BlockSpec(memory_space=pltpu.SMEM)
ANY = pl.BlockSpec(memory_space=pl.ANY)


def dot_nn(left, right):
    return lax.dot_general(left, right, (((1,), (0,)), ((), ())), preferred_element_type=F32)


def dot_nt(left, right):
    return lax.dot_general(left, right, (((1,), (1,)), ((), ())), preferred_element_type=F32)


def dot_tn(left, right):
    return lax.dot_general(left, right, (((0,), (0,)), ((), ())), preferred_element_type=F32)


def sds(shape, dtype):
    return jax.ShapeDtypeStruct(tuple(shape), dtype)


class Inward:
    def __init__(self, source, buffer, sem):
        self.copy = pltpu.make_async_copy(source, buffer, sem)
        self.buffer, self.waited = buffer, False
        self.copy.start()

    def __call__(self):
        if not self.waited:
            self.copy.wait()
            self.waited = True
        return self.buffer


class Outward:
    def __init__(self, target, buffer, sem):
        self.copy = None if buffer is None else pltpu.make_async_copy(buffer, target, sem)
        self.target, self.buffer, self.sent = target, buffer, False

    def __call__(self):
        return self.buffer

    def send(self):
        if not self.sent:
            self.copy.start()
            self.sent = True


def call(body, outs, scalars, args, scratch=(),  plain=(), after=(), direct=()):
    count = (len(scalars), len(args), len(plain), len(after), len(outs))

    def kernel(*refs):
        refs = list(refs)

        def take(k):
            got = refs[:k]
            del refs[:k]
            return got

        scalar_refs, sources, plain_refs, _, targets = [take(k) for k in count]
        in_buffers = take(len(args))
        out_buffers = [None if i in direct else refs.pop(0) for i in range(len(outs))]
        in_sems = refs.pop(0) if args else None
        out_sems = refs.pop(0)
        inward = [Inward(s, b, in_sems.at[i]) for i, (s, b) in enumerate(zip(sources, in_buffers))]
        outward = [Outward(t, b, out_sems.at[i]) for i, (t, b) in enumerate(zip(targets, out_buffers))]
        made = [item for item in outward if item.buffer is not None]
        body(scalar_refs, inward, outward, plain_refs, *refs)
        for item in inward:
            item()
        for item in made:
            item.send()
        for item in made:
            item.copy.wait()

    results = [x for i, x in enumerate(outs) if i not in direct]
    shapes = [pltpu.VMEM(x.shape, x.dtype) for x in list(args) + results]
    sems = ([pltpu.SemaphoreType.DMA((len(args),))] if args else []) + [
        pltpu.SemaphoreType.DMA((len(outs),))
    ]
    return pl.pallas_call(
        kernel,
        out_shape=list(outs),
        in_specs=[SMEM] * len(scalars) + [ANY] * (len(args) + len(plain) + len(after)),
        out_specs=[ANY] * len(outs),
        scratch_shapes=shapes + sems + list(scratch),
        compiler_params=pltpu.CompilerParams(vmem_limit_bytes=VMEM_MIB << 20),
        cost_estimate=pl.CostEstimate(flops=0, bytes_accessed=0, transcendentals=0),
    )(*scalars, *args, *plain, *after)


def gate(values, *after):
    def nothing(*refs):
        pass

    return pl.pallas_call(
        nothing,
        out_shape=[sds(v.shape, v.dtype) for v in values],
        in_specs=[ANY] * (len(values) + len(after)),
        out_specs=[ANY] * len(values),
        input_output_aliases={i: i for i in range(len(values))},
        compiler_params=pltpu.CompilerParams(vmem_limit_bytes=VMEM_MIB << 20),
    )(*values, *after)


def join_body(scalars, ins, outs, plain):
    at = 0
    for item in ins:
        rows = item.buffer.shape[0]
        outs[0]()[at : at + rows, :] = item()[...]
        at += rows


def join(*parts, after=()):
    rows = sum(x.shape[0] for x in parts)
    shape = sds((rows, parts[0].shape[1]), parts[0].dtype)
    return call(join_body, [shape], [], list(parts), after=after)[0]


def ppermute_xor(x, axis, mask):
    return lax.ppermute(x, axis, [(i, i ^ mask) for i in range(lax.axis_size(axis))])


def neighbours(x):
    n = lax.axis_size("ch")
    return {r: ppermute_xor(x, "ch", r) for r in range(n - 2, 0, -2)}


def with_cores(x, far):
    n = lax.axis_size("ch")
    pieces = [None] * n
    for r in range(0, n, 2):
        pieces[r] = far[r] if r else x
        pieces[r + 1] = ppermute_xor(pieces[r], "ch", 1)
    return pieces


def along_images(x):
    return [ppermute_xor(x, "img", m) for m in range(1, lax.axis_size("img"))]


def pair_sum(mine, low, after):
    masks = [1 << k for k in range(lax.axis_size("img").bit_length() - 1)]
    total, got = mine, ppermute_xor(low, "img", masks[0])
    for mask in masks[1:]:
        (got,) = gate([got], after)
        total = (total.astype(F32) + got.astype(F32)).astype(BF16)
        got = ppermute_xor(total, "img", mask)
    return total, got


def doubled(parts, held):
    planes = lax.axis_size("img")
    for mask in (1 << k for k in range(1, planes.bit_length() - 1)):
        parts.append(ppermute_xor(held, "img", mask))
        if 2 * mask < planes:
            held = join(held, parts[-1])
    return parts


def summed(left, right):
    return (left.astype(F32) + right.astype(F32)).astype(BF16)


def rows_of(value, index, count):
    return value[pl.ds(pl.multiple_of(index * count, count), count), :]


def half_of(value, second, count):
    return jnp.where(second == 1, value[count : 2 * count, :], value[0:count, :])


def columns(chan, mid):
    reduce_end = chan
    conv_end = reduce_end + TAPS * mid
    expand_end = conv_end + chan
    return reduce_end, conv_end, expand_end, expand_end + LANES, expand_end + 2 * LANES


def split_low(value):
    high = value.astype(BF16).astype(F32)
    return high, value - high


def cot_block(index, width):
    per = width // LANES
    return (index // per * 16, index % per * LANES), (index % 2 * 16, index // 2 * LANES)


def pack_body(layer, scalars, ins, outs, plain, scr, *bufs):
    feat, mid_gain, mid_bias, out_gain, out_bias = ins
    red, conv, exp = plain
    red_buf, conv_buf, exp_buf, sems = bufs
    copies = [
        pltpu.make_async_copy(source.at[layer], buffer, sems.at[i])
        for i, (source, buffer) in enumerate(((red, red_buf), (conv, conv_buf), (exp, exp_buf)))
    ]
    for copy in copies:
        copy.start()
    packet = outs[0]()
    held, chan, mid = red_buf.shape[0], red_buf.shape[1], conv_buf.shape[2]
    reduce_end, conv_end, expand_end, mid_end, end = columns(chan, mid)
    scr[...] = jnp.zeros_like(scr)
    for which in range(2):
        for kind, ref in enumerate((mid_gain(), mid_bias())):
            high, low = split_low(ref[layer, which : which + 1, :])
            at = 4 * which + 2 * kind
            scr[at : at + 1, 0:held] = high
            scr[at + 1 : at + 2, 0:held] = low
    packet[:, expand_end:mid_end] = scr[...].T[0:held, :].astype(BF16)
    scr[...] = jnp.zeros_like(scr)
    for kind, ref in enumerate((out_gain(), out_bias())):
        high, low = split_low(ref[layer : layer + 1, :])
        scr[2 * kind : 2 * kind + 1, :] = high
        scr[2 * kind + 1 : 2 * kind + 2, :] = low
    packet[:, mid_end:end] = scr[0:held, :].astype(BF16)
    feat = feat()
    if layer == 0:
        for b in range(feat.shape[0] // held):
            packet[:, end + b * LANES : end + (b + 1) * LANES] = feat[b * held : (b + 1) * held, :]
    else:
        for index in range(feat.shape[0] // 16 * (feat.shape[1] // LANES)):
            (row, lane), (low_row, low_lane) = cot_block(index, feat.shape[1])
            packet[low_row : low_row + 16, end + low_lane : end + low_lane + LANES] = feat[
                row : row + 16, lane : lane + LANES
            ]
        outs[1]()[...] = feat[...]
    for copy in copies:
        copy.wait()
    packet[:, 0:reduce_end] = red_buf[...]
    for j in range(TAPS):
        packet[:, reduce_end + j * mid : reduce_end + (j + 1) * mid] = conv_buf[j]
    packet[:, conv_end:expand_end] = exp_buf[...]


def pack(layer, extra, red, conv, exp, mid_gain, mid_bias, out_gain, out_bias, after=()):
    held, chan = red.shape[1:]
    mid = conv.shape[3]
    width = columns(chan, mid)[-1] + extra.shape[0] * extra.shape[1] // held
    outs = [sds((held, width), BF16)]
    if layer:
        outs.append(sds(extra.shape, BF16))
    return call(
        functools.partial(pack_body, layer),
        outs,
        [],
        [extra, mid_gain, mid_bias, out_gain, out_bias],
        [
            pltpu.VMEM((LANES, LANES), F32),
            pltpu.VMEM(red.shape[1:], BF16),
            pltpu.VMEM(conv.shape[1:], BF16),
            pltpu.VMEM(exp.shape[1:], BF16),
            pltpu.SemaphoreType.DMA((3,)),
        ],
        plain=[red, conv, exp],
        after=after,
    )


def assemble(me, pieces, x_ref, w_ref, mid_ref, out_ref, stage, scr, sems, then=()):
    held = pieces[0].shape[0]
    chan, mid = out_ref.shape[1], w_ref.shape[0]
    reduce_end, conv_end, expand_end, mid_end, end = columns(chan, mid)
    width = stage.shape[2]
    parts, copies = [], []
    for r, piece in enumerate(pieces):
        parts.append(
            pltpu.make_async_copy(piece.at[:, expand_end : expand_end + width], stage.at[r], sems.at[2, r])
        )
        parts[-1].start()
    for k, (start, stop) in enumerate(((0, reduce_end), (reduce_end, expand_end))):
        for r, piece in enumerate(pieces):
            rows = pl.ds(pl.multiple_of((me ^ r) * held, held), held)
            copies.append(
                pltpu.make_async_copy(piece.at[:, start:stop], w_ref.at[rows, start:stop], sems.at[k, r])
            )
            copies[-1].start()
    for copy in then:
        copy.start()
    for r in range(len(pieces)):
        parts[r].wait()
        rows = pl.ds(pl.multiple_of((me ^ r) * held, held), held)
        lanes = pl.ds(pl.multiple_of((me ^ r) * LANES, LANES), LANES)
        scr[rows, :] = stage[r, :, 0:LANES].astype(F32)
        block = stage[r, :, LANES : 2 * LANES].astype(F32)
        out_ref[0:1, lanes] = block[0:1, :] + block[1:2, :]
        out_ref[1:2, lanes] = block[2:3, :] + block[3:4, :]
        for b in range(width // LANES - 2 if x_ref is not None else 0):
            at = (b + 2) * LANES
            x_ref[b * held : (b + 1) * held, lanes] = stage[r, :, at : at + LANES]
    flat = scr[...].T
    for q in range(4):
        mid_ref[q : q + 1, :] = flat[2 * q : 2 * q + 1, :] + flat[2 * q + 1 : 2 * q + 2, :]

    def wait(some):
        def waiting():
            for copy in some:
                copy.wait()

        return waiting

    return wait(copies[: len(pieces)]), wait(copies[len(pieces) :])


def at_once():
    pass


def sigmoid(value):
    return 0.5 * jnp.tanh(0.5 * value) + 0.5


def silu(value):
    return value * sigmoid(value)


def silu_slope(value):
    gate = sigmoid(value)
    return gate * (1.0 + value * (1.0 - gate))


def unit_of(values):
    inverse = 1.0 / values.shape[-1]
    center = jnp.sum(values, axis=-1, keepdims=True) * inverse
    spread = jnp.sum(values * values, axis=-1, keepdims=True) * inverse - center * center
    factor = lax.rsqrt(spread + EPSILON)
    return (values - center) * factor, factor


def chunked(slots, body, carry=None):
    return body(slice(0, slots), 0, carry)


def pad_of(side):
    return -(-(side + 1) // 16) * 16


def shift_columns(field, side, slots, aux_ref):
    pad = pad_of(side)
    field[0, pad : pad + slots, :] = field[1, pad - 1 : pad - 1 + slots, :] * aux_ref[:, 1:2]
    field[2, pad : pad + slots, :] = field[1, pad + 1 : pad + 1 + slots, :] * aux_ref[:, 2:3]


def clear_edges(field, side, slots):
    pad = pad_of(side)
    for k in range(3):
        field[k, 0:pad, :] = jnp.zeros((pad, field.shape[2]), F32)
        field[k, pad + slots : pad + slots + pad, :] = jnp.zeros((pad, field.shape[2]), F32)


def tap(field, side, slots, rise, step):
    at = pad_of(side) + rise * side
    return field[step + 1, at : at + slots, :].astype(BF16)


def forward_body(side, aux, x_ref, w_ref, mid_ref, out_ref, keep, field, act, finish, ready=(at_once, at_once)):
    u1, u2, u3, fac, pat = [item() for item in keep]
    slots = x_ref.shape[0]
    chan, mid = out_ref.shape[1], w_ref.shape[0]
    reduce_end, conv_end, expand_end, _, _ = columns(chan, mid)
    pad = pad_of(side)
    clear_edges(field, side, slots)
    ready[0]()
    u1[...] = dot_nt(x_ref[...], w_ref[:, 0:reduce_end])

    def first(rows, start, carry):
        unit, factor = unit_of(u1[rows, :])
        u1[rows, :] = unit
        fac[rows, 0:1] = factor
        value = silu(unit * mid_ref[0:1, :] + mid_ref[1:2, :]) * aux[rows, 0:1]
        field[1, pl.ds(pad + start, unit.shape[0]), :] = value
        return carry

    chunked(slots, first)
    keep[0].send()
    shift_columns(field, side, slots, aux)
    for j, (rise, step) in enumerate(OFFSETS):
        pat[:, j * mid : (j + 1) * mid] = tap(field, side, slots, rise, step)
    keep[4].send()
    ready[1]()
    u2[...] = dot_nt(pat[...], w_ref[:, reduce_end:conv_end])

    def second(rows, start, carry):
        unit, factor = unit_of(u2[rows, :])
        u2[rows, :] = unit
        fac[rows, 1:2] = factor
        act[rows, :] = silu(unit * mid_ref[2:3, :] + mid_ref[3:4, :]).astype(BF16)
        return carry

    chunked(slots, second)
    keep[1].send()
    u3[...] = dot_nn(act[...], w_ref[:, conv_end:expand_end])

    def third(rows, start, carry):
        unit, factor = unit_of(u3[rows, :])
        u3[rows, :] = unit
        fac[rows, 2:3] = factor
        summed = unit * out_ref[0:1, :] + out_ref[1:2, :] + x_ref[rows, :].astype(F32)
        finish[rows, :] = (silu(summed) * aux[rows, 0:1]).astype(BF16)
        return carry

    chunked(slots, third)
    keep[2].send()
    keep[3].send()


def forward_kernel(side, pooling, assembled, scalars, ins, outs, plain, *scratch):
    field, act, *rest = scratch
    ins, outs = list(ins), list(outs)
    aux = ins.pop(0)()
    if pooling:
        spread, finish = ins.pop(0), rest.pop(0)
    ready, made = (at_once, at_once), []
    if assembled:
        sources = [item() for item in ins]
    else:
        made, outs = outs[:4], outs[4:]
        sources = [item() for item in made]
        ready = assemble(scalars[0][0], plain, *sources, *rest)
    result = outs[0]
    if not pooling:
        finish = result()
    if made:
        made[0].send()
    forward_body(side, aux, *sources, outs[1:], field, act, finish, ready)
    for item in made:
        item.send()
    if pooling:
        result()[...] = dot_nn(spread()[...], finish[...]).astype(BF16)


def kept_shapes(slots, chan, mid):
    return [
        sds((slots, mid), F32),
        sds((slots, mid), F32),
        sds((slots, chan), F32),
        sds((slots, LANES), F32),
        sds((slots, TAPS * mid), BF16),
    ]


def whole_shapes(chan, mid):
    return [sds((mid, columns(chan, mid)[2]), BF16), sds((8, mid), F32), sds((8, chan), F32)]


def forward_scratch(side, mid):
    slots = side * side
    return [
        pltpu.VMEM((3, slots + 2 * pad_of(side), mid), F32),
        pltpu.VMEM((slots, mid), BF16),
    ]


def assemble_scratch(pieces, mid, extra):
    held = mid // len(pieces)
    return [
        pltpu.VMEM((len(pieces), held, 2 * LANES + extra), BF16),
        pltpu.VMEM((mid, LANES), F32),
        pltpu.SemaphoreType.DMA((3, len(pieces))),
    ]


def block_forward(side, chan, mid, me, aux, spread, pieces, assembled):
    slots = side * side
    pooling = spread is not None
    args = [aux] + ([spread] if pooling else [])
    outs = [sds((spread.shape[0] if pooling else slots, chan), BF16)] + kept_shapes(slots, chan, mid)
    scratch = forward_scratch(side, mid)
    if pooling:
        scratch.append(pltpu.VMEM((slots, chan), BF16))
    if assembled is not None:
        args += list(assembled)
    else:
        outs = [sds((slots, chan), BF16)] + whole_shapes(chan, mid) + outs
        scratch += assemble_scratch(pieces, mid, slots * LANES * len(pieces) // mid)
    got = call(
        functools.partial(forward_kernel, side, pooling, assembled is not None),
        outs,
        [me],
        args,
        scratch,
        plain=list(pieces or []),
    )
    got = list(got)
    source, got = (list(assembled), got) if assembled is not None else (got[:4], got[4:])
    return got[0], source + got[1:]


def fold(value):
    return jnp.sum(value.reshape(value.shape[0] // 8, 8, value.shape[1]), axis=0)


def norm_back(upstream, unit, factor, gain):
    inverse = 1.0 / unit.shape[-1]
    scaled = upstream * gain
    first = jnp.sum(scaled, axis=-1, keepdims=True) * inverse
    second = jnp.sum(scaled * unit, axis=-1, keepdims=True) * inverse
    return factor * (scaled - first - unit * second)


def back_upper(side, me, aux, up, x_ref, w_in, mid_in, out_ref, u2_in, u3, fac, pat_in, sg, eg, turned, field, dense, accum, out_rows, grads):
    slots, chan = eg.shape
    mid = dense.shape[1]
    held = grads.shape[0]
    reduce_end, conv_end, expand_end, _, _ = columns(chan, mid)
    pad = pad_of(side)
    clear_edges(field, side, slots)

    def third(rows, start, carry):
        gain_acc, bias_acc = carry
        unit = u3[rows, :]
        summed = unit * out_ref[0:1, :] + out_ref[1:2, :] + x_ref[rows, :].astype(F32)
        grad = silu_slope(summed) * (up[rows, :] * aux[rows, 0:1])
        sg[rows, :] = grad
        eg[rows, :] = norm_back(grad, unit, fac[rows, 2:3], out_ref[0:1, :]).astype(BF16)
        return gain_acc + fold(grad * unit), bias_acc + fold(grad)

    zero = jnp.zeros((8, chan), F32)
    gain_acc, bias_acc = chunked(slots, third, (zero, zero))
    out_rows[...] = jnp.zeros_like(out_rows)
    out_rows[0:1, :] = jnp.sum(gain_acc, axis=0, keepdims=True)
    out_rows[1:2, :] = jnp.sum(bias_acc, axis=0, keepdims=True)

    u2, mid_ref, w_ref = u2_in(), mid_in(), w_in()
    dense[...] = silu(u2[...] * mid_ref[2:3, :] + mid_ref[3:4, :])
    turned[...] = dense[...].T
    grads[:, conv_end:expand_end] = dot_nn(rows_of(turned, me, held).astype(BF16), eg[...])
    dense[...] = dot_nt(eg[...], w_ref[:, conv_end:expand_end])
    small = jnp.zeros((8, mid), F32)

    def second(rows, start, carry):
        gain_sum, bias_sum = carry
        unit = u2[rows, :]
        grad = silu_slope(unit * mid_ref[2:3, :] + mid_ref[3:4, :]) * dense[rows, :]
        back = norm_back(grad, unit, fac[rows, 1:2], mid_ref[2:3, :])
        field[1, pl.ds(pad + start, unit.shape[0]), :] = back
        return gain_sum + fold(grad * unit), bias_sum + fold(grad)

    gain_two, bias_two = chunked(slots, second, (small, small))
    accum[2:3, :] = jnp.sum(gain_two, axis=0, keepdims=True)
    accum[3:4, :] = jnp.sum(bias_two, axis=0, keepdims=True)
    turned[...] = field[1, pad : pad + slots, :].T
    pat = pat_in()
    grads[:, reduce_end:conv_end] = dot_nn(rows_of(turned, me, held).astype(BF16), pat[...])


def back_lower(side, me, aux, x_ref, w_ref, mid_ref, u1_in, fac, turned, field, dense, accum, out_rows, grads, tail):
    slots, mid = dense.shape
    chan = x_ref.shape[1]
    held = grads.shape[0]
    reduce_end = columns(chan, mid)[0]
    shift_columns(field, side, slots, aux)
    for j, (rise, step) in enumerate(OFFSETS):
        at = reduce_end + j * mid
        term = dot_nn(tap(field, side, slots, -rise, -step), w_ref[:, at : at + mid])
        dense[...] = term if j == 0 else dense[...] + term
    u1 = u1_in()
    small = jnp.zeros((8, mid), F32)

    def first(rows, start, carry):
        gain_sum, bias_sum = carry
        unit = u1[rows, :]
        grad = silu_slope(unit * mid_ref[0:1, :] + mid_ref[1:2, :]) * (dense[rows, :] * aux[rows, 0:1])
        dense[rows, :] = norm_back(grad, unit, fac[rows, 0:1], mid_ref[0:1, :])
        return gain_sum + fold(grad * unit), bias_sum + fold(grad)

    gain_one, bias_one = chunked(slots, first, (small, small))
    accum[0:1, :] = jnp.sum(gain_one, axis=0, keepdims=True)
    accum[1:2, :] = jnp.sum(bias_one, axis=0, keepdims=True)
    turned[...] = dense[...].T
    grads[:, 0:reduce_end] = dot_nn(rows_of(turned, me, held).astype(BF16), x_ref[...])
    turned[:, 0:LANES] = accum[...].T
    grads[:, tail : tail + LANES] = rows_of(turned, me, held)[:, 0:LANES]
    grads[:, tail + LANES : tail + 2 * LANES] = jnp.zeros((held, LANES), F32)
    if chan // (mid // held) == LANES:
        lanes = pl.ds(pl.multiple_of(me * LANES, LANES), LANES)
        grads[0:8, tail + LANES : tail + 2 * LANES] = out_rows[:, lanes]


def split_rows(grads, plane, mine, theirs, start):
    count, width = mine.buffer.shape
    theirs()[...] = half_of(grads, 1 - plane, count)[:, start : start + width].astype(BF16)
    theirs.send()
    mine()[...] = half_of(grads, plane, count)[:, start : start + width]
    mine.send()


def back_scratch(side, slots, chan, mid):
    return [
        pltpu.VMEM((slots, chan), F32),
        pltpu.VMEM((slots, chan), BF16),
        pltpu.VMEM((mid, slots), F32),
        pltpu.VMEM((3, slots + 2 * pad_of(side), mid), F32),
        pltpu.VMEM((slots, mid), F32),
        pltpu.VMEM((LANES, mid), F32),
    ]


def late_kernel(side, scalars, ins, outs, plain, up, grads, sg, eg, turned, field, dense, accum):
    pieces = ins[:-10]
    aux, x_in, out_in, u3_in, fac_in, mid_in, u2_in, w_in, pat_in, u1_in = ins[-10:]
    x_grad, mine, theirs, out_rows = outs
    me, plane = scalars[0][0], scalars[1][0] & 1
    half = pieces[0].buffer.shape[1]
    for odd in range(2):
        core = (me & 1) ^ odd
        total = pieces[odd]()[...].astype(F32)
        for piece in pieces[odd + 2 :: 2]:
            total = total + piece()[...].astype(F32)
        up[:, pl.ds(pl.multiple_of(core * half, half), half)] = total
    aux, x_ref, out_ref, u3, fac = aux(), x_in(), out_in(), u3_in(), fac_in()
    chan, mid = eg.shape[1], dense.shape[1]
    reduce_end, _, expand_end, _, _ = columns(chan, mid)
    accum[...] = jnp.zeros_like(accum)
    back_upper(
        side, me, aux, up, x_ref, w_in, mid_in, out_ref, u2_in, u3, fac, pat_in,
        sg, eg, turned, field, dense, accum, out_rows(), grads,
    )
    back_lower(
        side, me, aux, x_ref, w_in(), mid_in(), u1_in, fac, turned, field, dense, accum, out_rows(), grads, expand_end,
    )
    split_rows(grads, plane, mine, theirs, 0)
    x_grad()[...] = (dot_nn(dense[...].astype(BF16), w_in()[:, 0:reduce_end]) + sg[...]).astype(BF16)


def late_backward(side, held, me, plane, aux, pieces, saved):
    x, w, mids, outs, u1, u2, u3, fac, pat = saved
    slots, chan = x.shape
    mid = w.shape[0]
    end = columns(chan, mid)[-1]
    return call(
        functools.partial(late_kernel, side),
        [
            sds((slots, chan), BF16),
            sds((held // 2, end), F32),
            sds((held // 2, end), BF16),
            sds((8, chan), F32),
        ],
        [me, plane],
        [*pieces, aux, x, outs, u3, fac, mids, u2, w, pat, u1],
        [pltpu.VMEM((slots, chan), F32), pltpu.VMEM((held, end), F32)] + back_scratch(side, slots, chan, mid),
    )


def upper_kernel(side, own_lanes, scalars, ins, outs, plain, up, grads, sg, eg, turned, field, dense, accum):
    aux, spread, pooled_grad, x_in, out_in, u3_in, fac_in, mid_in, u2_in, w_in, pat_in = ins
    mine, theirs, conv_grad, sg_own, accum_out, out_rows = outs
    me, plane = scalars[0][0], scalars[1][0] & 1
    slots = eg.shape[0]
    up[...] = dot_tn(spread()[...], pooled_grad()[...])
    aux, x_ref, out_ref, u3, fac = aux(), x_in(), out_in(), u3_in(), fac_in()
    accum[...] = jnp.zeros_like(accum)
    back_upper(
        side, me, aux, up, x_ref, w_in, mid_in, out_ref, u2_in, u3, fac, pat_in,
        sg, eg, turned, field, dense, accum, out_rows(), grads,
    )
    start = columns(eg.shape[1], dense.shape[1])[0]
    split_rows(grads, plane, mine, theirs, start)
    pad = pad_of(side)
    conv_grad()[...] = field[1, pad : pad + slots, :]
    accum_out()[...] = accum[0:8, :]
    if own_lanes:
        sg_own()[...] = sg[:, pl.ds(pl.multiple_of(me * own_lanes, own_lanes), own_lanes)]
    else:
        sg_own()[...] = sg[...]


def upper_backward(side, held, me, plane, aux, spread, pooled_grad, saved, own_lanes):
    x, w, mids, outs, u1, u2, u3, fac, pat = saved
    slots, chan = x.shape
    mid = w.shape[0]
    reduce_end, _, expand_end, _, end = columns(chan, mid)
    return call(
        functools.partial(upper_kernel, side, own_lanes),
        [
            sds((held // 2, expand_end - reduce_end), F32),
            sds((held // 2, expand_end - reduce_end), BF16),
            sds((slots, mid), F32),
            sds((slots, own_lanes or chan), F32),
            sds((8, mid), F32),
            sds((8, chan), F32),
        ],
        [me, plane],
        [aux, spread, pooled_grad, x, outs, u3, fac, mids, u2, w, pat],
        [pltpu.VMEM((slots, chan), F32), pltpu.VMEM((held, end), F32)] + back_scratch(side, slots, chan, mid),
    )


def lower_kernel(side, own_lanes, scalars, ins, outs, plain, turned, field, dense, accum):
    aux, conv_grad, w_in, u1_in, fac, mid_in, x_in, sg_own, accum_in, out_rows = ins
    x_grad, grads, grads_low = outs
    me = scalars[0][0]
    slots, mid = dense.shape
    pad = pad_of(side)
    clear_edges(field, side, slots)
    field[1, pad : pad + slots, :] = conv_grad()[...]
    accum[...] = jnp.zeros_like(accum)
    accum[0:8, :] = accum_in()[...]
    w_ref, x_ref = w_in(), x_in()
    reduce_end = x_ref.shape[1]
    back_lower(
        side, me, aux(), x_ref, w_ref, mid_in(), u1_in, fac(), turned, field, dense, accum, out_rows(), grads(), reduce_end,
    )
    grads_low()[...] = grads()[...].astype(BF16)
    grads_low.send()
    grads.send()
    low = dense[...].astype(BF16)
    if own_lanes:
        lanes = pl.ds(pl.multiple_of(me * own_lanes, own_lanes), own_lanes)
        x_grad()[...] = dot_nn(low, w_ref[:, lanes]) + sg_own()[...]
    else:
        x_grad()[...] = dot_nn(low, w_ref[:, 0:reduce_end]) + sg_own()[...]


def lower_backward(side, held, me, aux, upper, saved, own_lanes):
    x, w, mids, outs, u1, u2, u3, fac, pat = saved
    slots, chan = x.shape
    mid = w.shape[0]
    conv_grad, sg_own, accum, out_rows = upper
    return call(
        functools.partial(lower_kernel, side, own_lanes),
        [
            sds((slots, own_lanes or chan), F32),
            sds((held, chan + 2 * LANES), F32),
            sds((held, chan + 2 * LANES), BF16),
        ],
        [me],
        [aux, conv_grad, w, u1, fac, mids, x, sg_own, accum, out_rows],
        back_scratch(side, slots, chan, mid)[2:],
    )


GELU_A = 0.7978845608028654
GELU_B = 0.044715


def gelu_both(value):
    square = value * value
    curve = jnp.tanh(GELU_A * (value + GELU_B * value * square))
    slope = 0.5 * (1.0 + curve) + 0.5 * value * (1.0 - curve * curve) * (
        GELU_A * (1.0 + 3.0 * GELU_B * square)
    )
    return 0.5 * value * (1.0 + curve), slope


def readout_body(me, readin, w1, b1, w2, cot, outs, full):
    act, mine, theirs, grad, half_in, keep, send = outs
    half = full.shape[1] // 2
    core = me & 1
    lanes = pl.ds(pl.multiple_of(core * half, half), half)
    half_in()[...] = readin[:, lanes]
    half_in.send()
    hidden = dot_nn(readin[...], w1()[...]) + b1[...]
    value, slope = gelu_both(hidden)
    act[...] = value.astype(BF16)
    grad()[...] = dot_nt(cot()[...], w2()[...])
    grad.send()
    full[...] = dot_nt((slope * grad()[...]).astype(BF16), w1()[...])
    theirs()[...] = full[:, pl.ds(pl.multiple_of((1 - core) * half, half), half)].astype(BF16)
    theirs.send()
    mine()[...] = full[:, lanes]
    mine.send()
    width = keep.buffer.shape[2]
    for odd, out in ((1, send), (0, keep)):
        for q in range(out.buffer.shape[0]):
            lanes = pl.ds(pl.multiple_of((me ^ (2 * q + odd)) * width, width), width)
            out()[q] = dot_nn(act[...], w2()[:, lanes]).astype(BF16)
        out.send()


def readout_shapes(rows, chan, hidden, width, n):
    return [
        sds((rows, chan // 2), F32),
        sds((rows, chan // 2), BF16),
        sds((rows, hidden), F32),
        sds((rows, chan // 2), BF16),
        sds((n // 2, rows, width // n), BF16),
        sds((n // 2, rows, width // n), BF16),
    ]


def readout_kernel(scalars, ins, outs, plain, full, act):
    readin, w1, b1, w2, cot = ins
    readout_body(scalars[0][0], readin(), w1, b1(), w2, cot, [act, *outs], full)


def readout(me, readin, w1, b1, w2, cot, n):
    rows, chan = readin.shape
    return call(
        readout_kernel,
        readout_shapes(rows, chan, *w2.shape, n),
        [me],
        [readin, w1, b1, w2, cot],
        [pltpu.VMEM((rows, chan), F32), pltpu.VMEM((rows, w2.shape[0]), BF16)],
    )


class Later:
    def __init__(self, source, buffer, sem):
        self.copy, self.buffer, self.waited = pltpu.make_async_copy(source, buffer, sem), buffer, False

    def start(self):
        self.copy.start()

    def __call__(self):
        if not self.waited:
            self.copy.wait()
            self.waited = True
        return self.buffer


def second_kernel(side, count, scalars, ins, outs, plain, field, act, stage, scr, sems, full, hid, w1_buf, w2_buf, wsems):
    pieces, (w1, w2) = plain[:count], plain[count:]
    w1, w2 = Later(w1, w1_buf, wsems.at[0]), Later(w2, w2_buf, wsems.at[1])
    me = scalars[0][0]
    sources = [item() for item in outs[:3]]
    ready = assemble(me, pieces, None, *sources, stage, scr, sems, (w1, w2))
    aux, x, b1 = [item() for item in ins]
    readin, keep, rest, cot_out = outs[3], outs[4:9], outs[9:15], outs[15]
    cot = cot_out()
    share = cot.shape[1] // count
    for r in range(count):
        start = (me ^ r) * share
        for index in range((stage.shape[2] - 2 * LANES) // LANES * 2):
            (row, lane), (low_row, low_lane) = cot_block(index, share)
            lanes = pl.ds(pl.multiple_of(start + lane, LANES), LANES)
            low_lane = 2 * LANES + low_lane
            cot[row : row + 16, lanes] = stage[r, low_row : low_row + 16, low_lane : low_lane + LANES]
    cot_out.send()
    forward_body(side, aux, x, *sources, keep, field, act, readin(), ready)
    readin.send()
    for item in outs[:3]:
        item.send()
    readout_body(me, readin(), w1, b1, w2, cot_out, [hid, *rest], full)


def second_forward(side, chan, mid, me, aux, x, pieces, w1, b1, w2):
    slots = side * side
    hidden, width = w2.shape
    got = call(
        functools.partial(second_kernel, side, len(pieces)),
        whole_shapes(chan, mid)
        + [sds((slots, chan), BF16)]
        + kept_shapes(slots, chan, mid)
        + readout_shapes(slots, chan, hidden, width, len(pieces))
        + [sds((slots, width), BF16)],
        [me],
        [aux, x, b1],
        forward_scratch(side, mid)
        + assemble_scratch(pieces, mid, slots * width // mid)
        + [
            pltpu.VMEM((slots, chan), F32),
            pltpu.VMEM((slots, hidden), BF16),
            pltpu.VMEM(w1.shape, BF16),
            pltpu.VMEM(w2.shape, BF16),
            pltpu.SemaphoreType.DMA((2,)),
        ],
        plain=[*pieces, w1, w2],
    )
    got = list(got)
    return got[3], [x] + got[:3] + got[4:9], got[9:]


def tail_kernel(placed, count, scalars, ins, outs, plain, stacked, low, cot, w2_buf, buffer, sems, out_sems):
    parts, (readin, w1, b1, grad) = ins[:count], ins[count:]
    w1_grad, b1_grad, b2_grad, w2_out = outs
    me = scalars[0][0]
    rows = readin.buffer.shape[0]
    own, w2, *rest = plain
    w2 = Later(w2, w2_buf, sems.at[1 + len(rest)])
    copies = [pltpu.make_async_copy(own, cot.at[0:rows, :], sems.at[0])]
    for r, piece in enumerate(rest):
        share = piece.shape[1]
        lanes = pl.ds(pl.multiple_of((me ^ r) * share, share), share) if placed else slice(0, share)
        copies.append(pltpu.make_async_copy(piece, cot.at[rows:, lanes], sems.at[1 + r]))
    for copy in copies:
        copy.start()
    w2.start()
    split = len(parts) // 2
    half = parts[0].buffer.shape[1]
    lanes = [pl.ds(pl.multiple_of(((me & 1) ^ odd) * half, half), half) for odd in range(2)]
    stacked[0:rows, :] = readin()[...]
    for odd, group in enumerate((parts[:split], parts[split:])):
        at = rows
        for part in group:
            count = part.buffer.shape[0]
            stacked[at : at + count, lanes[odd]] = part()[...]
            at += count
    hidden = dot_nn(stacked[...], w1()[...]) + b1()[...]
    value, slope = gelu_both(hidden)
    turned = value.T.astype(BF16)
    low[0:rows, :] = (slope[0:rows] * grad()[...]).astype(BF16)
    width = buffer.shape[2]
    flights = []
    for copy in copies:
        copy.wait()
    for r in range(cot.shape[1] // width):
        if r >= 2:
            flights[r - 2].wait()
        lanes = slice(r * width, (r + 1) * width)
        buffer[r % 2] = dot_nn(turned, cot[:, lanes])
        flights.append(pltpu.make_async_copy(buffer.at[r % 2], w2_out.target.at[:, lanes], out_sems.at[r % 2]))
        flights[-1].start()
    low[rows:, :] = (slope[rows:] * dot_nt(cot[rows:, :], w2()[...])).astype(BF16)
    w1_grad()[...] = dot_tn(stacked[...], low[...])
    w1_grad.send()
    b1_grad()[...] = jnp.sum(low[...].astype(F32), axis=0, keepdims=True)
    share = b2_grad.buffer.shape[1]
    lanes = pl.ds(pl.multiple_of(me * share, share), share)
    b2_grad()[...] = jnp.sum(cot[:, lanes].astype(F32), axis=0, keepdims=True)
    for flight in flights[-2:]:
        flight.wait()


def tail(me, b1, w1, w2, grad, readin, parts, own, rest, placed, n):
    rows, chan = readin.shape
    total = rows + sum(x.shape[0] for x in parts) // 2
    hidden, width = w2.shape
    chunk = min(width, 1024)
    return call(
        functools.partial(tail_kernel, placed, len(parts)),
        [sds((chan, hidden), F32), sds((1, hidden), F32), sds((1, width // n), F32), sds((hidden, width), F32)],
        [me],
        [*parts, readin, w1, b1, grad],
        [
            pltpu.VMEM((total, chan), BF16),
            pltpu.VMEM((total, hidden), BF16),
            pltpu.VMEM((total, width), BF16),
            pltpu.VMEM(w2.shape, BF16),
            pltpu.VMEM((2, hidden, chunk), F32),
            pltpu.SemaphoreType.DMA((2 + len(rest),)),
            pltpu.SemaphoreType.DMA((2,)),
        ],
        plain=[own, w2, *rest],
        direct=(3,),
    )


def finish_kernel(count, scalars, ins, outs, plain, scr):
    red, conv, exp, mid_gain, mid_bias, out_gain, out_bias, tokens = [item() for item in outs]
    late, middle, parts = ins[0:2], ins[2:4], ins[4 : 4 + count]
    bias, *shares = ins[4 + count :]
    value = bias()[...]
    for item in shares:
        value = value + item()[...].astype(F32)
    tokens[...] = value.astype(BF16)
    outs[7].send()
    chan, mid = red.shape[2], conv.shape[3]
    held = red.shape[1]
    reduce_end, conv_end, expand_end, mid_end, end = columns(chan, mid)
    plane = scalars[1][0] & 1
    few = held // 2

    def from_pair(pair, base, k):
        mine, other = [item()[...] for item in pair]
        for odd in range(2):
            value = jnp.where(plane == odd, mine, other)
            rows = slice(odd * few, odd * few + few)
            for j in range(TAPS):
                at = reduce_end + j * mid - base
                conv[k, j, rows, :] = value[:, at : at + mid].astype(F32)
            exp[k, rows, :] = value[:, conv_end - base : expand_end - base].astype(F32)
            if base == 0:
                red[k, rows, :] = value[:, 0:reduce_end].astype(F32)
                scr[k, rows, :] = value[:, expand_end:end].astype(F32)

    scr[...] = jnp.zeros_like(scr)
    from_pair(late, 0, 1)
    from_pair(middle, reduce_end, 0)
    total = parts[0]()[...]
    for part in parts[1:]:
        total = total + part()[...].astype(F32)
    red[0] = total[:, 0:reduce_end]
    scr[0, 0:held, :] = total[:, reduce_end:]
    for k in range(2):
        flat = scr[k, :, 0:LANES].T
        for which in range(2):
            mid_gain[k, which : which + 1, :] = flat[2 * which : 2 * which + 1, 0:held]
            mid_bias[k, which : which + 1, :] = flat[2 * which + 1 : 2 * which + 2, 0:held]
        out_gain[k : k + 1, :] = scr[k, 0:1, LANES : LANES + out_gain.shape[1]]
        out_bias[k : k + 1, :] = scr[k, 1:2, LANES : LANES + out_bias.shape[1]]


def finish(me, plane, late, middle, parts, chan, mid, share, bias, shares):
    held = parts[0].shape[0]
    outs = [
        sds((2, held, chan), F32),
        sds((2, TAPS, held, mid), F32),
        sds((2, held, chan), F32),
        sds((2, 2, held), F32),
        sds((2, 2, held), F32),
        sds((2, share), F32),
        sds((2, share), F32),
        sds(shares[0].shape, BF16),
    ]
    return call(
        functools.partial(finish_kernel, len(parts)),
        outs,
        [me, plane],
        [*late, *middle, *parts, bias, *shares],
        [pltpu.VMEM((2, LANES, 2 * LANES), F32)],
    )


def iota(shape, dim):
    return lax.broadcasted_iota(jnp.int32, shape, dim).astype(F32)


def whole_part(value, divisor):
    return jnp.floor((value + 0.5) * (1.0 / divisor))


def table_at(target, place, extent):
    begin = whole_part(target * extent, POOLED)
    ending = whole_part((target + 1.0) * extent + (POOLED - 1), POOLED)
    inside = jnp.where((place >= begin) & (place < ending), 1.0, 0.0)
    return inside / (ending - begin)


def facts_kernel(scalars, ins, outs, plain):
    extent = scalars[0][0].astype(F32)
    for side, out in ((GRID, outs[0]), (POOLED, outs[1])):
        slots = side * side
        place = iota((slots, 1), 0)
        row = whole_part(place, side)
        column = place - row * side
        out()[:, 1:2] = jnp.where(column > 0.5, 1.0, 0.0)
        out()[:, 2:3] = jnp.where(column < side - 1.5, 1.0, 0.0)
        if side == GRID:
            out()[:, 0:1] = jnp.where((row < extent) & (column < extent), 1.0, 0.0)
        else:
            out()[:, 0:1] = jnp.ones((slots, 1), F32)
    shape = outs[2]().shape
    target, place = iota((shape[0], 1), 0), iota((1, shape[1]), 1)
    up, across = whole_part(target, POOLED), whole_part(place, GRID)
    rows = table_at(up, across, extent)
    lanes = table_at(target - up * POOLED, place - across * GRID, extent)
    outs[2]()[...] = (rows * lanes).astype(BF16)


def facts(grid):
    slots, few = GRID * GRID, POOLED * POOLED
    return call(
        facts_kernel,
        [sds((slots, LANES), F32), sds((few, LANES), F32), sds((few, slots), BF16)],
        [grid],
        [],
    )


def per_device(
    features,
    grid,
    reduce_w,
    conv_w,
    expand_w,
    mid_gain,
    mid_bias,
    out_gain,
    out_bias,
    read_w1,
    read_b1,
    read_w2,
    read_b2,
    cotangent,
):
    n = lax.axis_size("ch")
    chan, mid = reduce_w.shape[1], conv_w.shape[2]
    held, share = reduce_w.shape[2], features.shape[0]
    aligned = share == LANES and held % 16 == 0
    index = lax.axis_index("ch").astype(jnp.int32)
    planes = lax.axis_size("img")
    me = index[None]
    plane = lax.axis_index("img").astype(jnp.int32)[None]

    feat = jnp.transpose(features[:, 0, :])
    cot = jnp.transpose(cotangent[:, 0, :])
    red = jnp.transpose(reduce_w, (0, 2, 1))
    conv = jnp.transpose(conv_w, (0, 1, 3, 2))
    norms = (mid_gain, mid_bias, out_gain, out_bias)
    few = cot.shape[0]
    slot_facts, few_facts, spread = facts(grid)

    bias_one = read_b1[None, :]

    if aligned:
        (first_packet,) = pack(0, feat, red, conv, expand_w, *norms)
        far = neighbours(first_packet)
        second_packet, cot = pack(1, cot, red, conv, expand_w, *norms, after=[first_packet])

        (second_packet,) = gate([second_packet], far[2])

    cot_rest = [ppermute_xor(cot, "img", 1)]
    held_cot = join(cot, cot_rest[0])

    if aligned:
        second_far = neighbours(second_packet)
        far = dict(zip(far, gate(list(far.values()), held_cot, spread)))
        (held_cot,) = gate([held_cot], *far.values())
        cot_rest = doubled(cot_rest, held_cot)
        first_pieces = with_cores(first_packet, far)
        pooled, saved_first = block_forward(GRID, chan, mid, me, slot_facts, spread, first_pieces, None)
        far = dict(zip(second_far, gate(list(second_far.values()), pooled, *cot_rest)))
        second_pieces = with_cores(second_packet, far)
        readin, saved_second, got = second_forward(
            POOLED, chan, mid, me, few_facts, pooled, second_pieces, read_w1, bias_one, read_w2
        )
        mine, theirs, own_grad, half_in, keep, send, cot_own = got
    else:
        rows = jnp.concatenate(
            [red, jnp.transpose(conv, (0, 2, 1, 3)).reshape(2, held, TAPS * mid), expand_w], axis=2
        )
        rows = lax.all_gather(rows, "ch", axis=1, tiled=True)
        mids = jnp.stack([mid_gain, mid_bias], axis=2).reshape(2, 4, held)
        mids = jnp.pad(lax.all_gather(mids, "ch", axis=2, tiled=True), ((0, 0), (0, 4), (0, 0)))
        outs = jnp.stack([out_gain, out_bias], axis=1)
        outs = jnp.pad(lax.all_gather(outs, "ch", axis=2, tiled=True), ((0, 0), (0, 6), (0, 0)))
        x_whole = lax.all_gather(feat, "ch", axis=1, tiled=True)
        pooled, saved_first = block_forward(
            GRID, chan, mid, me, slot_facts, spread, None, (x_whole, rows[0], mids[0], outs[0])
        )
        readin, saved_second = block_forward(
            POOLED, chan, mid, me, few_facts, None, None, (pooled, rows[1], mids[1], outs[1])
        )
        cot_own = lax.all_gather(cot, "ch", axis=1, tiled=True)
        mine, theirs, own_grad, half_in, keep, send = readout(me, readin, read_w1, bias_one, read_w2, cot_own, n)

    if not aligned:
        cot_rest = doubled(cot_rest, held_cot)

    half = summed(mine, ppermute_xor(theirs, "ch", 1))
    far = neighbours(half)
    cot_rest = join(*cot_rest, after=[half])
    got = ppermute_xor(send, "ch", 1)
    shares = [summed(keep[q], got[q]) for q in range(n // 2)]
    far = dict(zip(far, gate(list(far.values()), cot_rest, shares[0])))
    if aligned:
        (cot_rest,) = gate([cot_rest], *far.values())
        cot_far = neighbours(cot_rest)
    (half_in,) = gate([half_in], half)
    parts = [ppermute_xor(half_in, "img", m) for m in (1, 2) if m < planes]
    grad_pieces = with_cores(half, far)

    pooled_grad, late_mine, late_theirs, late_out = late_backward(
        POOLED, held, me, plane, few_facts, grad_pieces, saved_second
    )
    late_got = ppermute_xor(late_theirs, "img", 1)
    (half_in,) = gate([half_in], pooled_grad)
    parts += [ppermute_xor(half_in, "img", m) for m in range(3, planes)]
    own_lanes = share if aligned else 0
    middle_mine, middle_theirs, *upper = upper_backward(
        GRID, held, me, plane, slot_facts, spread, pooled_grad, saved_first, own_lanes
    )
    middle_got = ppermute_xor(middle_theirs, "img", 1)
    (late_got,) = gate([late_got], upper[0])
    late_half = summed(late_mine, late_got)
    late_got = ppermute_xor(late_half, "img", 2)
    parts = gate(parts, upper[0])
    parts = [*parts, *[ppermute_xor(x, "ch", 1) for x in parts]]
    if aligned:
        cot_far = dict(zip(cot_far, gate(list(cot_far.values()), upper[0])))
        rest_pieces = with_cores(cot_rest, cot_far)
    else:
        rest_pieces = [lax.all_gather(cot_rest, "ch", axis=1, tiled=True)]
    feat_grad, last_grads, last_low = lower_backward(
        GRID, held, me, slot_facts, upper, saved_first, own_lanes
    )
    last = [last_grads] + along_images(last_low)
    late_got, middle_got = gate([late_got, middle_got], last_grads)
    middle_half = summed(middle_mine, middle_got)
    middle_got = ppermute_xor(middle_half, "img", 2)
    late_half = summed(late_half, late_got)
    for mask in (1 << k for k in range(2, planes.bit_length() - 1)):
        late_half = summed(late_half, ppermute_xor(late_half, "img", mask))
    late = (late_half, ppermute_xor(late_half, "img", 1))
    w1_grad, b1_grad, b2_grad, w2_grad = tail(
        me, bias_one, read_w1, read_w2, own_grad, readin, parts, cot_own, rest_pieces, aligned, n
    )
    (middle_got,) = gate([middle_got], b1_grad)
    middle_half = summed(middle_half, middle_got)
    for mask in (1 << k for k in range(2, planes.bit_length() - 1)):
        middle_half = summed(middle_half, ppermute_xor(middle_half, "img", mask))
    middle = (middle_half, ppermute_xor(middle_half, "img", 1))
    shares = gate(shares, middle_half)
    shares = [shares[0]] + [ppermute_xor(shares[q], "ch", 2 * q) for q in range(1, n // 2)]

    red_grad, conv_grad, exp_grad, mid_gain_grad, mid_bias_grad, out_gain_grad, out_bias_grad, tokens = finish(
        me, plane, late, middle, last, chan, mid, share, read_b2[None, :], shares
    )
    if not aligned:
        feat_grad = lax.dynamic_slice_in_dim(feat_grad, index * share, share, 1)
        both = jnp.stack([upper[3], late_out])
        both = lax.dynamic_slice_in_dim(both, index * share, share, 2)
        both = lax.psum(both.astype(BF16), "img").astype(F32)
        out_gain_grad, out_bias_grad = both[:, 0], both[:, 1]

    return (
        jnp.transpose(tokens)[:, None, :],
        jnp.transpose(feat_grad)[:, None, :],
        jnp.transpose(red_grad, (0, 2, 1)),
        jnp.transpose(conv_grad, (0, 1, 3, 2)),
        exp_grad,
        mid_gain_grad,
        mid_bias_grad,
        out_gain_grad,
        out_bias_grad,
        w1_grad,
        b1_grad[0],
        w2_grad,
        b2_grad[0],
    )


def solution(mesh):
    return jax.shard_map(
        per_device,
        mesh=mesh,
        in_specs=(
            P("ch", "img", None),
            P("img"),
            P(None, None, "ch"),
            P(None, None, None, "ch"),
            P(None, "ch", None),
            P(None, None, "ch"),
            P(None, None, "ch"),
            P(None, "ch"),
            P(None, "ch"),
            P(None, "ch"),
            P("ch"),
            P("ch", None),
            P("ch"),
            P("ch", "img", None),
        ),
        out_specs=(
            P("ch", "img", None),
            P("ch", "img", None),
            P(None, None, "ch"),
            P(None, None, None, "ch"),
            P(None, "ch", None),
            P(None, None, "ch"),
            P(None, None, "ch"),
            P(None, "ch"),
            P(None, "ch"),
            P(None, "ch"),
            P("ch"),
            P("ch", None),
            P("ch"),
        ),
        check_vma=False,
    )
```

```python
import functools

import jax
import jax.numpy as jnp
from jax import lax
from jax.experimental import pallas as pl
from jax.experimental.pallas import tpu as pltpu
from jax.sharding import PartitionSpec as P

GRID = 24
POOLED = 12
EPSILON = 1e-06
OFFSETS = [(-1, -1), (-1, 0), (-1, 1), (0, -1), (0, 0), (0, 1), (1, -1), (1, 0), (1, 1)]
TAPS = len(OFFSETS)
LANES = 128
VMEM_MIB = 64
BF16 = jnp.bfloat16
F32 = jnp.float32
SMEM = pl.BlockSpec(memory_space=pltpu.SMEM)
ANY = pl.BlockSpec(memory_space=pl.ANY)


def dot_nn(left, right):
    return lax.dot_general(left, right, (((1,), (0,)), ((), ())), preferred_element_type=F32)


def dot_nt(left, right):
    return lax.dot_general(left, right, (((1,), (1,)), ((), ())), preferred_element_type=F32)


def dot_tn(left, right):
    return lax.dot_general(left, right, (((0,), (0,)), ((), ())), preferred_element_type=F32)


def sds(shape, dtype):
    return jax.ShapeDtypeStruct(tuple(shape), dtype)


class Inward:
    def __init__(self, source, buffer, sem):
        self.copy = pltpu.make_async_copy(source, buffer, sem)
        self.buffer, self.waited = buffer, False
        self.copy.start()

    def __call__(self):
        if not self.waited:
            self.copy.wait()
            self.waited = True
        return self.buffer


class Outward:
    def __init__(self, target, buffer, sem):
        self.copy = None if buffer is None else pltpu.make_async_copy(buffer, target, sem)
        self.target, self.buffer, self.sent = target, buffer, False

    def __call__(self):
        return self.buffer

    def send(self):
        if not self.sent:
            self.copy.start()
            self.sent = True


def call(body, outs, scalars, args, scratch=(),  plain=(), after=(), direct=()):
    count = (len(scalars), len(args), len(plain), len(after), len(outs))

    def kernel(*refs):
        refs = list(refs)

        def take(k):
            got = refs[:k]
            del refs[:k]
            return got

        scalar_refs, sources, plain_refs, _, targets = [take(k) for k in count]
        in_buffers = take(len(args))
        out_buffers = [None if i in direct else refs.pop(0) for i in range(len(outs))]
        in_sems = refs.pop(0) if args else None
        out_sems = refs.pop(0)
        inward = [Inward(s, b, in_sems.at[i]) for i, (s, b) in enumerate(zip(sources, in_buffers))]
        outward = [Outward(t, b, out_sems.at[i]) for i, (t, b) in enumerate(zip(targets, out_buffers))]
        made = [item for item in outward if item.buffer is not None]
        body(scalar_refs, inward, outward, plain_refs, *refs)
        for item in inward:
            item()
        for item in made:
            item.send()
        for item in made:
            item.copy.wait()

    results = [x for i, x in enumerate(outs) if i not in direct]
    shapes = [pltpu.VMEM(x.shape, x.dtype) for x in list(args) + results]
    sems = ([pltpu.SemaphoreType.DMA((len(args),))] if args else []) + [
        pltpu.SemaphoreType.DMA((len(outs),))
    ]
    return pl.pallas_call(
        kernel,
        out_shape=list(outs),
        in_specs=[SMEM] * len(scalars) + [ANY] * (len(args) + len(plain) + len(after)),
        out_specs=[ANY] * len(outs),
        scratch_shapes=shapes + sems + list(scratch),
        compiler_params=pltpu.CompilerParams(vmem_limit_bytes=VMEM_MIB << 20),
        cost_estimate=pl.CostEstimate(flops=0, bytes_accessed=0, transcendentals=0),
    )(*scalars, *args, *plain, *after)


def gate(values, *after):
    def nothing(*refs):
        pass

    return pl.pallas_call(
        nothing,
        out_shape=[sds(v.shape, v.dtype) for v in values],
        in_specs=[ANY] * (len(values) + len(after)),
        out_specs=[ANY] * len(values),
        input_output_aliases={i: i for i in range(len(values))},
        compiler_params=pltpu.CompilerParams(vmem_limit_bytes=VMEM_MIB << 20),
    )(*values, *after)


def join_body(scalars, ins, outs, plain):
    at = 0
    for item in ins:
        rows = item.buffer.shape[0]
        outs[0]()[at : at + rows, :] = item()[...]
        at += rows


def join(*parts, after=()):
    rows = sum(x.shape[0] for x in parts)
    shape = sds((rows, parts[0].shape[1]), parts[0].dtype)
    return call(join_body, [shape], [], list(parts), after=after)[0]


def ppermute_xor(x, axis, mask):
    return lax.ppermute(x, axis, [(i, i ^ mask) for i in range(lax.axis_size(axis))])


def neighbours(x):
    n = lax.axis_size("ch")
    return {r: ppermute_xor(x, "ch", r) for r in range(n - 2, 0, -2)}


def with_cores(x, far):
    n = lax.axis_size("ch")
    pieces = [None] * n
    for r in range(0, n, 2):
        pieces[r] = far[r] if r else x
        pieces[r + 1] = ppermute_xor(pieces[r], "ch", 1)
    return pieces


def along_images(x):
    return [ppermute_xor(x, "img", m) for m in range(1, lax.axis_size("img"))]


def pair_sum(mine, low, after):
    masks = [1 << k for k in range(lax.axis_size("img").bit_length() - 1)]
    total, got = mine, ppermute_xor(low, "img", masks[0])
    for mask in masks[1:]:
        (got,) = gate([got], after)
        total = (total.astype(F32) + got.astype(F32)).astype(BF16)
        got = ppermute_xor(total, "img", mask)
    return total, got


def doubled(parts, held):
    planes = lax.axis_size("img")
    for mask in (1 << k for k in range(1, planes.bit_length() - 1)):
        parts.append(ppermute_xor(held, "img", mask))
        if 2 * mask < planes:
            held = join(held, parts[-1])
    return parts


def summed(left, right):
    return (left.astype(F32) + right.astype(F32)).astype(BF16)


def rows_of(value, index, count):
    return value[pl.ds(pl.multiple_of(index * count, count), count), :]


def half_of(value, second, count):
    return jnp.where(second == 1, value[count : 2 * count, :], value[0:count, :])


def columns(chan, mid):
    reduce_end = chan
    conv_end = reduce_end + TAPS * mid
    expand_end = conv_end + chan
    return reduce_end, conv_end, expand_end, expand_end + LANES, expand_end + 2 * LANES


def split_low(value):
    high = value.astype(BF16).astype(F32)
    return high, value - high


def cot_block(index, width):
    per = width // LANES
    return (index // per * 16, index % per * LANES), (index % 2 * 16, index // 2 * LANES)


def pack_body(layer, scalars, ins, outs, plain, scr, *bufs):
    feat, mid_gain, mid_bias, out_gain, out_bias = ins
    red, conv, exp = plain
    red_buf, conv_buf, exp_buf, sems = bufs
    copies = [
        pltpu.make_async_copy(source.at[layer], buffer, sems.at[i])
        for i, (source, buffer) in enumerate(((red, red_buf), (conv, conv_buf), (exp, exp_buf)))
    ]
    for copy in copies:
        copy.start()
    packet = outs[0]()
    held, chan, mid = red_buf.shape[0], red_buf.shape[1], conv_buf.shape[2]
    reduce_end, conv_end, expand_end, mid_end, end = columns(chan, mid)
    scr[...] = jnp.zeros_like(scr)
    for which in range(2):
        for kind, ref in enumerate((mid_gain(), mid_bias())):
            high, low = split_low(ref[layer, which : which + 1, :])
            at = 4 * which + 2 * kind
            scr[at : at + 1, 0:held] = high
            scr[at + 1 : at + 2, 0:held] = low
    packet[:, expand_end:mid_end] = scr[...].T[0:held, :].astype(BF16)
    scr[...] = jnp.zeros_like(scr)
    for kind, ref in enumerate((out_gain(), out_bias())):
        high, low = split_low(ref[layer : layer + 1, :])
        scr[2 * kind : 2 * kind + 1, :] = high
        scr[2 * kind + 1 : 2 * kind + 2, :] = low
    packet[:, mid_end:end] = scr[0:held, :].astype(BF16)
    feat = feat()
    if layer == 0:
        for b in range(feat.shape[0] // held):
            packet[:, end + b * LANES : end + (b + 1) * LANES] = feat[b * held : (b + 1) * held, :]
    else:
        for index in range(feat.shape[0] // 16 * (feat.shape[1] // LANES)):
            (row, lane), (low_row, low_lane) = cot_block(index, feat.shape[1])
            packet[low_row : low_row + 16, end + low_lane : end + low_lane + LANES] = feat[
                row : row + 16, lane : lane + LANES
            ]
        outs[1]()[...] = feat[...]
    for copy in copies:
        copy.wait()
    packet[:, 0:reduce_end] = red_buf[...]
    for j in range(TAPS):
        packet[:, reduce_end + j * mid : reduce_end + (j + 1) * mid] = conv_buf[j]
    packet[:, conv_end:expand_end] = exp_buf[...]


def pack(layer, extra, red, conv, exp, mid_gain, mid_bias, out_gain, out_bias, after=()):
    held, chan = red.shape[1:]
    mid = conv.shape[3]
    width = columns(chan, mid)[-1] + extra.shape[0] * extra.shape[1] // held
    outs = [sds((held, width), BF16)]
    if layer:
        outs.append(sds(extra.shape, BF16))
    return call(
        functools.partial(pack_body, layer),
        outs,
        [],
        [extra, mid_gain, mid_bias, out_gain, out_bias],
        [
            pltpu.VMEM((LANES, LANES), F32),
            pltpu.VMEM(red.shape[1:], BF16),
            pltpu.VMEM(conv.shape[1:], BF16),
            pltpu.VMEM(exp.shape[1:], BF16),
            pltpu.SemaphoreType.DMA((3,)),
        ],
        plain=[red, conv, exp],
        after=after,
    )


def assemble(me, pieces, x_ref, w_ref, mid_ref, out_ref, stage, scr, sems, then=()):
    held = pieces[0].shape[0]
    chan, mid = out_ref.shape[1], w_ref.shape[0]
    reduce_end, conv_end, expand_end, mid_end, end = columns(chan, mid)
    width = stage.shape[2]
    parts, copies = [], []
    for r, piece in enumerate(pieces):
        parts.append(
            pltpu.make_async_copy(piece.at[:, expand_end : expand_end + width], stage.at[r], sems.at[2, r])
        )
        parts[-1].start()
    for k, (start, stop) in enumerate(((0, reduce_end), (reduce_end, expand_end))):
        for r, piece in enumerate(pieces):
            rows = pl.ds(pl.multiple_of((me ^ r) * held, held), held)
            copies.append(
                pltpu.make_async_copy(piece.at[:, start:stop], w_ref.at[rows, start:stop], sems.at[k, r])
            )
            copies[-1].start()
    for copy in then:
        copy.start()
    for r in range(len(pieces)):
        parts[r].wait()
        rows = pl.ds(pl.multiple_of((me ^ r) * held, held), held)
        lanes = pl.ds(pl.multiple_of((me ^ r) * LANES, LANES), LANES)
        scr[rows, :] = stage[r, :, 0:LANES].astype(F32)
        block = stage[r, :, LANES : 2 * LANES].astype(F32)
        out_ref[0:1, lanes] = block[0:1, :] + block[1:2, :]
        out_ref[1:2, lanes] = block[2:3, :] + block[3:4, :]
        for b in range(width // LANES - 2 if x_ref is not None else 0):
            at = (b + 2) * LANES
            x_ref[b * held : (b + 1) * held, lanes] = stage[r, :, at : at + LANES]
    flat = scr[...].T
    for q in range(4):
        mid_ref[q : q + 1, :] = flat[2 * q : 2 * q + 1, :] + flat[2 * q + 1 : 2 * q + 2, :]

    def wait(some):
        def waiting():
            for copy in some:
                copy.wait()

        return waiting

    return wait(copies[: len(pieces)]), wait(copies[len(pieces) :])


def at_once():
    pass


def sigmoid(value):
    return 0.5 * jnp.tanh(0.5 * value) + 0.5


def silu(value):
    return value * sigmoid(value)


def silu_slope(value):
    gate = sigmoid(value)
    return gate * (1.0 + value * (1.0 - gate))


def unit_of(values):
    inverse = 1.0 / values.shape[-1]
    center = jnp.sum(values, axis=-1, keepdims=True) * inverse
    spread = jnp.sum(values * values, axis=-1, keepdims=True) * inverse - center * center
    factor = lax.rsqrt(spread + EPSILON)
    return (values - center) * factor, factor


def chunked(slots, body, carry=None):
    return body(slice(0, slots), 0, carry)


def pad_of(side):
    return -(-(side + 1) // 16) * 16


def shift_columns(field, side, slots, aux_ref):
    pad = pad_of(side)
    field[0, pad : pad + slots, :] = field[1, pad - 1 : pad - 1 + slots, :] * aux_ref[:, 1:2]
    field[2, pad : pad + slots, :] = field[1, pad + 1 : pad + 1 + slots, :] * aux_ref[:, 2:3]


def clear_edges(field, side, slots):
    pad = pad_of(side)
    for k in range(3):
        field[k, 0:pad, :] = jnp.zeros((pad, field.shape[2]), F32)
        field[k, pad + slots : pad + slots + pad, :] = jnp.zeros((pad, field.shape[2]), F32)


def tap(field, side, slots, rise, step):
    at = pad_of(side) + rise * side
    return field[step + 1, at : at + slots, :].astype(BF16)


def forward_body(side, aux, x_ref, w_ref, mid_ref, out_ref, keep, field, act, finish, ready=(at_once, at_once), between=at_once):
    u1, u2, u3, fac, pat = [item() for item in keep]
    slots = x_ref.shape[0]
    chan, mid = out_ref.shape[1], w_ref.shape[0]
    reduce_end, conv_end, expand_end, _, _ = columns(chan, mid)
    pad = pad_of(side)
    clear_edges(field, side, slots)
    ready[0]()
    u1[...] = dot_nt(x_ref[...], w_ref[:, 0:reduce_end])

    def first(rows, start, carry):
        unit, factor = unit_of(u1[rows, :])
        u1[rows, :] = unit
        fac[rows, 0:1] = factor
        value = silu(unit * mid_ref[0:1, :] + mid_ref[1:2, :]) * aux[rows, 0:1]
        field[1, pl.ds(pad + start, unit.shape[0]), :] = value
        return carry

    chunked(slots, first)
    keep[0].send()
    shift_columns(field, side, slots, aux)
    for j, (rise, step) in enumerate(OFFSETS):
        pat[:, j * mid : (j + 1) * mid] = tap(field, side, slots, rise, step)
    keep[4].send()
    ready[1]()
    u2[...] = dot_nt(pat[...], w_ref[:, reduce_end:conv_end])

    def second(rows, start, carry):
        unit, factor = unit_of(u2[rows, :])
        u2[rows, :] = unit
        fac[rows, 1:2] = factor
        act[rows, :] = silu(unit * mid_ref[2:3, :] + mid_ref[3:4, :]).astype(BF16)
        return carry

    chunked(slots, second)
    keep[1].send()
    between()
    u3[...] = dot_nn(act[...], w_ref[:, conv_end:expand_end])

    def third(rows, start, carry):
        unit, factor = unit_of(u3[rows, :])
        u3[rows, :] = unit
        fac[rows, 2:3] = factor
        summed = unit * out_ref[0:1, :] + out_ref[1:2, :] + x_ref[rows, :].astype(F32)
        finish[rows, :] = (silu(summed) * aux[rows, 0:1]).astype(BF16)
        return carry

    chunked(slots, third)
    keep[2].send()
    keep[3].send()


def forward_kernel(side, pooling, assembled, scalars, ins, outs, plain, *scratch):
    field, act, *rest = scratch
    ins, outs = list(ins), list(outs)
    aux = ins.pop(0)()
    if pooling:
        spread, finish = ins.pop(0), rest.pop(0)
    ready, made = (at_once, at_once), []
    if assembled:
        sources = [item() for item in ins]
    else:
        made, outs = outs[:4], outs[4:]
        sources = [item() for item in made]
        ready = assemble(scalars[0][0], plain, *sources, *rest)
    result = outs[0]
    if not pooling:
        finish = result()
    if made:
        made[0].send()
    forward_body(side, aux, *sources, outs[1:], field, act, finish, ready)
    for item in made:
        item.send()
    if pooling:
        result()[...] = dot_nn(spread()[...], finish[...]).astype(BF16)


def kept_shapes(slots, chan, mid):
    return [
        sds((slots, mid), F32),
        sds((slots, mid), F32),
        sds((slots, chan), F32),
        sds((slots, LANES), F32),
        sds((slots, TAPS * mid), BF16),
    ]


def whole_shapes(chan, mid):
    return [sds((mid, columns(chan, mid)[2]), BF16), sds((8, mid), F32), sds((8, chan), F32)]


def forward_scratch(side, mid):
    slots = side * side
    return [
        pltpu.VMEM((3, slots + 2 * pad_of(side), mid), F32),
        pltpu.VMEM((slots, mid), BF16),
    ]


def assemble_scratch(pieces, mid, extra):
    held = mid // len(pieces)
    return [
        pltpu.VMEM((len(pieces), held, 2 * LANES + extra), BF16),
        pltpu.VMEM((mid, LANES), F32),
        pltpu.SemaphoreType.DMA((3, len(pieces))),
    ]


def block_forward(side, chan, mid, me, aux, spread, pieces, assembled):
    slots = side * side
    pooling = spread is not None
    args = [aux] + ([spread] if pooling else [])
    outs = [sds((spread.shape[0] if pooling else slots, chan), BF16)] + kept_shapes(slots, chan, mid)
    scratch = forward_scratch(side, mid)
    if pooling:
        scratch.append(pltpu.VMEM((slots, chan), BF16))
    if assembled is not None:
        args += list(assembled)
    else:
        outs = [sds((slots, chan), BF16)] + whole_shapes(chan, mid) + outs
        scratch += assemble_scratch(pieces, mid, slots * LANES * len(pieces) // mid)
    got = call(
        functools.partial(forward_kernel, side, pooling, assembled is not None),
        outs,
        [me],
        args,
        scratch,
        plain=list(pieces or []),
    )
    got = list(got)
    source, got = (list(assembled), got) if assembled is not None else (got[:4], got[4:])
    return got[0], source + got[1:]


def fold(value):
    return jnp.sum(value.reshape(value.shape[0] // 8, 8, value.shape[1]), axis=0)


def norm_back(upstream, unit, factor, gain):
    inverse = 1.0 / unit.shape[-1]
    scaled = upstream * gain
    first = jnp.sum(scaled, axis=-1, keepdims=True) * inverse
    second = jnp.sum(scaled * unit, axis=-1, keepdims=True) * inverse
    return factor * (scaled - first - unit * second)


def back_upper(side, me, aux, up, x_ref, w_in, mid_in, out_ref, u2_in, u3, fac, pat_in, sg, eg, turned, field, dense, accum, out_rows, grads):
    slots, chan = eg.shape
    mid = dense.shape[1]
    held = grads.shape[0]
    reduce_end, conv_end, expand_end, _, _ = columns(chan, mid)
    pad = pad_of(side)
    clear_edges(field, side, slots)

    def third(rows, start, carry):
        gain_acc, bias_acc = carry
        unit = u3[rows, :]
        summed = unit * out_ref[0:1, :] + out_ref[1:2, :] + x_ref[rows, :].astype(F32)
        grad = silu_slope(summed) * (up[rows, :] * aux[rows, 0:1])
        sg[rows, :] = grad
        eg[rows, :] = norm_back(grad, unit, fac[rows, 2:3], out_ref[0:1, :]).astype(BF16)
        return gain_acc + fold(grad * unit), bias_acc + fold(grad)

    zero = jnp.zeros((8, chan), F32)
    gain_acc, bias_acc = chunked(slots, third, (zero, zero))
    out_rows[...] = jnp.zeros_like(out_rows)
    out_rows[0:1, :] = jnp.sum(gain_acc, axis=0, keepdims=True)
    out_rows[1:2, :] = jnp.sum(bias_acc, axis=0, keepdims=True)

    u2, mid_ref, w_ref = u2_in(), mid_in(), w_in()
    dense[...] = silu(u2[...] * mid_ref[2:3, :] + mid_ref[3:4, :])
    turned[...] = dense[...].T
    grads[:, conv_end:expand_end] = dot_nn(rows_of(turned, me, held).astype(BF16), eg[...])
    dense[...] = dot_nt(eg[...], w_ref[:, conv_end:expand_end])
    small = jnp.zeros((8, mid), F32)

    def second(rows, start, carry):
        gain_sum, bias_sum = carry
        unit = u2[rows, :]
        grad = silu_slope(unit * mid_ref[2:3, :] + mid_ref[3:4, :]) * dense[rows, :]
        back = norm_back(grad, unit, fac[rows, 1:2], mid_ref[2:3, :])
        field[1, pl.ds(pad + start, unit.shape[0]), :] = back
        return gain_sum + fold(grad * unit), bias_sum + fold(grad)

    gain_two, bias_two = chunked(slots, second, (small, small))
    accum[2:3, :] = jnp.sum(gain_two, axis=0, keepdims=True)
    accum[3:4, :] = jnp.sum(bias_two, axis=0, keepdims=True)
    turned[...] = field[1, pad : pad + slots, :].T
    pat = pat_in()
    grads[:, reduce_end:conv_end] = dot_nn(rows_of(turned, me, held).astype(BF16), pat[...])


def back_lower(side, me, aux, x_ref, w_ref, mid_ref, u1_in, fac, turned, field, dense, accum, out_rows, grads, tail):
    slots, mid = dense.shape
    chan = x_ref.shape[1]
    held = grads.shape[0]
    reduce_end = columns(chan, mid)[0]
    shift_columns(field, side, slots, aux)
    for j, (rise, step) in enumerate(OFFSETS):
        at = reduce_end + j * mid
        term = dot_nn(tap(field, side, slots, -rise, -step), w_ref[:, at : at + mid])
        dense[...] = term if j == 0 else dense[...] + term
    u1 = u1_in()
    small = jnp.zeros((8, mid), F32)

    def first(rows, start, carry):
        gain_sum, bias_sum = carry
        unit = u1[rows, :]
        grad = silu_slope(unit * mid_ref[0:1, :] + mid_ref[1:2, :]) * (dense[rows, :] * aux[rows, 0:1])
        dense[rows, :] = norm_back(grad, unit, fac[rows, 0:1], mid_ref[0:1, :])
        return gain_sum + fold(grad * unit), bias_sum + fold(grad)

    gain_one, bias_one = chunked(slots, first, (small, small))
    accum[0:1, :] = jnp.sum(gain_one, axis=0, keepdims=True)
    accum[1:2, :] = jnp.sum(bias_one, axis=0, keepdims=True)
    turned[...] = dense[...].T
    grads[:, 0:reduce_end] = dot_nn(rows_of(turned, me, held).astype(BF16), x_ref[...])
    turned[:, 0:LANES] = accum[...].T
    grads[:, tail : tail + LANES] = rows_of(turned, me, held)[:, 0:LANES]
    grads[:, tail + LANES : tail + 2 * LANES] = jnp.zeros((held, LANES), F32)
    if chan // (mid // held) == LANES:
        lanes = pl.ds(pl.multiple_of(me * LANES, LANES), LANES)
        grads[0:8, tail + LANES : tail + 2 * LANES] = out_rows[:, lanes]


def split_rows(grads, plane, mine, theirs, start):
    count, width = mine.buffer.shape
    theirs()[...] = half_of(grads, 1 - plane, count)[:, start : start + width].astype(BF16)
    theirs.send()
    mine()[...] = half_of(grads, plane, count)[:, start : start + width]
    mine.send()


def back_scratch(side, slots, chan, mid):
    return [
        pltpu.VMEM((slots, chan), F32),
        pltpu.VMEM((slots, chan), BF16),
        pltpu.VMEM((mid, slots), F32),
        pltpu.VMEM((3, slots + 2 * pad_of(side), mid), F32),
        pltpu.VMEM((slots, mid), F32),
        pltpu.VMEM((LANES, mid), F32),
    ]


def late_kernel(side, scalars, ins, outs, plain, up, grads, sg, eg, turned, field, dense, accum):
    pieces = ins[:-10]
    aux, x_in, out_in, u3_in, fac_in, mid_in, u2_in, w_in, pat_in, u1_in = ins[-10:]
    x_grad, mine, theirs, out_rows = outs
    me, plane = scalars[0][0], scalars[1][0] & 1
    half = pieces[0].buffer.shape[1]
    for odd in range(2):
        core = (me & 1) ^ odd
        total = pieces[odd]()[...].astype(F32)
        for piece in pieces[odd + 2 :: 2]:
            total = total + piece()[...].astype(F32)
        up[:, pl.ds(pl.multiple_of(core * half, half), half)] = total
    aux, x_ref, out_ref, u3, fac = aux(), x_in(), out_in(), u3_in(), fac_in()
    chan, mid = eg.shape[1], dense.shape[1]
    reduce_end, _, expand_end, _, _ = columns(chan, mid)
    accum[...] = jnp.zeros_like(accum)
    back_upper(
        side, me, aux, up, x_ref, w_in, mid_in, out_ref, u2_in, u3, fac, pat_in,
        sg, eg, turned, field, dense, accum, out_rows(), grads,
    )
    back_lower(
        side, me, aux, x_ref, w_in(), mid_in(), u1_in, fac, turned, field, dense, accum, out_rows(), grads, expand_end,
    )
    split_rows(grads, plane, mine, theirs, 0)
    x_grad()[...] = (dot_nn(dense[...].astype(BF16), w_in()[:, 0:reduce_end]) + sg[...]).astype(BF16)


def late_backward(side, held, me, plane, aux, pieces, saved):
    x, w, mids, outs, u1, u2, u3, fac, pat = saved
    slots, chan = x.shape
    mid = w.shape[0]
    end = columns(chan, mid)[-1]
    return call(
        functools.partial(late_kernel, side),
        [
            sds((slots, chan), BF16),
            sds((held // 2, end), F32),
            sds((held // 2, end), BF16),
            sds((8, chan), F32),
        ],
        [me, plane],
        [*pieces, aux, x, outs, u3, fac, mids, u2, w, pat, u1],
        [pltpu.VMEM((slots, chan), F32), pltpu.VMEM((held, end), F32)] + back_scratch(side, slots, chan, mid),
    )


def upper_kernel(side, own_lanes, scalars, ins, outs, plain, up, grads, sg, eg, turned, field, dense, accum):
    aux, spread, pooled_grad, x_in, out_in, u3_in, fac_in, mid_in, u2_in, w_in, pat_in = ins
    mine, theirs, conv_grad, sg_own, accum_out, out_rows = outs
    me, plane = scalars[0][0], scalars[1][0] & 1
    slots = eg.shape[0]
    up[...] = dot_tn(spread()[...], pooled_grad()[...])
    aux, x_ref, out_ref, u3, fac = aux(), x_in(), out_in(), u3_in(), fac_in()
    accum[...] = jnp.zeros_like(accum)
    back_upper(
        side, me, aux, up, x_ref, w_in, mid_in, out_ref, u2_in, u3, fac, pat_in,
        sg, eg, turned, field, dense, accum, out_rows(), grads,
    )
    start = columns(eg.shape[1], dense.shape[1])[0]
    split_rows(grads, plane, mine, theirs, start)
    pad = pad_of(side)
    conv_grad()[...] = field[1, pad : pad + slots, :]
    accum_out()[...] = accum[0:8, :]
    if own_lanes:
        sg_own()[...] = sg[:, pl.ds(pl.multiple_of(me * own_lanes, own_lanes), own_lanes)]
    else:
        sg_own()[...] = sg[...]


def upper_backward(side, held, me, plane, aux, spread, pooled_grad, saved, own_lanes):
    x, w, mids, outs, u1, u2, u3, fac, pat = saved
    slots, chan = x.shape
    mid = w.shape[0]
    reduce_end, _, expand_end, _, end = columns(chan, mid)
    return call(
        functools.partial(upper_kernel, side, own_lanes),
        [
            sds((held // 2, expand_end - reduce_end), F32),
            sds((held // 2, expand_end - reduce_end), BF16),
            sds((slots, mid), F32),
            sds((slots, own_lanes or chan), F32),
            sds((8, mid), F32),
            sds((8, chan), F32),
        ],
        [me, plane],
        [aux, spread, pooled_grad, x, outs, u3, fac, mids, u2, w, pat],
        [pltpu.VMEM((slots, chan), F32), pltpu.VMEM((held, end), F32)] + back_scratch(side, slots, chan, mid),
    )


def lower_kernel(side, own_lanes, scalars, ins, outs, plain, turned, field, dense, accum):
    aux, conv_grad, w_in, u1_in, fac, mid_in, x_in, sg_own, accum_in, out_rows = ins
    x_grad, grads, grads_low = outs
    me = scalars[0][0]
    slots, mid = dense.shape
    pad = pad_of(side)
    clear_edges(field, side, slots)
    field[1, pad : pad + slots, :] = conv_grad()[...]
    accum[...] = jnp.zeros_like(accum)
    accum[0:8, :] = accum_in()[...]
    w_ref, x_ref = w_in(), x_in()
    reduce_end = x_ref.shape[1]
    back_lower(
        side, me, aux(), x_ref, w_ref, mid_in(), u1_in, fac(), turned, field, dense, accum, out_rows(), grads(), reduce_end,
    )
    grads_low()[...] = grads()[...].astype(BF16)
    grads_low.send()
    grads.send()
    low = dense[...].astype(BF16)
    if own_lanes:
        lanes = pl.ds(pl.multiple_of(me * own_lanes, own_lanes), own_lanes)
        x_grad()[...] = dot_nn(low, w_ref[:, lanes]) + sg_own()[...]
    else:
        x_grad()[...] = dot_nn(low, w_ref[:, 0:reduce_end]) + sg_own()[...]


def lower_backward(side, held, me, aux, upper, saved, own_lanes):
    x, w, mids, outs, u1, u2, u3, fac, pat = saved
    slots, chan = x.shape
    mid = w.shape[0]
    conv_grad, sg_own, accum, out_rows = upper
    return call(
        functools.partial(lower_kernel, side, own_lanes),
        [
            sds((slots, own_lanes or chan), F32),
            sds((held, chan + 2 * LANES), F32),
            sds((held, chan + 2 * LANES), BF16),
        ],
        [me],
        [aux, conv_grad, w, u1, fac, mids, x, sg_own, accum, out_rows],
        back_scratch(side, slots, chan, mid)[2:],
    )


GELU_A = 0.7978845608028654
GELU_B = 0.044715


def gelu_both(value):
    square = value * value
    curve = jnp.tanh(GELU_A * (value + GELU_B * value * square))
    slope = 0.5 * (1.0 + curve) + 0.5 * value * (1.0 - curve * curve) * (
        GELU_A * (1.0 + 3.0 * GELU_B * square)
    )
    return 0.5 * value * (1.0 + curve), slope


def readout_body(me, readin, w1, b1, w2, outs, full):
    act, mine, theirs, grad, half_in, keep, send = outs
    half = full.shape[1] // 2
    core = me & 1
    lanes = pl.ds(pl.multiple_of(core * half, half), half)
    half_in()[...] = readin[:, lanes]
    half_in.send()
    hidden = dot_nn(readin[...], w1()[...]) + b1[...]
    value, slope = gelu_both(hidden)
    act[...] = value.astype(BF16)
    width = keep.buffer.shape[2]
    for odd, out in ((1, send), (0, keep)):
        for q in range(out.buffer.shape[0]):
            at = pl.ds(pl.multiple_of((me ^ (2 * q + odd)) * width, width), width)
            out()[q] = dot_nn(act[...], w2()[:, at]).astype(BF16)
        out.send()
    full[...] = dot_nt((slope * grad()[...]).astype(BF16), w1()[...])
    theirs()[...] = full[:, pl.ds(pl.multiple_of((1 - core) * half, half), half)].astype(BF16)
    theirs.send()
    mine()[...] = full[:, lanes]
    mine.send()


def readout_shapes(rows, chan, hidden, width, n):
    return [
        sds((rows, chan // 2), F32),
        sds((rows, chan // 2), BF16),
        sds((rows, hidden), F32),
        sds((rows, chan // 2), BF16),
        sds((n // 2, rows, width // n), BF16),
        sds((n // 2, rows, width // n), BF16),
    ]


def readout_kernel(scalars, ins, outs, plain, full, act):
    readin, w1, b1, w2, cot = ins
    outs[2]()[...] = dot_nt(cot()[...], w2()[...])
    outs[2].send()
    readout_body(scalars[0][0], readin(), w1, b1(), w2, [act, *outs], full)


def readout(me, readin, w1, b1, w2, cot, n):
    rows, chan = readin.shape
    return call(
        readout_kernel,
        readout_shapes(rows, chan, *w2.shape, n),
        [me],
        [readin, w1, b1, w2, cot],
        [pltpu.VMEM((rows, chan), F32), pltpu.VMEM((rows, w2.shape[0]), BF16)],
    )


class Later:
    def __init__(self, source, buffer, sem):
        self.copy, self.buffer, self.waited = pltpu.make_async_copy(source, buffer, sem), buffer, False

    def start(self):
        self.copy.start()

    def __call__(self):
        if not self.waited:
            self.copy.wait()
            self.waited = True
        return self.buffer


def second_kernel(side, count, scalars, ins, outs, plain, field, act, stage, scr, sems, full, hid, w1_buf, w2_buf, wsems):
    pieces, (w1, w2) = plain[:count], plain[count:]
    w1, w2 = Later(w1, w1_buf, wsems.at[0]), Later(w2, w2_buf, wsems.at[1])
    me = scalars[0][0]
    sources = [item() for item in outs[:3]]
    ready = assemble(me, pieces, None, *sources, stage, scr, sems, (w1, w2))
    aux, x, b1 = [item() for item in ins]
    readin, keep, rest, cot_out = outs[3], outs[4:9], outs[9:15], outs[15]
    cot = cot_out()
    share = cot.shape[1] // count
    for r in range(count):
        start = (me ^ r) * share
        for index in range((stage.shape[2] - 2 * LANES) // LANES * 2):
            (row, lane), (low_row, low_lane) = cot_block(index, share)
            lanes = pl.ds(pl.multiple_of(start + lane, LANES), LANES)
            low_lane = 2 * LANES + low_lane
            cot[row : row + 16, lanes] = stage[r, low_row : low_row + 16, low_lane : low_lane + LANES]
    cot_out.send()

    def between():
        rest[2]()[...] = dot_nt(cot[...], w2()[...])
        rest[2].send()

    forward_body(side, aux, x, *sources, keep, field, act, readin(), ready, between)
    readin.send()
    for item in outs[:3]:
        item.send()
    readout_body(me, readin(), w1, b1, w2, [hid, *rest], full)


def second_forward(side, chan, mid, me, aux, x, pieces, w1, b1, w2):
    slots = side * side
    hidden, width = w2.shape
    got = call(
        functools.partial(second_kernel, side, len(pieces)),
        whole_shapes(chan, mid)
        + [sds((slots, chan), BF16)]
        + kept_shapes(slots, chan, mid)
        + readout_shapes(slots, chan, hidden, width, len(pieces))
        + [sds((slots, width), BF16)],
        [me],
        [aux, x, b1],
        forward_scratch(side, mid)
        + assemble_scratch(pieces, mid, slots * width // mid)
        + [
            pltpu.VMEM((slots, chan), F32),
            pltpu.VMEM((slots, hidden), BF16),
            pltpu.VMEM(w1.shape, BF16),
            pltpu.VMEM(w2.shape, BF16),
            pltpu.SemaphoreType.DMA((2,)),
        ],
        plain=[*pieces, w1, w2],
    )
    got = list(got)
    return got[3], [x] + got[:3] + got[4:9], got[9:]


def tail_kernel(placed, count, scalars, ins, outs, plain, stacked, low, cot, w2_buf, buffer, sems, out_sems):
    parts, (readin, w1, b1, grad) = ins[:count], ins[count:]
    w1_grad, b1_grad, b2_grad, w2_out = outs
    me = scalars[0][0]
    rows = readin.buffer.shape[0]
    own, w2, *rest = plain
    w2 = Later(w2, w2_buf, sems.at[1 + len(rest)])
    copies = [pltpu.make_async_copy(own, cot.at[0:rows, :], sems.at[0])]
    for r, piece in enumerate(rest):
        share = piece.shape[1]
        lanes = pl.ds(pl.multiple_of((me ^ r) * share, share), share) if placed else slice(0, share)
        copies.append(pltpu.make_async_copy(piece, cot.at[rows:, lanes], sems.at[1 + r]))
    for copy in copies:
        copy.start()
    w2.start()
    split = len(parts) // 2
    half = parts[0].buffer.shape[1]
    lanes = [pl.ds(pl.multiple_of(((me & 1) ^ odd) * half, half), half) for odd in range(2)]
    stacked[0:rows, :] = readin()[...]
    for odd, group in enumerate((parts[:split], parts[split:])):
        at = rows
        for part in group:
            count = part.buffer.shape[0]
            stacked[at : at + count, lanes[odd]] = part()[...]
            at += count
    hidden = dot_nn(stacked[...], w1()[...]) + b1()[...]
    value, slope = gelu_both(hidden)
    turned = value.T.astype(BF16)
    low[0:rows, :] = (slope[0:rows] * grad()[...]).astype(BF16)
    width = buffer.shape[2]
    flights = []
    for copy in copies:
        copy.wait()
    for r in range(cot.shape[1] // width):
        if r >= 2:
            flights[r - 2].wait()
        lanes = slice(r * width, (r + 1) * width)
        buffer[r % 2] = dot_nn(turned, cot[:, lanes])
        flights.append(pltpu.make_async_copy(buffer.at[r % 2], w2_out.target.at[:, lanes], out_sems.at[r % 2]))
        flights[-1].start()
    low[rows:, :] = (slope[rows:] * dot_nt(cot[rows:, :], w2()[...])).astype(BF16)
    w1_grad()[...] = dot_tn(stacked[...], low[...])
    w1_grad.send()
    b1_grad()[...] = jnp.sum(low[...].astype(F32), axis=0, keepdims=True)
    share = b2_grad.buffer.shape[1]
    lanes = pl.ds(pl.multiple_of(me * share, share), share)
    b2_grad()[...] = jnp.sum(cot[:, lanes].astype(F32), axis=0, keepdims=True)
    for flight in flights[-2:]:
        flight.wait()


def tail(me, b1, w1, w2, grad, readin, parts, own, rest, placed, n):
    rows, chan = readin.shape
    total = rows + sum(x.shape[0] for x in parts) // 2
    hidden, width = w2.shape
    chunk = min(width, 2048)
    return call(
        functools.partial(tail_kernel, placed, len(parts)),
        [sds((chan, hidden), F32), sds((1, hidden), F32), sds((1, width // n), F32), sds((hidden, width), F32)],
        [me],
        [*parts, readin, w1, b1, grad],
        [
            pltpu.VMEM((total, chan), BF16),
            pltpu.VMEM((total, hidden), BF16),
            pltpu.VMEM((total, width), BF16),
            pltpu.VMEM(w2.shape, BF16),
            pltpu.VMEM((2, hidden, chunk), F32),
            pltpu.SemaphoreType.DMA((2 + len(rest),)),
            pltpu.SemaphoreType.DMA((2,)),
        ],
        plain=[own, w2, *rest],
        direct=(3,),
    )


def finish_kernel(count, scalars, ins, outs, plain, scr):
    red, conv, exp, mid_gain, mid_bias, out_gain, out_bias, tokens = [item() for item in outs]
    late, middle, parts = ins[0:2], ins[2:4], ins[4 : 4 + count]
    bias, *shares = ins[4 + count :]
    value = bias()[...]
    for item in shares:
        value = value + item()[...].astype(F32)
    tokens[...] = value.astype(BF16)
    outs[7].send()
    chan, mid = red.shape[2], conv.shape[3]
    held = red.shape[1]
    reduce_end, conv_end, expand_end, mid_end, end = columns(chan, mid)
    plane = scalars[1][0] & 1
    few = held // 2

    def from_pair(pair, base, k):
        mine, other = [item()[...] for item in pair]
        for odd in range(2):
            value = jnp.where(plane == odd, mine, other)
            rows = slice(odd * few, odd * few + few)
            for j in range(TAPS):
                at = reduce_end + j * mid - base
                conv[k, j, rows, :] = value[:, at : at + mid].astype(F32)
            exp[k, rows, :] = value[:, conv_end - base : expand_end - base].astype(F32)
            if base == 0:
                red[k, rows, :] = value[:, 0:reduce_end].astype(F32)
                scr[k, rows, :] = value[:, expand_end:end].astype(F32)

    scr[...] = jnp.zeros_like(scr)
    from_pair(late, 0, 1)
    from_pair(middle, reduce_end, 0)
    total = parts[0]()[...]
    for part in parts[1:]:
        total = total + part()[...].astype(F32)
    red[0] = total[:, 0:reduce_end]
    scr[0, 0:held, :] = total[:, reduce_end:]
    for k in range(2):
        flat = scr[k, :, 0:LANES].T
        for which in range(2):
            mid_gain[k, which : which + 1, :] = flat[2 * which : 2 * which + 1, 0:held]
            mid_bias[k, which : which + 1, :] = flat[2 * which + 1 : 2 * which + 2, 0:held]
        out_gain[k : k + 1, :] = scr[k, 0:1, LANES : LANES + out_gain.shape[1]]
        out_bias[k : k + 1, :] = scr[k, 1:2, LANES : LANES + out_bias.shape[1]]


def finish(me, plane, late, middle, parts, chan, mid, share, bias, shares):
    held = parts[0].shape[0]
    outs = [
        sds((2, held, chan), F32),
        sds((2, TAPS, held, mid), F32),
        sds((2, held, chan), F32),
        sds((2, 2, held), F32),
        sds((2, 2, held), F32),
        sds((2, share), F32),
        sds((2, share), F32),
        sds(shares[0].shape, BF16),
    ]
    return call(
        functools.partial(finish_kernel, len(parts)),
        outs,
        [me, plane],
        [*late, *middle, *parts, bias, *shares],
        [pltpu.VMEM((2, LANES, 2 * LANES), F32)],
    )


def iota(shape, dim):
    return lax.broadcasted_iota(jnp.int32, shape, dim).astype(F32)


def whole_part(value, divisor):
    return jnp.floor((value + 0.5) * (1.0 / divisor))


def table_at(target, place, extent):
    begin = whole_part(target * extent, POOLED)
    ending = whole_part((target + 1.0) * extent + (POOLED - 1), POOLED)
    inside = jnp.where((place >= begin) & (place < ending), 1.0, 0.0)
    return inside / (ending - begin)


def facts_kernel(scalars, ins, outs, plain):
    extent = scalars[0][0].astype(F32)
    for side, out in ((GRID, outs[0]), (POOLED, outs[1])):
        slots = side * side
        place = iota((slots, 1), 0)
        row = whole_part(place, side)
        column = place - row * side
        out()[:, 1:2] = jnp.where(column > 0.5, 1.0, 0.0)
        out()[:, 2:3] = jnp.where(column < side - 1.5, 1.0, 0.0)
        if side == GRID:
            out()[:, 0:1] = jnp.where((row < extent) & (column < extent), 1.0, 0.0)
        else:
            out()[:, 0:1] = jnp.ones((slots, 1), F32)
    shape = outs[2]().shape
    target, place = iota((shape[0], 1), 0), iota((1, shape[1]), 1)
    up, across = whole_part(target, POOLED), whole_part(place, GRID)
    rows = table_at(up, across, extent)
    lanes = table_at(target - up * POOLED, place - across * GRID, extent)
    outs[2]()[...] = (rows * lanes).astype(BF16)


def facts(grid):
    slots, few = GRID * GRID, POOLED * POOLED
    return call(
        facts_kernel,
        [sds((slots, LANES), F32), sds((few, LANES), F32), sds((few, slots), BF16)],
        [grid],
        [],
    )


def per_device(
    features,
    grid,
    reduce_w,
    conv_w,
    expand_w,
    mid_gain,
    mid_bias,
    out_gain,
    out_bias,
    read_w1,
    read_b1,
    read_w2,
    read_b2,
    cotangent,
):
    n = lax.axis_size("ch")
    chan, mid = reduce_w.shape[1], conv_w.shape[2]
    held, share = reduce_w.shape[2], features.shape[0]
    aligned = share == LANES and held % 16 == 0
    index = lax.axis_index("ch").astype(jnp.int32)
    planes = lax.axis_size("img")
    me = index[None]
    plane = lax.axis_index("img").astype(jnp.int32)[None]

    feat = jnp.transpose(features[:, 0, :])
    cot = jnp.transpose(cotangent[:, 0, :])
    red = jnp.transpose(reduce_w, (0, 2, 1))
    conv = jnp.transpose(conv_w, (0, 1, 3, 2))
    norms = (mid_gain, mid_bias, out_gain, out_bias)
    few = cot.shape[0]
    slot_facts, few_facts, spread = facts(grid)

    bias_one = read_b1[None, :]

    if aligned:
        (first_packet,) = pack(0, feat, red, conv, expand_w, *norms)
        far = neighbours(first_packet)
        second_packet, cot = pack(1, cot, red, conv, expand_w, *norms, after=[first_packet])

        (second_packet,) = gate([second_packet], far[2])

    cot_rest = [ppermute_xor(cot, "img", 1)]
    held_cot = join(cot, cot_rest[0])

    if aligned:
        second_far = neighbours(second_packet)
        far = dict(zip(far, gate(list(far.values()), held_cot, spread)))
        (held_cot,) = gate([held_cot], *far.values())
        cot_rest = doubled(cot_rest, held_cot)
        first_pieces = with_cores(first_packet, far)
        pooled, saved_first = block_forward(GRID, chan, mid, me, slot_facts, spread, first_pieces, None)
        far = dict(zip(second_far, gate(list(second_far.values()), pooled, *cot_rest)))
        second_pieces = with_cores(second_packet, far)
        readin, saved_second, got = second_forward(
            POOLED, chan, mid, me, few_facts, pooled, second_pieces, read_w1, bias_one, read_w2
        )
        mine, theirs, own_grad, half_in, keep, send, cot_own = got
    else:
        rows = jnp.concatenate(
            [red, jnp.transpose(conv, (0, 2, 1, 3)).reshape(2, held, TAPS * mid), expand_w], axis=2
        )
        rows = lax.all_gather(rows, "ch", axis=1, tiled=True)
        mids = jnp.stack([mid_gain, mid_bias], axis=2).reshape(2, 4, held)
        mids = jnp.pad(lax.all_gather(mids, "ch", axis=2, tiled=True), ((0, 0), (0, 4), (0, 0)))
        outs = jnp.stack([out_gain, out_bias], axis=1)
        outs = jnp.pad(lax.all_gather(outs, "ch", axis=2, tiled=True), ((0, 0), (0, 6), (0, 0)))
        x_whole = lax.all_gather(feat, "ch", axis=1, tiled=True)
        pooled, saved_first = block_forward(
            GRID, chan, mid, me, slot_facts, spread, None, (x_whole, rows[0], mids[0], outs[0])
        )
        readin, saved_second = block_forward(
            POOLED, chan, mid, me, few_facts, None, None, (pooled, rows[1], mids[1], outs[1])
        )
        cot_own = lax.all_gather(cot, "ch", axis=1, tiled=True)
        mine, theirs, own_grad, half_in, keep, send = readout(me, readin, read_w1, bias_one, read_w2, cot_own, n)

    if not aligned:
        cot_rest = doubled(cot_rest, held_cot)

    half = summed(mine, ppermute_xor(theirs, "ch", 1))
    far = neighbours(half)
    cot_rest = join(*cot_rest, after=[half])
    got = ppermute_xor(send, "ch", 1)
    shares = [summed(keep[q], got[q]) for q in range(n // 2)]
    far = dict(zip(far, gate(list(far.values()), cot_rest, shares[0])))
    if aligned:
        (cot_rest,) = gate([cot_rest], *far.values())
        cot_far = neighbours(cot_rest)
    (half_in,) = gate([half_in], half)
    parts = [ppermute_xor(half_in, "img", m) for m in (1, 2) if m < planes]
    grad_pieces = with_cores(half, far)

    pooled_grad, late_mine, late_theirs, late_out = late_backward(
        POOLED, held, me, plane, few_facts, grad_pieces, saved_second
    )
    late_got = ppermute_xor(late_theirs, "img", 1)
    (half_in,) = gate([half_in], pooled_grad)
    parts += [ppermute_xor(half_in, "img", m) for m in range(3, planes)]
    own_lanes = share if aligned else 0
    middle_mine, middle_theirs, *upper = upper_backward(
        GRID, held, me, plane, slot_facts, spread, pooled_grad, saved_first, own_lanes
    )
    middle_got = ppermute_xor(middle_theirs, "img", 1)
    (late_got,) = gate([late_got], upper[0])
    late_half = summed(late_mine, late_got)
    late_got = ppermute_xor(late_half, "img", 2)
    parts = gate(parts, upper[0])
    parts = [*parts, *[ppermute_xor(x, "ch", 1) for x in parts]]
    if aligned:
        cot_far = dict(zip(cot_far, gate(list(cot_far.values()), upper[0])))
        rest_pieces = with_cores(cot_rest, cot_far)
    else:
        rest_pieces = [lax.all_gather(cot_rest, "ch", axis=1, tiled=True)]
    feat_grad, last_grads, last_low = lower_backward(
        GRID, held, me, slot_facts, upper, saved_first, own_lanes
    )
    last = [last_grads] + along_images(last_low)
    late_got, middle_got = gate([late_got, middle_got], last_grads)
    middle_half = summed(middle_mine, middle_got)
    middle_got = ppermute_xor(middle_half, "img", 2)
    late_half = summed(late_half, late_got)
    for mask in (1 << k for k in range(2, planes.bit_length() - 1)):
        late_half = summed(late_half, ppermute_xor(late_half, "img", mask))
    late = (late_half, ppermute_xor(late_half, "img", 1))
    w1_grad, b1_grad, b2_grad, w2_grad = tail(
        me, bias_one, read_w1, read_w2, own_grad, readin, parts, cot_own, rest_pieces, aligned, n
    )
    (middle_got,) = gate([middle_got], b1_grad)
    middle_half = summed(middle_half, middle_got)
    for mask in (1 << k for k in range(2, planes.bit_length() - 1)):
        middle_half = summed(middle_half, ppermute_xor(middle_half, "img", mask))
    middle = (middle_half, ppermute_xor(middle_half, "img", 1))
    shares = gate(shares, middle_half)
    shares = [shares[0]] + [ppermute_xor(shares[q], "ch", 2 * q) for q in range(1, n // 2)]

    red_grad, conv_grad, exp_grad, mid_gain_grad, mid_bias_grad, out_gain_grad, out_bias_grad, tokens = finish(
        me, plane, late, middle, last, chan, mid, share, read_b2[None, :], shares
    )
    if not aligned:
        feat_grad = lax.dynamic_slice_in_dim(feat_grad, index * share, share, 1)
        both = jnp.stack([upper[3], late_out])
        both = lax.dynamic_slice_in_dim(both, index * share, share, 2)
        both = lax.psum(both.astype(BF16), "img").astype(F32)
        out_gain_grad, out_bias_grad = both[:, 0], both[:, 1]

    return (
        jnp.transpose(tokens)[:, None, :],
        jnp.transpose(feat_grad)[:, None, :],
        jnp.transpose(red_grad, (0, 2, 1)),
        jnp.transpose(conv_grad, (0, 1, 3, 2)),
        exp_grad,
        mid_gain_grad,
        mid_bias_grad,
        out_gain_grad,
        out_bias_grad,
        w1_grad,
        b1_grad[0],
        w2_grad,
        b2_grad[0],
    )


def solution(mesh):
    return jax.shard_map(
        per_device,
        mesh=mesh,
        in_specs=(
            P("ch", "img", None),
            P("img"),
            P(None, None, "ch"),
            P(None, None, None, "ch"),
            P(None, "ch", None),
            P(None, None, "ch"),
            P(None, None, "ch"),
            P(None, "ch"),
            P(None, "ch"),
            P(None, "ch"),
            P("ch"),
            P("ch", None),
            P("ch"),
            P("ch", "img", None),
        ),
        out_specs=(
            P("ch", "img", None),
            P("ch", "img", None),
            P(None, None, "ch"),
            P(None, None, None, "ch"),
            P(None, "ch", None),
            P(None, None, "ch"),
            P(None, None, "ch"),
            P(None, "ch"),
            P(None, "ch"),
            P(None, "ch"),
            P("ch"),
            P("ch", None),
            P("ch"),
        ),
        check_vma=False,
    )
```

```python
import functools

import jax
import jax.numpy as jnp
from jax import lax
from jax.experimental import pallas as pl
from jax.experimental.pallas import tpu as pltpu
from jax.sharding import PartitionSpec as P

GRID = 24
POOLED = 12
EPSILON = 1e-06
OFFSETS = [(-1, -1), (-1, 0), (-1, 1), (0, -1), (0, 0), (0, 1), (1, -1), (1, 0), (1, 1)]
TAPS = len(OFFSETS)
LANES = 128
VMEM_MIB = 64
BF16 = jnp.bfloat16
F32 = jnp.float32
SMEM = pl.BlockSpec(memory_space=pltpu.SMEM)
ANY = pl.BlockSpec(memory_space=pl.ANY)


def dot_nn(left, right):
    return lax.dot_general(left, right, (((1,), (0,)), ((), ())), preferred_element_type=F32)


def dot_nt(left, right):
    return lax.dot_general(left, right, (((1,), (1,)), ((), ())), preferred_element_type=F32)


def dot_tn(left, right):
    return lax.dot_general(left, right, (((0,), (0,)), ((), ())), preferred_element_type=F32)


def sds(shape, dtype):
    return jax.ShapeDtypeStruct(tuple(shape), dtype)


class Inward:
    def __init__(self, source, buffer, sem):
        self.copy = pltpu.make_async_copy(source, buffer, sem)
        self.buffer, self.waited = buffer, False
        self.copy.start()

    def __call__(self):
        if not self.waited:
            self.copy.wait()
            self.waited = True
        return self.buffer


class Outward:
    def __init__(self, target, buffer, sem):
        self.copy = None if buffer is None else pltpu.make_async_copy(buffer, target, sem)
        self.target, self.buffer, self.sent = target, buffer, False

    def __call__(self):
        return self.buffer

    def send(self):
        if not self.sent:
            self.copy.start()
            self.sent = True


def call(body, outs, scalars, args, scratch=(),  plain=(), after=(), direct=()):
    count = (len(scalars), len(args), len(plain), len(after), len(outs))

    def kernel(*refs):
        refs = list(refs)

        def take(k):
            got = refs[:k]
            del refs[:k]
            return got

        scalar_refs, sources, plain_refs, _, targets = [take(k) for k in count]
        in_buffers = take(len(args))
        out_buffers = [None if i in direct else refs.pop(0) for i in range(len(outs))]
        in_sems = refs.pop(0) if args else None
        out_sems = refs.pop(0)
        inward = [Inward(s, b, in_sems.at[i]) for i, (s, b) in enumerate(zip(sources, in_buffers))]
        outward = [Outward(t, b, out_sems.at[i]) for i, (t, b) in enumerate(zip(targets, out_buffers))]
        made = [item for item in outward if item.buffer is not None]
        body(scalar_refs, inward, outward, plain_refs, *refs)
        for item in inward:
            item()
        for item in made:
            item.send()
        for item in made:
            item.copy.wait()

    results = [x for i, x in enumerate(outs) if i not in direct]
    shapes = [pltpu.VMEM(x.shape, x.dtype) for x in list(args) + results]
    sems = ([pltpu.SemaphoreType.DMA((len(args),))] if args else []) + [
        pltpu.SemaphoreType.DMA((len(outs),))
    ]
    return pl.pallas_call(
        kernel,
        out_shape=list(outs),
        in_specs=[SMEM] * len(scalars) + [ANY] * (len(args) + len(plain) + len(after)),
        out_specs=[ANY] * len(outs),
        scratch_shapes=shapes + sems + list(scratch),
        compiler_params=pltpu.CompilerParams(vmem_limit_bytes=VMEM_MIB << 20),
        cost_estimate=pl.CostEstimate(flops=0, bytes_accessed=0, transcendentals=0),
    )(*scalars, *args, *plain, *after)


def gate(values, *after):
    def nothing(*refs):
        pass

    return pl.pallas_call(
        nothing,
        out_shape=[sds(v.shape, v.dtype) for v in values],
        in_specs=[ANY] * (len(values) + len(after)),
        out_specs=[ANY] * len(values),
        input_output_aliases={i: i for i in range(len(values))},
        compiler_params=pltpu.CompilerParams(vmem_limit_bytes=VMEM_MIB << 20),
    )(*values, *after)


def join_body(scalars, ins, outs, plain):
    at = 0
    for item in ins:
        rows = item.buffer.shape[0]
        outs[0]()[at : at + rows, :] = item()[...]
        at += rows


def join(*parts, after=()):
    rows = sum(x.shape[0] for x in parts)
    shape = sds((rows, parts[0].shape[1]), parts[0].dtype)
    return call(join_body, [shape], [], list(parts), after=after)[0]


def ppermute_xor(x, axis, mask):
    return lax.ppermute(x, axis, [(i, i ^ mask) for i in range(lax.axis_size(axis))])


def neighbours(x):
    n = lax.axis_size("ch")
    return {r: ppermute_xor(x, "ch", r) for r in range(n - 2, 0, -2)}


def with_cores(x, far):
    n = lax.axis_size("ch")
    pieces = [None] * n
    for r in range(0, n, 2):
        pieces[r] = far[r] if r else x
        pieces[r + 1] = ppermute_xor(pieces[r], "ch", 1)
    return pieces


def along_images(x):
    return [ppermute_xor(x, "img", m) for m in range(1, lax.axis_size("img"))]


def pair_sum(mine, low, after):
    masks = [1 << k for k in range(lax.axis_size("img").bit_length() - 1)]
    total, got = mine, ppermute_xor(low, "img", masks[0])
    for mask in masks[1:]:
        (got,) = gate([got], after)
        total = (total.astype(F32) + got.astype(F32)).astype(BF16)
        got = ppermute_xor(total, "img", mask)
    return total, got


def doubled(parts, held):
    planes = lax.axis_size("img")
    for mask in (1 << k for k in range(1, planes.bit_length() - 1)):
        parts.append(ppermute_xor(held, "img", mask))
        if 2 * mask < planes:
            held = join(held, parts[-1])
    return parts


def summed(left, right):
    return (left.astype(F32) + right.astype(F32)).astype(BF16)


def rows_of(value, index, count):
    return value[pl.ds(pl.multiple_of(index * count, count), count), :]


def half_of(value, second, count):
    return jnp.where(second == 1, value[count : 2 * count, :], value[0:count, :])


def columns(chan, mid):
    reduce_end = chan
    conv_end = reduce_end + TAPS * mid
    expand_end = conv_end + chan
    return reduce_end, conv_end, expand_end, expand_end + LANES, expand_end + 2 * LANES


def split_low(value):
    high = value.astype(BF16).astype(F32)
    return high, value - high


def cot_block(index, width):
    per = width // LANES
    return (index // per * 16, index % per * LANES), (index % 2 * 16, index // 2 * LANES)


def pack_body(layer, scalars, ins, outs, plain, scr, *bufs):
    feat, mid_gain, mid_bias, out_gain, out_bias = ins
    red, conv, exp = plain
    red_buf, conv_buf, exp_buf, sems = bufs
    copies = [
        pltpu.make_async_copy(source.at[layer], buffer, sems.at[i])
        for i, (source, buffer) in enumerate(((red, red_buf), (conv, conv_buf), (exp, exp_buf)))
    ]
    for copy in copies:
        copy.start()
    packet = outs[0]()
    held, chan, mid = red_buf.shape[0], red_buf.shape[1], conv_buf.shape[2]
    reduce_end, conv_end, expand_end, mid_end, end = columns(chan, mid)
    scr[...] = jnp.zeros_like(scr)
    for which in range(2):
        for kind, ref in enumerate((mid_gain(), mid_bias())):
            high, low = split_low(ref[layer, which : which + 1, :])
            at = 4 * which + 2 * kind
            scr[at : at + 1, 0:held] = high
            scr[at + 1 : at + 2, 0:held] = low
    packet[:, expand_end:mid_end] = scr[...].T[0:held, :].astype(BF16)
    scr[...] = jnp.zeros_like(scr)
    for kind, ref in enumerate((out_gain(), out_bias())):
        high, low = split_low(ref[layer : layer + 1, :])
        scr[2 * kind : 2 * kind + 1, :] = high
        scr[2 * kind + 1 : 2 * kind + 2, :] = low
    packet[:, mid_end:end] = scr[0:held, :].astype(BF16)
    feat = feat()
    if layer == 0:
        for b in range(feat.shape[0] // held):
            packet[:, end + b * LANES : end + (b + 1) * LANES] = feat[b * held : (b + 1) * held, :]
    else:
        for index in range(feat.shape[0] // 16 * (feat.shape[1] // LANES)):
            (row, lane), (low_row, low_lane) = cot_block(index, feat.shape[1])
            packet[low_row : low_row + 16, end + low_lane : end + low_lane + LANES] = feat[
                row : row + 16, lane : lane + LANES
            ]
        outs[1]()[...] = feat[...]
    for copy in copies:
        copy.wait()
    packet[:, 0:reduce_end] = red_buf[...]
    for j in range(TAPS):
        packet[:, reduce_end + j * mid : reduce_end + (j + 1) * mid] = conv_buf[j]
    packet[:, conv_end:expand_end] = exp_buf[...]


def pack(layer, extra, red, conv, exp, mid_gain, mid_bias, out_gain, out_bias, after=()):
    held, chan = red.shape[1:]
    mid = conv.shape[3]
    width = columns(chan, mid)[-1] + extra.shape[0] * extra.shape[1] // held
    outs = [sds((held, width), BF16)]
    if layer:
        outs.append(sds(extra.shape, BF16))
    return call(
        functools.partial(pack_body, layer),
        outs,
        [],
        [extra, mid_gain, mid_bias, out_gain, out_bias],
        [
            pltpu.VMEM((LANES, LANES), F32),
            pltpu.VMEM(red.shape[1:], BF16),
            pltpu.VMEM(conv.shape[1:], BF16),
            pltpu.VMEM(exp.shape[1:], BF16),
            pltpu.SemaphoreType.DMA((3,)),
        ],
        plain=[red, conv, exp],
        after=after,
    )


def assemble(me, pieces, x_ref, w_ref, mid_ref, out_ref, stage, scr, sems, then=()):
    held = pieces[0].shape[0]
    chan, mid = out_ref.shape[1], w_ref.shape[0]
    reduce_end, conv_end, expand_end, mid_end, end = columns(chan, mid)
    width = stage.shape[2]
    parts, copies = [], []
    for r, piece in enumerate(pieces):
        parts.append(
            pltpu.make_async_copy(piece.at[:, expand_end : expand_end + width], stage.at[r], sems.at[2, r])
        )
        parts[-1].start()
    for k, (start, stop) in enumerate(((0, reduce_end), (reduce_end, expand_end))):
        for r, piece in enumerate(pieces):
            rows = pl.ds(pl.multiple_of((me ^ r) * held, held), held)
            copies.append(
                pltpu.make_async_copy(piece.at[:, start:stop], w_ref.at[rows, start:stop], sems.at[k, r])
            )
            copies[-1].start()
    for copy in then:
        copy.start()
    for r in range(len(pieces)):
        parts[r].wait()
        rows = pl.ds(pl.multiple_of((me ^ r) * held, held), held)
        lanes = pl.ds(pl.multiple_of((me ^ r) * LANES, LANES), LANES)
        scr[rows, :] = stage[r, :, 0:LANES].astype(F32)
        block = stage[r, :, LANES : 2 * LANES].astype(F32)
        out_ref[0:1, lanes] = block[0:1, :] + block[1:2, :]
        out_ref[1:2, lanes] = block[2:3, :] + block[3:4, :]
        for b in range(width // LANES - 2 if x_ref is not None else 0):
            at = (b + 2) * LANES
            x_ref[b * held : (b + 1) * held, lanes] = stage[r, :, at : at + LANES]
    flat = scr[...].T
    for q in range(4):
        mid_ref[q : q + 1, :] = flat[2 * q : 2 * q + 1, :] + flat[2 * q + 1 : 2 * q + 2, :]

    def wait(some):
        def waiting():
            for copy in some:
                copy.wait()

        return waiting

    return wait(copies[: len(pieces)]), wait(copies[len(pieces) :])


def at_once():
    pass


def sigmoid(value):
    return 0.5 * jnp.tanh(0.5 * value) + 0.5


def silu(value):
    return value * sigmoid(value)


def silu_slope(value):
    gate = sigmoid(value)
    return gate * (1.0 + value * (1.0 - gate))


def unit_of(values):
    inverse = 1.0 / values.shape[-1]
    center = jnp.sum(values, axis=-1, keepdims=True) * inverse
    spread = jnp.sum(values * values, axis=-1, keepdims=True) * inverse - center * center
    factor = lax.rsqrt(spread + EPSILON)
    return (values - center) * factor, factor


def chunked(slots, body, carry=None):
    return body(slice(0, slots), 0, carry)


def pad_of(side):
    return -(-(side + 1) // 16) * 16


def shift_columns(field, side, slots, aux_ref):
    pad = pad_of(side)
    field[0, pad : pad + slots, :] = field[1, pad - 1 : pad - 1 + slots, :] * aux_ref[:, 1:2]
    field[2, pad : pad + slots, :] = field[1, pad + 1 : pad + 1 + slots, :] * aux_ref[:, 2:3]


def clear_edges(field, side, slots):
    pad = pad_of(side)
    for k in range(3):
        field[k, 0:pad, :] = jnp.zeros((pad, field.shape[2]), F32)
        field[k, pad + slots : pad + slots + pad, :] = jnp.zeros((pad, field.shape[2]), F32)


def tap(field, side, slots, rise, step):
    at = pad_of(side) + rise * side
    return field[step + 1, at : at + slots, :].astype(BF16)


def forward_body(side, aux, x_ref, w_ref, mid_ref, out_ref, keep, field, act, finish, ready=(at_once, at_once), between=at_once):
    u1, u2, u3, fac, pat = [item() for item in keep]
    slots = x_ref.shape[0]
    chan, mid = out_ref.shape[1], w_ref.shape[0]
    reduce_end, conv_end, expand_end, _, _ = columns(chan, mid)
    pad = pad_of(side)
    clear_edges(field, side, slots)
    ready[0]()
    u1[...] = dot_nt(x_ref[...], w_ref[:, 0:reduce_end])

    def first(rows, start, carry):
        unit, factor = unit_of(u1[rows, :])
        u1[rows, :] = unit
        fac[rows, 0:1] = factor
        value = silu(unit * mid_ref[0:1, :] + mid_ref[1:2, :]) * aux[rows, 0:1]
        field[1, pl.ds(pad + start, unit.shape[0]), :] = value
        return carry

    chunked(slots, first)
    keep[0].send()
    shift_columns(field, side, slots, aux)
    for j, (rise, step) in enumerate(OFFSETS):
        pat[:, j * mid : (j + 1) * mid] = tap(field, side, slots, rise, step)
    keep[4].send()
    ready[1]()
    u2[...] = dot_nt(pat[...], w_ref[:, reduce_end:conv_end])

    def second(rows, start, carry):
        unit, factor = unit_of(u2[rows, :])
        u2[rows, :] = unit
        fac[rows, 1:2] = factor
        act[rows, :] = silu(unit * mid_ref[2:3, :] + mid_ref[3:4, :]).astype(BF16)
        return carry

    chunked(slots, second)
    keep[1].send()
    between()
    u3[...] = dot_nn(act[...], w_ref[:, conv_end:expand_end])

    def third(rows, start, carry):
        unit, factor = unit_of(u3[rows, :])
        u3[rows, :] = unit
        fac[rows, 2:3] = factor
        summed = unit * out_ref[0:1, :] + out_ref[1:2, :] + x_ref[rows, :].astype(F32)
        finish[rows, :] = (silu(summed) * aux[rows, 0:1]).astype(BF16)
        return carry

    chunked(slots, third)
    keep[2].send()
    keep[3].send()


def forward_kernel(side, pooling, assembled, scalars, ins, outs, plain, *scratch):
    field, act, *rest = scratch
    ins, outs = list(ins), list(outs)
    aux = ins.pop(0)()
    if pooling:
        spread, finish = ins.pop(0), rest.pop(0)
    ready, made = (at_once, at_once), []
    if assembled:
        sources = [item() for item in ins]
    else:
        made, outs = outs[:4], outs[4:]
        sources = [item() for item in made]
        ready = assemble(scalars[0][0], plain, *sources, *rest)
    result = outs[0]
    if not pooling:
        finish = result()
    if made:
        made[0].send()
    forward_body(side, aux, *sources, outs[1:], field, act, finish, ready)
    for item in made:
        item.send()
    if pooling:
        result()[...] = dot_nn(spread()[...], finish[...]).astype(BF16)


def kept_shapes(slots, chan, mid):
    return [
        sds((slots, mid), F32),
        sds((slots, mid), F32),
        sds((slots, chan), F32),
        sds((slots, LANES), F32),
        sds((slots, TAPS * mid), BF16),
    ]


def whole_shapes(chan, mid):
    return [sds((mid, columns(chan, mid)[2]), BF16), sds((8, mid), F32), sds((8, chan), F32)]


def forward_scratch(side, mid):
    slots = side * side
    return [
        pltpu.VMEM((3, slots + 2 * pad_of(side), mid), F32),
        pltpu.VMEM((slots, mid), BF16),
    ]


def assemble_scratch(pieces, mid, extra):
    held = mid // len(pieces)
    return [
        pltpu.VMEM((len(pieces), held, 2 * LANES + extra), BF16),
        pltpu.VMEM((mid, LANES), F32),
        pltpu.SemaphoreType.DMA((3, len(pieces))),
    ]


def block_forward(side, chan, mid, me, aux, spread, pieces, assembled):
    slots = side * side
    pooling = spread is not None
    args = [aux] + ([spread] if pooling else [])
    outs = [sds((spread.shape[0] if pooling else slots, chan), BF16)] + kept_shapes(slots, chan, mid)
    scratch = forward_scratch(side, mid)
    if pooling:
        scratch.append(pltpu.VMEM((slots, chan), BF16))
    if assembled is not None:
        args += list(assembled)
    else:
        outs = [sds((slots, chan), BF16)] + whole_shapes(chan, mid) + outs
        scratch += assemble_scratch(pieces, mid, slots * LANES * len(pieces) // mid)
    got = call(
        functools.partial(forward_kernel, side, pooling, assembled is not None),
        outs,
        [me],
        args,
        scratch,
        plain=list(pieces or []),
    )
    got = list(got)
    source, got = (list(assembled), got) if assembled is not None else (got[:4], got[4:])
    return got[0], source + got[1:]


def fold(value):
    return jnp.sum(value.reshape(value.shape[0] // 8, 8, value.shape[1]), axis=0)


def norm_back(upstream, unit, factor, gain):
    inverse = 1.0 / unit.shape[-1]
    scaled = upstream * gain
    first = jnp.sum(scaled, axis=-1, keepdims=True) * inverse
    second = jnp.sum(scaled * unit, axis=-1, keepdims=True) * inverse
    return factor * (scaled - first - unit * second)


def back_upper(side, me, aux, up, x_ref, w_in, mid_in, out_ref, u2_in, u3, fac, pat_in, sg, eg, turned, field, dense, accum, out_rows, grads):
    slots, chan = eg.shape
    mid = dense.shape[1]
    held = grads.shape[0]
    reduce_end, conv_end, expand_end, _, _ = columns(chan, mid)
    pad = pad_of(side)
    clear_edges(field, side, slots)

    def third(rows, start, carry):
        gain_acc, bias_acc = carry
        unit = u3[rows, :]
        summed = unit * out_ref[0:1, :] + out_ref[1:2, :] + x_ref[rows, :].astype(F32)
        grad = silu_slope(summed) * (up[rows, :] * aux[rows, 0:1])
        sg[rows, :] = grad
        eg[rows, :] = norm_back(grad, unit, fac[rows, 2:3], out_ref[0:1, :]).astype(BF16)
        return gain_acc + fold(grad * unit), bias_acc + fold(grad)

    zero = jnp.zeros((8, chan), F32)
    gain_acc, bias_acc = chunked(slots, third, (zero, zero))
    out_rows[...] = jnp.zeros_like(out_rows)
    out_rows[0:1, :] = jnp.sum(gain_acc, axis=0, keepdims=True)
    out_rows[1:2, :] = jnp.sum(bias_acc, axis=0, keepdims=True)

    u2, mid_ref, w_ref = u2_in(), mid_in(), w_in()
    dense[...] = silu(u2[...] * mid_ref[2:3, :] + mid_ref[3:4, :])
    turned[...] = dense[...].T
    grads[:, conv_end:expand_end] = dot_nn(rows_of(turned, me, held).astype(BF16), eg[...])
    dense[...] = dot_nt(eg[...], w_ref[:, conv_end:expand_end])
    small = jnp.zeros((8, mid), F32)

    def second(rows, start, carry):
        gain_sum, bias_sum = carry
        unit = u2[rows, :]
        grad = silu_slope(unit * mid_ref[2:3, :] + mid_ref[3:4, :]) * dense[rows, :]
        back = norm_back(grad, unit, fac[rows, 1:2], mid_ref[2:3, :])
        field[1, pl.ds(pad + start, unit.shape[0]), :] = back
        return gain_sum + fold(grad * unit), bias_sum + fold(grad)

    gain_two, bias_two = chunked(slots, second, (small, small))
    accum[2:3, :] = jnp.sum(gain_two, axis=0, keepdims=True)
    accum[3:4, :] = jnp.sum(bias_two, axis=0, keepdims=True)
    turned[...] = field[1, pad : pad + slots, :].T
    pat = pat_in()
    grads[:, reduce_end:conv_end] = dot_nn(rows_of(turned, me, held).astype(BF16), pat[...])


def back_lower(side, me, aux, x_ref, w_ref, mid_ref, u1_in, fac, turned, field, dense, accum, out_rows, grads, tail):
    slots, mid = dense.shape
    chan = x_ref.shape[1]
    held = grads.shape[0]
    reduce_end = columns(chan, mid)[0]
    shift_columns(field, side, slots, aux)
    for j, (rise, step) in enumerate(OFFSETS):
        at = reduce_end + j * mid
        term = dot_nn(tap(field, side, slots, -rise, -step), w_ref[:, at : at + mid])
        dense[...] = term if j == 0 else dense[...] + term
    u1 = u1_in()
    small = jnp.zeros((8, mid), F32)

    def first(rows, start, carry):
        gain_sum, bias_sum = carry
        unit = u1[rows, :]
        grad = silu_slope(unit * mid_ref[0:1, :] + mid_ref[1:2, :]) * (dense[rows, :] * aux[rows, 0:1])
        dense[rows, :] = norm_back(grad, unit, fac[rows, 0:1], mid_ref[0:1, :])
        return gain_sum + fold(grad * unit), bias_sum + fold(grad)

    gain_one, bias_one = chunked(slots, first, (small, small))
    accum[0:1, :] = jnp.sum(gain_one, axis=0, keepdims=True)
    accum[1:2, :] = jnp.sum(bias_one, axis=0, keepdims=True)
    turned[...] = dense[...].T
    grads[:, 0:reduce_end] = dot_nn(rows_of(turned, me, held).astype(BF16), x_ref[...])
    turned[:, 0:LANES] = accum[...].T
    grads[:, tail : tail + LANES] = rows_of(turned, me, held)[:, 0:LANES]
    grads[:, tail + LANES : tail + 2 * LANES] = jnp.zeros((held, LANES), F32)
    if chan // (mid // held) == LANES:
        lanes = pl.ds(pl.multiple_of(me * LANES, LANES), LANES)
        grads[0:8, tail + LANES : tail + 2 * LANES] = out_rows[:, lanes]


def split_rows(grads, plane, mine, theirs, start):
    count, width = mine.buffer.shape
    theirs()[...] = half_of(grads, 1 - plane, count)[:, start : start + width].astype(BF16)
    theirs.send()
    mine()[...] = half_of(grads, plane, count)[:, start : start + width]
    mine.send()


def back_scratch(side, slots, chan, mid):
    return [
        pltpu.VMEM((slots, chan), F32),
        pltpu.VMEM((slots, chan), BF16),
        pltpu.VMEM((mid, slots), F32),
        pltpu.VMEM((3, slots + 2 * pad_of(side), mid), F32),
        pltpu.VMEM((slots, mid), F32),
        pltpu.VMEM((LANES, mid), F32),
    ]


def late_kernel(side, scalars, ins, outs, plain, up, grads, sg, eg, turned, field, dense, accum):
    pieces = ins[:-10]
    aux, x_in, out_in, u3_in, fac_in, mid_in, u2_in, w_in, pat_in, u1_in = ins[-10:]
    x_grad, mine, theirs, out_rows = outs
    me, plane = scalars[0][0], scalars[1][0] & 1
    half = pieces[0].buffer.shape[1]
    for odd in range(2):
        core = (me & 1) ^ odd
        total = pieces[odd]()[...].astype(F32)
        for piece in pieces[odd + 2 :: 2]:
            total = total + piece()[...].astype(F32)
        up[:, pl.ds(pl.multiple_of(core * half, half), half)] = total
    aux, x_ref, out_ref, u3, fac = aux(), x_in(), out_in(), u3_in(), fac_in()
    chan, mid = eg.shape[1], dense.shape[1]
    reduce_end, _, expand_end, _, _ = columns(chan, mid)
    accum[...] = jnp.zeros_like(accum)
    back_upper(
        side, me, aux, up, x_ref, w_in, mid_in, out_ref, u2_in, u3, fac, pat_in,
        sg, eg, turned, field, dense, accum, out_rows(), grads,
    )
    back_lower(
        side, me, aux, x_ref, w_in(), mid_in(), u1_in, fac, turned, field, dense, accum, out_rows(), grads, expand_end,
    )
    split_rows(grads, plane, mine, theirs, 0)
    x_grad()[...] = (dot_nn(dense[...].astype(BF16), w_in()[:, 0:reduce_end]) + sg[...]).astype(BF16)


def late_backward(side, held, me, plane, aux, pieces, saved):
    x, w, mids, outs, u1, u2, u3, fac, pat = saved
    slots, chan = x.shape
    mid = w.shape[0]
    end = columns(chan, mid)[-1]
    return call(
        functools.partial(late_kernel, side),
        [
            sds((slots, chan), BF16),
            sds((held // 2, end), F32),
            sds((held // 2, end), BF16),
            sds((8, chan), F32),
        ],
        [me, plane],
        [*pieces, aux, x, outs, u3, fac, mids, u2, w, pat, u1],
        [pltpu.VMEM((slots, chan), F32), pltpu.VMEM((held, end), F32)] + back_scratch(side, slots, chan, mid),
    )


def upper_kernel(side, own_lanes, scalars, ins, outs, plain, up, grads, sg, eg, turned, field, dense, accum):
    aux, spread, pooled_grad, x_in, out_in, u3_in, fac_in, mid_in, u2_in, w_in, pat_in = ins
    mine, theirs, conv_grad, sg_own, accum_out, out_rows = outs
    me, plane = scalars[0][0], scalars[1][0] & 1
    slots = eg.shape[0]
    up[...] = dot_tn(spread()[...], pooled_grad()[...])
    aux, x_ref, out_ref, u3, fac = aux(), x_in(), out_in(), u3_in(), fac_in()
    accum[...] = jnp.zeros_like(accum)
    back_upper(
        side, me, aux, up, x_ref, w_in, mid_in, out_ref, u2_in, u3, fac, pat_in,
        sg, eg, turned, field, dense, accum, out_rows(), grads,
    )
    start = columns(eg.shape[1], dense.shape[1])[0]
    split_rows(grads, plane, mine, theirs, start)
    pad = pad_of(side)
    conv_grad()[...] = field[1, pad : pad + slots, :]
    accum_out()[...] = accum[0:8, :]
    if own_lanes:
        sg_own()[...] = sg[:, pl.ds(pl.multiple_of(me * own_lanes, own_lanes), own_lanes)]
    else:
        sg_own()[...] = sg[...]


def upper_backward(side, held, me, plane, aux, spread, pooled_grad, saved, own_lanes):
    x, w, mids, outs, u1, u2, u3, fac, pat = saved
    slots, chan = x.shape
    mid = w.shape[0]
    reduce_end, _, expand_end, _, end = columns(chan, mid)
    return call(
        functools.partial(upper_kernel, side, own_lanes),
        [
            sds((held // 2, expand_end - reduce_end), F32),
            sds((held // 2, expand_end - reduce_end), BF16),
            sds((slots, mid), F32),
            sds((slots, own_lanes or chan), F32),
            sds((8, mid), F32),
            sds((8, chan), F32),
        ],
        [me, plane],
        [aux, spread, pooled_grad, x, outs, u3, fac, mids, u2, w, pat],
        [pltpu.VMEM((slots, chan), F32), pltpu.VMEM((held, end), F32)] + back_scratch(side, slots, chan, mid),
    )


def lower_kernel(side, own_lanes, scalars, ins, outs, plain, turned, field, dense, accum):
    aux, conv_grad, w_in, u1_in, fac, mid_in, x_in, sg_own, accum_in, out_rows = ins
    x_grad, grads, grads_low = outs
    me = scalars[0][0]
    slots, mid = dense.shape
    pad = pad_of(side)
    clear_edges(field, side, slots)
    field[1, pad : pad + slots, :] = conv_grad()[...]
    accum[...] = jnp.zeros_like(accum)
    accum[0:8, :] = accum_in()[...]
    w_ref, x_ref = w_in(), x_in()
    reduce_end = x_ref.shape[1]
    back_lower(
        side, me, aux(), x_ref, w_ref, mid_in(), u1_in, fac(), turned, field, dense, accum, out_rows(), grads(), reduce_end,
    )
    grads_low()[...] = grads()[...].astype(BF16)
    grads_low.send()
    grads.send()
    low = dense[...].astype(BF16)
    if own_lanes:
        lanes = pl.ds(pl.multiple_of(me * own_lanes, own_lanes), own_lanes)
        x_grad()[...] = dot_nn(low, w_ref[:, lanes]) + sg_own()[...]
    else:
        x_grad()[...] = dot_nn(low, w_ref[:, 0:reduce_end]) + sg_own()[...]


def lower_backward(side, held, me, aux, upper, saved, own_lanes):
    x, w, mids, outs, u1, u2, u3, fac, pat = saved
    slots, chan = x.shape
    mid = w.shape[0]
    conv_grad, sg_own, accum, out_rows = upper
    return call(
        functools.partial(lower_kernel, side, own_lanes),
        [
            sds((slots, own_lanes or chan), F32),
            sds((held, chan + 2 * LANES), F32),
            sds((held, chan + 2 * LANES), BF16),
        ],
        [me],
        [aux, conv_grad, w, u1, fac, mids, x, sg_own, accum, out_rows],
        back_scratch(side, slots, chan, mid)[2:],
    )


GELU_A = 0.7978845608028654
GELU_B = 0.044715


def gelu_both(value):
    square = value * value
    curve = jnp.tanh(GELU_A * (value + GELU_B * value * square))
    slope = 0.5 * (1.0 + curve) + 0.5 * value * (1.0 - curve * curve) * (
        GELU_A * (1.0 + 3.0 * GELU_B * square)
    )
    return 0.5 * value * (1.0 + curve), slope


def readout_body(me, readin, w1, b1, w2, outs, full):
    act, mine, theirs, grad, half_in, keep, send = outs
    half = full.shape[1] // 2
    core = me & 1
    lanes = pl.ds(pl.multiple_of(core * half, half), half)
    half_in()[...] = readin[:, lanes]
    half_in.send()
    hidden = dot_nn(readin[...], w1()[...]) + b1[...]
    value, slope = gelu_both(hidden)
    act[...] = value.astype(BF16)
    width = keep.buffer.shape[2]
    for odd, out in ((1, send), (0, keep)):
        for q in range(out.buffer.shape[0]):
            at = pl.ds(pl.multiple_of((me ^ (2 * q + odd)) * width, width), width)
            out()[q] = dot_nn(act[...], w2()[:, at]).astype(BF16)
        out.send()
    full[...] = dot_nt((slope * grad()[...]).astype(BF16), w1()[...])
    theirs()[...] = full[:, pl.ds(pl.multiple_of((1 - core) * half, half), half)].astype(BF16)
    theirs.send()
    mine()[...] = full[:, lanes]
    mine.send()


def readout_shapes(rows, chan, hidden, width, n):
    return [
        sds((rows, chan // 2), F32),
        sds((rows, chan // 2), BF16),
        sds((rows, hidden), F32),
        sds((rows, chan // 2), BF16),
        sds((n // 2, rows, width // n), BF16),
        sds((n // 2, rows, width // n), BF16),
    ]


def readout_kernel(scalars, ins, outs, plain, full, act):
    readin, w1, b1, w2, cot = ins
    outs[2]()[...] = dot_nt(cot()[...], w2()[...])
    outs[2].send()
    readout_body(scalars[0][0], readin(), w1, b1(), w2, [act, *outs], full)


def readout(me, readin, w1, b1, w2, cot, n):
    rows, chan = readin.shape
    return call(
        readout_kernel,
        readout_shapes(rows, chan, *w2.shape, n),
        [me],
        [readin, w1, b1, w2, cot],
        [pltpu.VMEM((rows, chan), F32), pltpu.VMEM((rows, w2.shape[0]), BF16)],
    )


class Later:
    def __init__(self, source, buffer, sem):
        self.copy, self.buffer, self.waited = pltpu.make_async_copy(source, buffer, sem), buffer, False

    def start(self):
        self.copy.start()

    def __call__(self):
        if not self.waited:
            self.copy.wait()
            self.waited = True
        return self.buffer


def second_kernel(side, count, scalars, ins, outs, plain, field, act, stage, scr, sems, full, hid, w1_buf, w2_buf, wsems):
    pieces, (w1, w2) = plain[:count], plain[count:]
    w1, w2 = Later(w1, w1_buf, wsems.at[0]), Later(w2, w2_buf, wsems.at[1])
    me = scalars[0][0]
    sources = [item() for item in outs[:3]]
    ready = assemble(me, pieces, None, *sources, stage, scr, sems, (w1, w2))
    aux, x, b1 = [item() for item in ins]
    readin, keep, rest, cot_out = outs[3], outs[4:9], outs[9:15], outs[15]
    cot = cot_out()
    share = cot.shape[1] // count
    for r in range(count):
        start = (me ^ r) * share
        for index in range((stage.shape[2] - 2 * LANES) // LANES * 2):
            (row, lane), (low_row, low_lane) = cot_block(index, share)
            lanes = pl.ds(pl.multiple_of(start + lane, LANES), LANES)
            low_lane = 2 * LANES + low_lane
            cot[row : row + 16, lanes] = stage[r, low_row : low_row + 16, low_lane : low_lane + LANES]
    cot_out.send()

    def between():
        rest[2]()[...] = dot_nt(cot[...], w2()[...])
        rest[2].send()

    forward_body(side, aux, x, *sources, keep, field, act, readin(), ready, between)
    readin.send()
    for item in outs[:3]:
        item.send()
    readout_body(me, readin(), w1, b1, w2, [hid, *rest], full)


def second_forward(side, chan, mid, me, aux, x, pieces, w1, b1, w2):
    slots = side * side
    hidden, width = w2.shape
    got = call(
        functools.partial(second_kernel, side, len(pieces)),
        whole_shapes(chan, mid)
        + [sds((slots, chan), BF16)]
        + kept_shapes(slots, chan, mid)
        + readout_shapes(slots, chan, hidden, width, len(pieces))
        + [sds((slots, width), BF16)],
        [me],
        [aux, x, b1],
        forward_scratch(side, mid)
        + assemble_scratch(pieces, mid, slots * width // mid)
        + [
            pltpu.VMEM((slots, chan), F32),
            pltpu.VMEM((slots, hidden), BF16),
            pltpu.VMEM(w1.shape, BF16),
            pltpu.VMEM(w2.shape, BF16),
            pltpu.SemaphoreType.DMA((2,)),
        ],
        plain=[*pieces, w1, w2],
    )
    got = list(got)
    return got[3], [x] + got[:3] + got[4:9], got[9:]


def tail_kernel(placed, count, scalars, ins, outs, plain, stacked, low, cot, w2_buf, buffer, sems, out_sems):
    parts, (readin, w1, b1, grad) = ins[:count], ins[count:]
    w1_grad, b1_grad, b2_grad, w2_out = outs
    me = scalars[0][0]
    rows = readin.buffer.shape[0]
    own, w2, *rest = plain
    w2 = Later(w2, w2_buf, sems.at[1 + len(rest)])
    copies = [pltpu.make_async_copy(own, cot.at[0:rows, :], sems.at[0])]
    for r, piece in enumerate(rest):
        share = piece.shape[1]
        lanes = pl.ds(pl.multiple_of((me ^ r) * share, share), share) if placed else slice(0, share)
        copies.append(pltpu.make_async_copy(piece, cot.at[rows:, lanes], sems.at[1 + r]))
    for copy in copies:
        copy.start()
    w2.start()
    split = len(parts) // 2
    half = parts[0].buffer.shape[1]
    lanes = [pl.ds(pl.multiple_of(((me & 1) ^ odd) * half, half), half) for odd in range(2)]
    stacked[0:rows, :] = readin()[...]
    for odd, group in enumerate((parts[:split], parts[split:])):
        at = rows
        for part in group:
            count = part.buffer.shape[0]
            stacked[at : at + count, lanes[odd]] = part()[...]
            at += count
    hidden = dot_nn(stacked[...], w1()[...]) + b1()[...]
    value, slope = gelu_both(hidden)
    turned = value.T.astype(BF16)
    low[0:rows, :] = (slope[0:rows] * grad()[...]).astype(BF16)
    width = buffer.shape[2]
    flights = []
    for copy in copies:
        copy.wait()
    for r in range(cot.shape[1] // width):
        if r >= 2:
            flights[r - 2].wait()
        lanes = slice(r * width, (r + 1) * width)
        buffer[r % 2] = dot_nn(turned, cot[:, lanes])
        flights.append(pltpu.make_async_copy(buffer.at[r % 2], w2_out.target.at[:, lanes], out_sems.at[r % 2]))
        flights[-1].start()
    low[rows:, :] = (slope[rows:] * dot_nt(cot[rows:, :], w2()[...])).astype(BF16)
    w1_grad()[...] = dot_tn(stacked[...], low[...])
    w1_grad.send()
    b1_grad()[...] = jnp.sum(low[...].astype(F32), axis=0, keepdims=True)
    share = b2_grad.buffer.shape[1]
    lanes = pl.ds(pl.multiple_of(me * share, share), share)
    b2_grad()[...] = jnp.sum(cot[:, lanes].astype(F32), axis=0, keepdims=True)
    for flight in flights[-2:]:
        flight.wait()


def tail(me, b1, w1, w2, grad, readin, parts, own, rest, placed, n):
    rows, chan = readin.shape
    total = rows + sum(x.shape[0] for x in parts) // 2
    hidden, width = w2.shape
    chunk = min(width, 2048)
    return call(
        functools.partial(tail_kernel, placed, len(parts)),
        [sds((chan, hidden), F32), sds((1, hidden), F32), sds((1, width // n), F32), sds((hidden, width), F32)],
        [me],
        [*parts, readin, w1, b1, grad],
        [
            pltpu.VMEM((total, chan), BF16),
            pltpu.VMEM((total, hidden), BF16),
            pltpu.VMEM((total, width), BF16),
            pltpu.VMEM(w2.shape, BF16),
            pltpu.VMEM((2, hidden, chunk), F32),
            pltpu.SemaphoreType.DMA((2 + len(rest),)),
            pltpu.SemaphoreType.DMA((2,)),
        ],
        plain=[own, w2, *rest],
        direct=(3,),
    )


def finish_kernel(count, scalars, ins, outs, plain, scr):
    red, conv, exp, mid_gain, mid_bias, out_gain, out_bias, tokens = [item() for item in outs]
    late, middle, parts = ins[0:2], ins[2:4], ins[4 : 4 + count]
    bias, *shares = ins[4 + count :]
    value = bias()[...]
    for item in shares:
        value = value + item()[...].astype(F32)
    tokens[...] = value.astype(BF16)
    outs[7].send()
    chan, mid = red.shape[2], conv.shape[3]
    held = red.shape[1]
    reduce_end, conv_end, expand_end, mid_end, end = columns(chan, mid)
    plane = scalars[1][0] & 1
    few = held // 2

    def from_pair(pair, base, k):
        mine, other = [item()[...] for item in pair]
        for odd in range(2):
            value = jnp.where(plane == odd, mine, other)
            rows = slice(odd * few, odd * few + few)
            for j in range(TAPS):
                at = reduce_end + j * mid - base
                conv[k, j, rows, :] = value[:, at : at + mid].astype(F32)
            exp[k, rows, :] = value[:, conv_end - base : expand_end - base].astype(F32)
            if base == 0:
                red[k, rows, :] = value[:, 0:reduce_end].astype(F32)
                scr[k, rows, :] = value[:, expand_end:end].astype(F32)

    scr[...] = jnp.zeros_like(scr)
    from_pair(late, 0, 1)
    from_pair(middle, reduce_end, 0)
    for item in outs[1:3]:
        item.send()
    total = parts[0]()[...]
    for part in parts[1:]:
        total = total + part()[...].astype(F32)
    red[0] = total[:, 0:reduce_end]
    outs[0].send()
    scr[0, 0:held, :] = total[:, reduce_end:]
    for k in range(2):
        flat = scr[k, :, 0:LANES].T
        for which in range(2):
            mid_gain[k, which : which + 1, :] = flat[2 * which : 2 * which + 1, 0:held]
            mid_bias[k, which : which + 1, :] = flat[2 * which + 1 : 2 * which + 2, 0:held]
        out_gain[k : k + 1, :] = scr[k, 0:1, LANES : LANES + out_gain.shape[1]]
        out_bias[k : k + 1, :] = scr[k, 1:2, LANES : LANES + out_bias.shape[1]]


def finish(me, plane, late, middle, parts, chan, mid, share, bias, shares):
    held = parts[0].shape[0]
    outs = [
        sds((2, held, chan), F32),
        sds((2, TAPS, held, mid), F32),
        sds((2, held, chan), F32),
        sds((2, 2, held), F32),
        sds((2, 2, held), F32),
        sds((2, share), F32),
        sds((2, share), F32),
        sds(shares[0].shape, BF16),
    ]
    return call(
        functools.partial(finish_kernel, len(parts)),
        outs,
        [me, plane],
        [*late, *middle, *parts, bias, *shares],
        [pltpu.VMEM((2, LANES, 2 * LANES), F32)],
    )


def iota(shape, dim):
    return lax.broadcasted_iota(jnp.int32, shape, dim).astype(F32)


def whole_part(value, divisor):
    return jnp.floor((value + 0.5) * (1.0 / divisor))


def table_at(target, place, extent):
    begin = whole_part(target * extent, POOLED)
    ending = whole_part((target + 1.0) * extent + (POOLED - 1), POOLED)
    inside = jnp.where((place >= begin) & (place < ending), 1.0, 0.0)
    return inside / (ending - begin)


def facts_kernel(scalars, ins, outs, plain):
    extent = scalars[0][0].astype(F32)
    for side, out in ((GRID, outs[0]), (POOLED, outs[1])):
        slots = side * side
        place = iota((slots, 1), 0)
        row = whole_part(place, side)
        column = place - row * side
        out()[:, 1:2] = jnp.where(column > 0.5, 1.0, 0.0)
        out()[:, 2:3] = jnp.where(column < side - 1.5, 1.0, 0.0)
        if side == GRID:
            out()[:, 0:1] = jnp.where((row < extent) & (column < extent), 1.0, 0.0)
        else:
            out()[:, 0:1] = jnp.ones((slots, 1), F32)
    shape = outs[2]().shape
    target, place = iota((shape[0], 1), 0), iota((1, shape[1]), 1)
    up, across = whole_part(target, POOLED), whole_part(place, GRID)
    rows = table_at(up, across, extent)
    lanes = table_at(target - up * POOLED, place - across * GRID, extent)
    outs[2]()[...] = (rows * lanes).astype(BF16)


def facts(grid):
    slots, few = GRID * GRID, POOLED * POOLED
    return call(
        facts_kernel,
        [sds((slots, LANES), F32), sds((few, LANES), F32), sds((few, slots), BF16)],
        [grid],
        [],
    )


def per_device(
    features,
    grid,
    reduce_w,
    conv_w,
    expand_w,
    mid_gain,
    mid_bias,
    out_gain,
    out_bias,
    read_w1,
    read_b1,
    read_w2,
    read_b2,
    cotangent,
):
    n = lax.axis_size("ch")
    chan, mid = reduce_w.shape[1], conv_w.shape[2]
    held, share = reduce_w.shape[2], features.shape[0]
    aligned = share == LANES and held % 16 == 0
    index = lax.axis_index("ch").astype(jnp.int32)
    planes = lax.axis_size("img")
    me = index[None]
    plane = lax.axis_index("img").astype(jnp.int32)[None]

    feat = jnp.transpose(features[:, 0, :])
    cot = jnp.transpose(cotangent[:, 0, :])
    red = jnp.transpose(reduce_w, (0, 2, 1))
    conv = jnp.transpose(conv_w, (0, 1, 3, 2))
    norms = (mid_gain, mid_bias, out_gain, out_bias)
    few = cot.shape[0]
    slot_facts, few_facts, spread = facts(grid)

    bias_one = read_b1[None, :]

    if aligned:
        (first_packet,) = pack(0, feat, red, conv, expand_w, *norms)
        far = neighbours(first_packet)
        second_packet, cot = pack(1, cot, red, conv, expand_w, *norms, after=[first_packet])

        (second_packet,) = gate([second_packet], far[2])

    cot_rest = [ppermute_xor(cot, "img", 1)]
    held_cot = join(cot, cot_rest[0])

    if aligned:
        second_far = neighbours(second_packet)
        far = dict(zip(far, gate(list(far.values()), held_cot, spread)))
        (held_cot,) = gate([held_cot], *far.values())
        cot_rest = doubled(cot_rest, held_cot)
        first_pieces = with_cores(first_packet, far)
        pooled, saved_first = block_forward(GRID, chan, mid, me, slot_facts, spread, first_pieces, None)
        far = dict(zip(second_far, gate(list(second_far.values()), pooled, *cot_rest)))
        second_pieces = with_cores(second_packet, far)
        readin, saved_second, got = second_forward(
            POOLED, chan, mid, me, few_facts, pooled, second_pieces, read_w1, bias_one, read_w2
        )
        mine, theirs, own_grad, half_in, keep, send, cot_own = got
    else:
        rows = jnp.concatenate(
            [red, jnp.transpose(conv, (0, 2, 1, 3)).reshape(2, held, TAPS * mid), expand_w], axis=2
        )
        rows = lax.all_gather(rows, "ch", axis=1, tiled=True)
        mids = jnp.stack([mid_gain, mid_bias], axis=2).reshape(2, 4, held)
        mids = jnp.pad(lax.all_gather(mids, "ch", axis=2, tiled=True), ((0, 0), (0, 4), (0, 0)))
        outs = jnp.stack([out_gain, out_bias], axis=1)
        outs = jnp.pad(lax.all_gather(outs, "ch", axis=2, tiled=True), ((0, 0), (0, 6), (0, 0)))
        x_whole = lax.all_gather(feat, "ch", axis=1, tiled=True)
        pooled, saved_first = block_forward(
            GRID, chan, mid, me, slot_facts, spread, None, (x_whole, rows[0], mids[0], outs[0])
        )
        readin, saved_second = block_forward(
            POOLED, chan, mid, me, few_facts, None, None, (pooled, rows[1], mids[1], outs[1])
        )
        cot_own = lax.all_gather(cot, "ch", axis=1, tiled=True)
        mine, theirs, own_grad, half_in, keep, send = readout(me, readin, read_w1, bias_one, read_w2, cot_own, n)

    if not aligned:
        cot_rest = doubled(cot_rest, held_cot)

    half = summed(mine, ppermute_xor(theirs, "ch", 1))
    far = neighbours(half)
    cot_rest = join(*cot_rest, after=[half])
    got = ppermute_xor(send, "ch", 1)
    shares = [summed(keep[q], got[q]) for q in range(n // 2)]
    far = dict(zip(far, gate(list(far.values()), cot_rest, shares[0])))
    if aligned:
        (cot_rest,) = gate([cot_rest], *far.values())
        cot_far = neighbours(cot_rest)
    (half_in,) = gate([half_in], half)
    parts = [ppermute_xor(half_in, "img", m) for m in (1, 2) if m < planes]
    grad_pieces = with_cores(half, far)

    pooled_grad, late_mine, late_theirs, late_out = late_backward(
        POOLED, held, me, plane, few_facts, grad_pieces, saved_second
    )
    late_got = ppermute_xor(late_theirs, "img", 1)
    (half_in,) = gate([half_in], pooled_grad)
    parts += [ppermute_xor(half_in, "img", m) for m in range(3, planes)]
    own_lanes = share if aligned else 0
    middle_mine, middle_theirs, *upper = upper_backward(
        GRID, held, me, plane, slot_facts, spread, pooled_grad, saved_first, own_lanes
    )
    middle_got = ppermute_xor(middle_theirs, "img", 1)
    (late_got,) = gate([late_got], upper[0])
    late_half = summed(late_mine, late_got)
    late_got = ppermute_xor(late_half, "img", 2)
    parts = gate(parts, upper[0])
    parts = [*parts, *[ppermute_xor(x, "ch", 1) for x in parts]]
    if aligned:
        cot_far = dict(zip(cot_far, gate(list(cot_far.values()), upper[0])))
        rest_pieces = with_cores(cot_rest, cot_far)
    else:
        rest_pieces = [lax.all_gather(cot_rest, "ch", axis=1, tiled=True)]
    feat_grad, last_grads, last_low = lower_backward(
        GRID, held, me, slot_facts, upper, saved_first, own_lanes
    )
    last = [last_grads] + along_images(last_low)
    late_got, middle_got = gate([late_got, middle_got], last_grads)
    middle_half = summed(middle_mine, middle_got)
    middle_got = ppermute_xor(middle_half, "img", 2)
    late_half = summed(late_half, late_got)
    for mask in (1 << k for k in range(2, planes.bit_length() - 1)):
        late_half = summed(late_half, ppermute_xor(late_half, "img", mask))
    late = (late_half, ppermute_xor(late_half, "img", 1))
    w1_grad, b1_grad, b2_grad, w2_grad = tail(
        me, bias_one, read_w1, read_w2, own_grad, readin, parts, cot_own, rest_pieces, aligned, n
    )
    (middle_got,) = gate([middle_got], b1_grad)
    middle_half = summed(middle_half, middle_got)
    for mask in (1 << k for k in range(2, planes.bit_length() - 1)):
        middle_half = summed(middle_half, ppermute_xor(middle_half, "img", mask))
    middle = (middle_half, ppermute_xor(middle_half, "img", 1))
    shares = gate(shares, middle_half)
    shares = [shares[0]] + [ppermute_xor(shares[q], "ch", 2 * q) for q in range(1, n // 2)]

    red_grad, conv_grad, exp_grad, mid_gain_grad, mid_bias_grad, out_gain_grad, out_bias_grad, tokens = finish(
        me, plane, late, middle, last, chan, mid, share, read_b2[None, :], shares
    )
    if not aligned:
        feat_grad = lax.dynamic_slice_in_dim(feat_grad, index * share, share, 1)
        both = jnp.stack([upper[3], late_out])
        both = lax.dynamic_slice_in_dim(both, index * share, share, 2)
        both = lax.psum(both.astype(BF16), "img").astype(F32)
        out_gain_grad, out_bias_grad = both[:, 0], both[:, 1]

    return (
        jnp.transpose(tokens)[:, None, :],
        jnp.transpose(feat_grad)[:, None, :],
        jnp.transpose(red_grad, (0, 2, 1)),
        jnp.transpose(conv_grad, (0, 1, 3, 2)),
        exp_grad,
        mid_gain_grad,
        mid_bias_grad,
        out_gain_grad,
        out_bias_grad,
        w1_grad,
        b1_grad[0],
        w2_grad,
        b2_grad[0],
    )


def solution(mesh):
    return jax.shard_map(
        per_device,
        mesh=mesh,
        in_specs=(
            P("ch", "img", None),
            P("img"),
            P(None, None, "ch"),
            P(None, None, None, "ch"),
            P(None, "ch", None),
            P(None, None, "ch"),
            P(None, None, "ch"),
            P(None, "ch"),
            P(None, "ch"),
            P(None, "ch"),
            P("ch"),
            P("ch", None),
            P("ch"),
            P("ch", "img", None),
        ),
        out_specs=(
            P("ch", "img", None),
            P("ch", "img", None),
            P(None, None, "ch"),
            P(None, None, None, "ch"),
            P(None, "ch", None),
            P(None, None, "ch"),
            P(None, None, "ch"),
            P(None, "ch"),
            P(None, "ch"),
            P(None, "ch"),
            P("ch"),
            P("ch", None),
            P("ch"),
        ),
        check_vma=False,
    )
```
